32 devices in a mesh: rep: 8 (over y, x, core), tp: 4 (over z).
Axes of the slice: x: 2, y: 2, z: 4, core: 2. Of those that a mesh axis runs over, the one named last changes fastest.
Arguments:
- hidden: bfloat16 [36864, 1024], P('rep', 'tp'), may hold values from -0.09375 to 0.09375
- out_grad: bfloat16 [36864, 512], P(('rep', 'tp')), may hold values from -6 to 6
- momentum: float32 [8, 1024, 512], P('rep', 'tp'), may hold values from -6 to 6
- band_rows: int32 [16, 8], P('tp'), may hold values from 0 to 48, as said below
- band_start_columns: int32 [16, 8], P('tp'), may hold values from 0 to 48, as said below
Outputs:
- momentum_out: float32 [8, 1024, 512], P('rep', 'tp')
- update: bfloat16 [1024, 512], P('tp')
The draws below stay inside these ranges and needn't reach their ends.
Inputs may be any that keep to these rules, and one draw needn't show every extreme that they name: `band_rows`: multiples of 16, the same for every replica. `band_start_columns`: multiples of 16, the same for every replica.
All inputs are finite; a program needn't handle non-finite values.
Results may differ from the reference program's by a relative error of at most 0.001.
Values may be sent and summed in bfloat16 or wider, within the bound.
No kernel may reach another device: no remote copies, remote signals or barrier semaphores. Data moves between devices by JAX's collectives and lax.ppermute only.
A program may use at most 64 MiB of HBM per device.

```python
import jax
import jax.numpy as jnp
from jax import lax

TOK = 4608
CCH = 8
ALL_TOK = 36864
FFW = 1024
COLS = 512
CROWS = 16
N_REP = 8


def draw_band_rows(key, part):
    values = jax.random.randint(jax.random.fold_in(key, 11), (CROWS, CCH), 0, 4) * 16
    return values.at[0, 0].set(48).at[0, 1].set(0).astype(jnp.int32)


def draw_band_start_columns(key, part):
    values = jax.random.randint(jax.random.fold_in(key, 23), (CROWS, CCH), 0, 4) * 16
    return values.at[0, 0].set(0).at[0, 1].set(48).astype(jnp.int32)


def steps_of(own_key, shape, pieces, least, top_value):
    def one(dim, parts):
        draws = jax.random.uniform(jax.random.fold_in(jax.random.fold_in(own_key, 6), dim), (parts,), jnp.float32, least / len(pieces), top_value / len(pieces))
        return jnp.repeat(jnp.exp(draws), shape[dim] // parts).reshape((-1,) + (1,) * (len(shape) - dim - 1))

    loudness = one(*pieces[0])
    for cut in pieces[1:]:
        loudness = loudness * one(*cut)
    return loudness


def normal_values(rng, shape, width, limit, split=(), held_as=jnp.bfloat16):
    values = jax.random.normal(rng, shape, jnp.float32) * width
    if len(split) > 0:
        values = steps_of(rng, shape, split, -0.22, 0.18) * values
    return jnp.clip(values, min=-limit, max=limit).astype(held_as)


def setup_inputs(seed: int = 0) -> dict:
    seeds = jax.random.split(jax.random.key(seed), 6)
    hidden = normal_values(seeds[0], (ALL_TOK, FFW), TOK ** -0.5, 0.09375, ((0, 8), (1, 4)))
    out_grad = normal_values(seeds[1], (ALL_TOK, COLS), 1.0, 6.0, ((0, 32),))
    momentum = normal_values(seeds[2], (N_REP, FFW, COLS), 1.0, 6.0, ((0, 8), (1, 4)), jnp.float32)
    band_rows = draw_band_rows(jax.random.fold_in(seeds[5], 71), 0)
    band_start_columns = draw_band_start_columns(jax.random.fold_in(seeds[5], 71), 0)
    return {"hidden": hidden, "out_grad": out_grad, "momentum": momentum, "band_rows": band_rows, "band_start_columns": band_start_columns}


decay_rate = 0.9
highest_precision = lax.Precision.HIGHEST

def basis_matrix():
    frequency = jnp.arange(64, dtype=jnp.float32)[:, None]
    sample_pos = jnp.arange(64, dtype=jnp.float32)[None, :]
    norm_scale = jnp.where(frequency == 0, jnp.sqrt(jnp.float32(1.0 / 64)), jnp.sqrt(jnp.float32(2.0 / 64)))
    return norm_scale * jnp.cos(jnp.pi * (sample_pos + 0.5) * frequency / 64)

def reference(hidden, out_grad, momentum, band_rows, band_start_columns):
    basis = basis_matrix()
    tok_rows = hidden.shape[0] // N_REP
    row_count = hidden.shape[1]
    col_count = out_grad.shape[1]
    group_rows = row_count // 64
    group_cols = col_count // 64
    rows_flat = band_rows.reshape(-1).astype(jnp.int32)
    flattened_columns = band_start_columns.reshape(-1).astype(jnp.int32)

    def to_blocks(matrix):
        return matrix.reshape(group_rows, 64, group_cols, 64).transpose(0, 2, 1, 3).reshape(group_rows * group_cols, 64, 64)

    def from_blocks(blocks):
        return blocks.reshape(group_rows, group_cols, 64, 64).transpose(0, 2, 1, 3).reshape(row_count, col_count)
    inner_row = jnp.arange(64, dtype=jnp.int32)[None, :, None]
    inner_col = jnp.arange(64, dtype=jnp.int32)[None, None, :]
    inside = (inner_row >= rows_flat[:, None, None]) & (inner_row < rows_flat[:, None, None] + 16)
    inside = inside & (inner_col >= flattened_columns[:, None, None]) & (inner_col < flattened_columns[:, None, None] + 16)
    keep_mask = jnp.where(inside, jnp.float32(0.0), jnp.float32(1.0))

    def one_replica(replica):
        hidden_part = lax.dynamic_slice_in_dim(hidden, replica * tok_rows, tok_rows, 0)
        grad_part = lax.dynamic_slice_in_dim(out_grad, replica * tok_rows, tok_rows, 0)
        gradient = jnp.dot(hidden_part.T, grad_part, preferred_element_type=jnp.float32)
        merged = decay_rate * momentum[replica] + gradient
        coefficients = jnp.einsum('ij,cjk,lk->cil', basis, to_blocks(merged), basis, precision=highest_precision)
        frequency_bands = jax.vmap(lambda block, row_at, col_at: lax.dynamic_slice(block, (row_at, col_at), (16, 16)))(coefficients, rows_flat, flattened_columns)
        restored = jnp.einsum('ji,cjk,kl->cil', basis, coefficients * keep_mask, basis, precision=highest_precision)
        return (from_blocks(restored), frequency_bands)
    momentum_out, all_bands = lax.map(one_replica, jnp.arange(N_REP, dtype=jnp.int32))
    summed = lax.optimization_barrier(jnp.sum(all_bands, axis=0))
    placed = jax.vmap(lambda frequency_bands, row_at, col_at: lax.dynamic_update_slice(jnp.zeros((64, 64), jnp.float32), frequency_bands, (row_at, col_at)))(summed, rows_flat, flattened_columns)
    update = from_blocks(jnp.einsum('ji,cjk,kl->cil', basis, placed, basis, precision=highest_precision))
    return (momentum_out, update.astype(jnp.bfloat16))
```

```python
import functools

import jax
import jax.numpy as jnp
import numpy as np
from jax import lax
from jax.experimental import pallas as pl
from jax.experimental.pallas import tpu as pltpu
from jax.sharding import PartitionSpec as P

decay_rate = 0.9
order = 64
band = 16
steps = order // band


def basis_matrix():
    frequency = np.arange(order, dtype=np.float64)[:, None]
    sample_pos = np.arange(order, dtype=np.float64)[None, :]
    norm_scale = np.where(frequency == 0, np.sqrt(1.0 / order), np.sqrt(2.0 / order))
    return norm_scale * np.cos(np.pi * (sample_pos + 0.5) * frequency / order)


def halves_of(matrix):
    high = matrix.astype(jnp.bfloat16)
    low = (matrix - high.astype(matrix.dtype)).astype(jnp.bfloat16)
    return np.stack([high, low])


def diagonal_blocks(width):
    count = next(c for c in (4, 2, 1) if width % (c * order) == 0)
    return halves_of(np.kron(np.eye(count), basis_matrix()))


def fold_matrix(width):
    return np.kron(np.eye(width // order), np.kron(np.ones((steps, 1)), np.eye(band))).astype(jnp.bfloat16)


def split2(x):
    high = x.astype(jnp.bfloat16)
    return high, (x - high.astype(jnp.float32)).astype(jnp.bfloat16)


def split3(x):
    high, low = split2(x)
    rest = x - high.astype(jnp.float32) - low.astype(jnp.float32)
    return high, low, rest.astype(jnp.bfloat16)


def dot(a, b, dims=((1,), (0,))):
    return lax.dot_general(a, b, (dims, ((), ())), preferred_element_type=jnp.float32)


def dot3(a, b, dims=((1,), (0,))):
    return dot(a[0], b[0], dims) + (dot(a[0], b[1], dims) + dot(a[1], b[0], dims))


def on_rows(basis_ref, x, transposed):
    basis = basis_ref[0], basis_ref[1]
    side = basis[0].shape[0]
    dims = ((0,), (0,)) if transposed else ((1,), (0,))
    parts = [dot3(basis, split2(x[i : i + side]), dims) for i in range(0, x.shape[0], side)]
    return parts[0] if len(parts) == 1 else jnp.concatenate(parts, axis=0)


def on_columns(basis_ref, x, transposed):
    basis = basis_ref[0], basis_ref[1]
    side = basis[0].shape[0]
    dims = ((1,), (0,)) if transposed else ((1,), (1,))
    parts = [dot3(split2(x[:, i : i + side]), basis, dims) for i in range(0, x.shape[1], side)]
    return parts[0] if len(parts) == 1 else jnp.concatenate(parts, axis=1)


def column_mask(row, cols_ref, width):
    group = lax.rem(lax.broadcasted_iota(jnp.int32, (band, width), 1), order) // band
    return group == cols_ref[row : row + 1, :]


def lifted(folded, rows_ref, cols_ref, fold_ref, row_basis_ref, column_basis_ref):
    width = cols_ref.shape[1]
    spread = sum(dot(part, fold_ref[...], ((1,), (1,))) for part in split3(folded))
    pieces = []
    for row in range(rows_ref.shape[0]):
        inside = jnp.where(column_mask(row, cols_ref, width), spread[row * band : (row + 1) * band], 0.0)
        for step in range(steps):
            pieces.append(jnp.where(rows_ref[row : row + 1, :] == step, inside, 0.0))
    coefficients = jnp.concatenate(pieces, axis=0)
    return on_columns(column_basis_ref, on_rows(row_basis_ref, coefficients, True), True)


def bands_kernel(m_ref, rows_ref, cols_ref, fold_ref, row_basis_ref, column_basis_ref, bands_ref):
    width = cols_ref.shape[1]
    coefficients = on_columns(column_basis_ref, on_rows(row_basis_ref, m_ref[...], False), False)
    pieces = []
    for row in range(rows_ref.shape[0]):
        taken = jnp.zeros((band, width), jnp.float32)
        for step in range(steps):
            at = row * order + step * band
            taken = jnp.where(rows_ref[row : row + 1, :] == step, coefficients[at : at + band], taken)
        pieces.append(jnp.where(column_mask(row, cols_ref, width), taken, 0.0))
    taken = jnp.concatenate(pieces, axis=0)
    bands_ref[...] = sum(dot(part, fold_ref[...]) for part in split3(taken))


def remove_kernel(m_ref, bands_ref, rows_ref, cols_ref, fold_ref, row_basis_ref, column_basis_ref, out_ref):
    out_ref[...] = m_ref[...] - lifted(
        bands_ref[...], rows_ref, cols_ref, fold_ref, row_basis_ref, column_basis_ref
    )


def update_kernel(*refs):
    *part_refs, rows_ref, cols_ref, fold_ref, row_basis_ref, column_basis_ref, out_ref = refs
    parts = [ref[...] for ref in part_refs]
    out_ref[...] = lifted(
        pair_sum(parts), rows_ref, cols_ref, fold_ref, row_basis_ref, column_basis_ref
    ).astype(out_ref.dtype)


def pair_sum(parts):
    while len(parts) > 1:
        parts = [a + b for a, b in zip(parts[::2], parts[1::2])]
    return parts[0]


def call(kernel, shape, dtype, *operands):
    return pl.pallas_call(
        kernel,
        out_shape=jax.ShapeDtypeStruct(shape, dtype),
        compiler_params=pltpu.CompilerParams(vmem_limit_bytes=32 * 2**20),
        cost_estimate=pl.CostEstimate(
            flops=4 * 10**8, bytes_accessed=4 * 10**6, transcendentals=0
        ),
    )(*operands)


def spread_sum(x, axis):
    size = lax.axis_size(axis)
    if size & (size - 1):
        return [lax.psum(x, axis)]
    stride, parts = 1, [x]
    while stride < size:
        count = min(8, size // stride)
        x = pair_sum(parts)
        parts = [x] + [
            lax.ppermute(x, axis, [(i, i ^ (stride * k)) for i in range(size)]) for k in range(1, count)
        ]
        stride *= count
    return parts


def product(hidden_rows, grad_rows):
    return dot(hidden_rows, grad_rows, ((0,), (0,)))


def gathered_gradient(hidden, out_grad):
    return product(hidden, lax.all_gather(out_grad, "tp", axis=0, tiled=True))


def line_gradient(hidden, out_grad):
    tok = out_grad.shape[0]
    me = lax.axis_index("tp")
    left = me < 2
    pair = me ^ 1
    cross = jnp.where(left, 2, 1)
    far = jnp.where(left, 3, 0)

    def rows_of(part):
        return lax.dynamic_slice_in_dim(hidden, part * tok, tok, 0)

    def send(x, perm):
        return lax.ppermute(x, "tp", perm)

    both_ways = [(0, 1), (1, 0), (2, 3), (3, 2)]
    across = [(1, 2), (2, 1)]
    outward = [(1, 0), (2, 3)]
    inward = [(0, 1), (3, 2)]

    pair_grad = send(out_grad, both_ways)
    cross_grad = send(out_grad, across)
    far_hidden = rows_of(far)
    sent_hidden, pair_grad = lax.optimization_barrier((far_hidden, pair_grad))
    far_grad = send(pair_grad, across)
    cross_grad = cross_grad + send(cross_grad, outward)
    helped_hidden = send(sent_hidden, inward)
    helped = send(product(helped_hidden, far_grad), outward)
    gradient = product(rows_of(me), out_grad) + product(rows_of(pair), pair_grad)
    gradient = gradient + product(rows_of(cross), cross_grad)
    return gradient + product(far_hidden, far_grad) + helped


def local(hidden, out_grad, momentum, band_rows, band_start_columns):
    row_count = hidden.shape[1]
    col_count = out_grad.shape[1]
    rows = jnp.repeat(band_rows.astype(jnp.int32) // band, order, axis=1)
    cols = jnp.repeat(band_start_columns.astype(jnp.int32) // band, order, axis=1)
    tables = (
        rows,
        cols,
        jnp.asarray(fold_matrix(col_count)),
        jnp.asarray(diagonal_blocks(row_count)),
        jnp.asarray(diagonal_blocks(col_count)),
    )
    gradient = (line_gradient if lax.axis_size("tp") == 4 else gathered_gradient)(hidden, out_grad)
    m = decay_rate * momentum[0] + gradient
    folded_shape = (row_count // steps, col_count // steps)
    bands = call(bands_kernel, folded_shape, jnp.float32, m, *tables)
    parts = spread_sum(bands, "rep")
    momentum_out = call(remove_kernel, m.shape, jnp.float32, m, bands, *tables)
    update = call(update_kernel, m.shape, jnp.bfloat16, *parts, *tables)
    return (momentum_out[None], update)


def solution(mesh):
    return jax.shard_map(
        local,
        mesh=mesh,
        in_specs=(
            P("rep", "tp"),
            P(("rep", "tp"), None),
            P("rep", "tp", None),
            P("tp", None),
            P("tp", None),
        ),
        out_specs=(P("rep", "tp", None), P("tp", None)),
        check_vma=False,
    )
```

```python
import functools

import jax
import jax.numpy as jnp
import numpy as np
from jax import lax
from jax.experimental import pallas as pl
from jax.experimental.pallas import tpu as pltpu
from jax.sharding import PartitionSpec as P

decay_rate = 0.9
order = 64
band = 16
steps = order // band


def basis_matrix():
    frequency = np.arange(order, dtype=np.float64)[:, None]
    sample_pos = np.arange(order, dtype=np.float64)[None, :]
    norm_scale = np.where(frequency == 0, np.sqrt(1.0 / order), np.sqrt(2.0 / order))
    return norm_scale * np.cos(np.pi * (sample_pos + 0.5) * frequency / order)


def halves_of(matrix):
    high = matrix.astype(jnp.bfloat16)
    low = (matrix - high.astype(matrix.dtype)).astype(jnp.bfloat16)
    return np.stack([high, low])


def diagonal_blocks(width):
    count = next(c for c in (4, 2, 1) if width % (c * order) == 0)
    return halves_of(np.kron(np.eye(count), basis_matrix()))


def fold_matrix(width):
    return np.kron(np.eye(width // order), np.kron(np.ones((steps, 1)), np.eye(band))).astype(jnp.bfloat16)


def split2(x):
    high = x.astype(jnp.bfloat16)
    return high, (x - high.astype(jnp.float32)).astype(jnp.bfloat16)


def split3(x):
    high, low = split2(x)
    rest = x - high.astype(jnp.float32) - low.astype(jnp.float32)
    return high, low, rest.astype(jnp.bfloat16)


def dot(a, b, dims=((1,), (0,))):
    return lax.dot_general(a, b, (dims, ((), ())), preferred_element_type=jnp.float32)


def dot3(a, b, dims=((1,), (0,))):
    return dot(a[0], b[0], dims) + (dot(a[0], b[1], dims) + dot(a[1], b[0], dims))


def on_rows(basis_ref, x, transposed):
    basis = basis_ref[0], basis_ref[1]
    side = basis[0].shape[0]
    dims = ((0,), (0,)) if transposed else ((1,), (0,))
    parts = [dot3(basis, split2(x[i : i + side]), dims) for i in range(0, x.shape[0], side)]
    return parts[0] if len(parts) == 1 else jnp.concatenate(parts, axis=0)


def on_columns(basis_ref, x, transposed):
    basis = basis_ref[0], basis_ref[1]
    side = basis[0].shape[0]
    dims = ((1,), (0,)) if transposed else ((1,), (1,))
    parts = [dot3(split2(x[:, i : i + side]), basis, dims) for i in range(0, x.shape[1], side)]
    return parts[0] if len(parts) == 1 else jnp.concatenate(parts, axis=1)


def column_mask(row, cols_ref, width):
    group = lax.rem(lax.broadcasted_iota(jnp.int32, (band, width), 1), order) // band
    return group == cols_ref[row : row + 1, :]


def lifted(folded, rows_ref, cols_ref, fold_ref, row_basis_ref, column_basis_ref):
    width = cols_ref.shape[1]
    spread = sum(dot(part, fold_ref[...], ((1,), (1,))) for part in split3(folded))
    pieces = []
    for row in range(rows_ref.shape[0]):
        inside = jnp.where(column_mask(row, cols_ref, width), spread[row * band : (row + 1) * band], 0.0)
        for step in range(steps):
            pieces.append(jnp.where(rows_ref[row : row + 1, :] == step, inside, 0.0))
    coefficients = jnp.concatenate(pieces, axis=0)
    return on_columns(column_basis_ref, on_rows(row_basis_ref, coefficients, True), True)


def bands_kernel(m_ref, rows_ref, cols_ref, fold_ref, row_basis_ref, column_basis_ref, bands_ref):
    width = cols_ref.shape[1]
    coefficients = on_columns(column_basis_ref, on_rows(row_basis_ref, m_ref[...], False), False)
    pieces = []
    for row in range(rows_ref.shape[0]):
        taken = jnp.zeros((band, width), jnp.float32)
        for step in range(steps):
            at = row * order + step * band
            taken = jnp.where(rows_ref[row : row + 1, :] == step, coefficients[at : at + band], taken)
        pieces.append(jnp.where(column_mask(row, cols_ref, width), taken, 0.0))
    taken = jnp.concatenate(pieces, axis=0)
    bands_ref[...] = sum(dot(part, fold_ref[...]) for part in split3(taken))


def remove_kernel(m_ref, bands_ref, rows_ref, cols_ref, fold_ref, row_basis_ref, column_basis_ref, out_ref):
    out_ref[...] = m_ref[...] - lifted(
        bands_ref[...], rows_ref, cols_ref, fold_ref, row_basis_ref, column_basis_ref
    )


def update_kernel(parts_ref, rows_ref, cols_ref, fold_ref, row_basis_ref, column_basis_ref, out_ref):
    count = rows_ref.shape[0] * band
    parts = [parts_ref[i : i + count] for i in range(0, parts_ref.shape[0], count)]
    while len(parts) > 1:
        parts = [sum(parts[i : i + 2]) for i in range(0, len(parts), 2)]
    out_ref[...] = lifted(
        parts[0], rows_ref, cols_ref, fold_ref, row_basis_ref, column_basis_ref
    ).astype(out_ref.dtype)


def call(kernel, shape, dtype, *operands):
    return pl.pallas_call(
        kernel,
        out_shape=jax.ShapeDtypeStruct(shape, dtype),
        compiler_params=pltpu.CompilerParams(vmem_limit_bytes=32 * 2**20),
        cost_estimate=pl.CostEstimate(
            flops=4 * 10**8, bytes_accessed=4 * 10**6, transcendentals=0
        ),
    )(*operands)


def spread(x, axis):
    size = lax.axis_size(axis)
    copies = jnp.broadcast_to(x[None], (size,) + x.shape).reshape((size * x.shape[0],) + x.shape[1:])
    return lax.all_to_all(copies, axis, 0, 0, tiled=True)


def product(hidden_rows, grad_rows):
    return dot(hidden_rows, grad_rows, ((0,), (0,)))


def gathered_gradient(hidden, out_grad):
    return product(hidden, lax.all_gather(out_grad, "tp", axis=0, tiled=True))


def line_gradient(hidden, out_grad):
    tok = out_grad.shape[0]
    me = lax.axis_index("tp")
    left = me < 2
    pair = me ^ 1
    cross = jnp.where(left, 2, 1)
    far = jnp.where(left, 3, 0)

    def rows_of(part):
        return lax.dynamic_slice_in_dim(hidden, part * tok, tok, 0)

    def send(x, perm):
        return lax.ppermute(x, "tp", perm)

    both_ways = [(0, 1), (1, 0), (2, 3), (3, 2)]
    across = [(1, 2), (2, 1)]
    outward = [(1, 0), (2, 3)]
    inward = [(0, 1), (3, 2)]

    pair_grad = send(out_grad, both_ways)
    cross_grad = send(out_grad, across)
    far_hidden = rows_of(far)
    sent_hidden, pair_grad = lax.optimization_barrier((far_hidden, pair_grad))
    far_grad = send(pair_grad, across)
    cross_grad = cross_grad + send(cross_grad, outward)
    helped_hidden = send(sent_hidden, inward)
    helped = send(product(helped_hidden, far_grad), outward)
    gradient = product(rows_of(me), out_grad) + product(rows_of(pair), pair_grad)
    gradient = gradient + product(rows_of(cross), cross_grad)
    return gradient + product(far_hidden, far_grad) + helped


def local(hidden, out_grad, momentum, band_rows, band_start_columns):
    row_count = hidden.shape[1]
    col_count = out_grad.shape[1]
    rows = jnp.repeat(band_rows.astype(jnp.int32) // band, order, axis=1)
    cols = jnp.repeat(band_start_columns.astype(jnp.int32) // band, order, axis=1)
    tables = (
        rows,
        cols,
        jnp.asarray(fold_matrix(col_count)),
        jnp.asarray(diagonal_blocks(row_count)),
        jnp.asarray(diagonal_blocks(col_count)),
    )
    gradient = (line_gradient if lax.axis_size("tp") == 4 else gathered_gradient)(hidden, out_grad)
    m = decay_rate * momentum[0] + gradient
    folded_shape = (row_count // steps, col_count // steps)
    bands = call(bands_kernel, folded_shape, jnp.float32, m, *tables)
    parts = spread(bands, "rep")
    momentum_out = call(remove_kernel, m.shape, jnp.float32, m, bands, *tables)
    update = call(update_kernel, m.shape, jnp.bfloat16, parts, *tables)
    return (momentum_out[None], update)


def solution(mesh):
    return jax.shard_map(
        local,
        mesh=mesh,
        in_specs=(
            P("rep", "tp"),
            P(("rep", "tp"), None),
            P("rep", "tp", None),
            P("tp", None),
            P("tp", None),
        ),
        out_specs=(P("rep", "tp", None), P("tp", None)),
        check_vma=False,
    )
```

```python
import functools

import jax
import jax.numpy as jnp
import numpy as np
from jax import lax
from jax.experimental import pallas as pl
from jax.experimental.pallas import tpu as pltpu
from jax.sharding import PartitionSpec as P

decay_rate = 0.9
order = 64
band = 16
steps = order // band


def basis_matrix():
    frequency = np.arange(order, dtype=np.float64)[:, None]
    sample_pos = np.arange(order, dtype=np.float64)[None, :]
    norm_scale = np.where(frequency == 0, np.sqrt(1.0 / order), np.sqrt(2.0 / order))
    return norm_scale * np.cos(np.pi * (sample_pos + 0.5) * frequency / order)


def halves_of(matrix):
    high = matrix.astype(jnp.bfloat16)
    low = (matrix - high.astype(matrix.dtype)).astype(jnp.bfloat16)
    return np.stack([high, low])


def diagonal_blocks(width):
    count = next(c for c in (4, 2, 1) if width % (c * order) == 0)
    return halves_of(np.kron(np.eye(count), basis_matrix()))


def fold_matrix(width):
    return np.kron(np.eye(width // order), np.kron(np.ones((steps, 1)), np.eye(band))).astype(jnp.bfloat16)


def split2(x):
    high = x.astype(jnp.bfloat16)
    return high, (x - high.astype(jnp.float32)).astype(jnp.bfloat16)


def split3(x):
    high, low = split2(x)
    rest = x - high.astype(jnp.float32) - low.astype(jnp.float32)
    return high, low, rest.astype(jnp.bfloat16)


def dot(a, b, dims=((1,), (0,))):
    return lax.dot_general(a, b, (dims, ((), ())), preferred_element_type=jnp.float32)


def dot3(a, b, dims=((1,), (0,))):
    return dot(a[0], b[0], dims) + (dot(a[0], b[1], dims) + dot(a[1], b[0], dims))


def on_rows(basis_ref, x, transposed):
    basis = basis_ref[0], basis_ref[1]
    side = basis[0].shape[0]
    dims = ((0,), (0,)) if transposed else ((1,), (0,))
    parts = [dot3(basis, split2(x[i : i + side]), dims) for i in range(0, x.shape[0], side)]
    return parts[0] if len(parts) == 1 else jnp.concatenate(parts, axis=0)


def on_columns(basis_ref, x, transposed):
    basis = basis_ref[0], basis_ref[1]
    side = basis[0].shape[0]
    dims = ((1,), (0,)) if transposed else ((1,), (1,))
    parts = [dot3(split2(x[:, i : i + side]), basis, dims) for i in range(0, x.shape[1], side)]
    return parts[0] if len(parts) == 1 else jnp.concatenate(parts, axis=1)


def column_mask(row, cols_ref, width):
    group = lax.rem(lax.broadcasted_iota(jnp.int32, (band, width), 1), order) // band
    return group == cols_ref[row : row + 1, :]


def lifted(folded, rows_ref, cols_ref, fold_ref, row_basis_ref, column_basis_ref):
    width = cols_ref.shape[1]
    spread = sum(dot(part, fold_ref[...], ((1,), (1,))) for part in split3(folded))
    pieces = []
    for row in range(rows_ref.shape[0]):
        inside = jnp.where(column_mask(row, cols_ref, width), spread[row * band : (row + 1) * band], 0.0)
        for step in range(steps):
            pieces.append(jnp.where(rows_ref[row : row + 1, :] == step, inside, 0.0))
    coefficients = jnp.concatenate(pieces, axis=0)
    return on_columns(column_basis_ref, on_rows(row_basis_ref, coefficients, True), True)


def bands_of(x, rows_ref, cols_ref, fold_ref, row_basis_ref, column_basis_ref):
    width = cols_ref.shape[1]
    coefficients = on_columns(column_basis_ref, on_rows(row_basis_ref, x, False), False)
    pieces = []
    for row in range(rows_ref.shape[0]):
        taken = jnp.zeros((band, width), jnp.float32)
        for step in range(steps):
            at = row * order + step * band
            taken = jnp.where(rows_ref[row : row + 1, :] == step, coefficients[at : at + band], taken)
        pieces.append(jnp.where(column_mask(row, cols_ref, width), taken, 0.0))
    taken = jnp.concatenate(pieces, axis=0)
    return sum(dot(part, fold_ref[...]) for part in split3(taken))


def bands_kernel(m_ref, *refs):
    *table_refs, bands_ref = refs
    bands_ref[...] = bands_of(m_ref[...], *table_refs)


def last_rows_kernel(m_ref, hidden_ref, *refs):
    *grad_refs, rows_ref, cols_ref, fold_ref, row_basis_ref, column_basis_ref, out_ref, bands_ref = refs
    grad = sum(ref[...] for ref in grad_refs[1:]) + grad_refs[0][...]
    out_ref[...] = m_ref[...] + dot(hidden_ref[...], grad, ((0,), (0,)))
    bands_ref[...] = bands_of(out_ref[...], rows_ref, cols_ref, fold_ref, row_basis_ref, column_basis_ref)


def remove_kernel(count, *refs):
    m_refs, band_refs, (*table_refs, out_ref) = refs[:count], refs[count : 2 * count], refs[2 * count :]
    bands = pair_sum([ref[...] for ref in band_refs])
    out_ref[...] = pair_sum([ref[...] for ref in m_refs]) - lifted(bands, *table_refs)


def update_kernel(*refs):
    *part_refs, rows_ref, cols_ref, fold_ref, row_basis_ref, column_basis_ref, out_ref = refs
    parts = [ref[...] for ref in part_refs]
    out_ref[...] = lifted(
        pair_sum(parts), rows_ref, cols_ref, fold_ref, row_basis_ref, column_basis_ref
    ).astype(out_ref.dtype)


def pair_sum(parts):
    while len(parts) > 1:
        parts = [sum(parts[i + 1 : i + 2], parts[i]) for i in range(0, len(parts), 2)]
    return parts[0]


def call(kernel, out_shapes, *operands):
    return pl.pallas_call(
        kernel,
        out_shape=out_shapes,
        compiler_params=pltpu.CompilerParams(vmem_limit_bytes=32 * 2**20),
        cost_estimate=pl.CostEstimate(flops=4 * 10**8, bytes_accessed=4 * 10**6, transcendentals=0),
    )(*operands)


def spread_sum(x, axis):
    size = lax.axis_size(axis)
    if size & (size - 1):
        return [lax.psum(x, axis)]
    stride, parts = 1, [x]
    while stride < size:
        count = min(8, size // stride)
        x = pair_sum(parts)
        parts = [x] + [
            lax.ppermute(x, axis, [(i, i ^ (stride * k)) for i in range(size)]) for k in range(1, count)
        ]
        stride *= count
    return parts


def product(hidden_rows, grad_rows):
    return dot(hidden_rows, grad_rows, ((0,), (0,)))


def after(x, *others):
    return lax.optimization_barrier((x, *others))[0]


def gathered(hidden, out_grad, carried, tables, make_tables, band_rows, band_start_columns):
    m = carried + product(hidden, lax.all_gather(out_grad, "tp", axis=0, tiled=True))
    folded = jax.ShapeDtypeStruct((m.shape[0] // steps, m.shape[1] // steps), jnp.float32)
    return [m], [call(bands_kernel, folded, m, *tables)]


def lined(hidden, out_grad, carried, tables, make_tables, band_rows, band_start_columns):
    tok = out_grad.shape[0]
    me = lax.axis_index("tp")
    left = me < 2
    middle = (me == 1) | (me == 2)
    cross = jnp.where(left, 2, 1)
    far = jnp.where(left, 3, 0)
    head = tok - max(tok // 4 // 128 * 128, 16)
    chunks = ((0, head), (head, tok))

    def rows_of(part, chunk=(0, tok)):
        return lax.dynamic_slice_in_dim(hidden, part * tok + chunk[0], chunk[1] - chunk[0], 0)

    def send(x, perm):
        return lax.ppermute(x, "tp", perm)

    both_ways = [(0, 1), (1, 0), (2, 3), (3, 2)]
    across = [(1, 2), (2, 1)]
    outward = [(1, 0), (2, 3)]
    inward = [(0, 1), (3, 2)]

    own = [out_grad[slice(*c)] for c in chunks]
    pair_grad = [send(own[0], both_ways), None]
    cross_grad = [send(own[0], across), None]
    pair_grad[1] = send(own[1], both_ways)
    cross_grad[1] = send(own[1], across)
    places = jnp.concatenate([band_rows, band_start_columns], axis=0)
    places = send(after(places, pair_grad[0]), inward)
    end_tables = make_tables(*(places[i * band_rows.shape[0] :][: band_rows.shape[0]] for i in range(2)))
    pair_grad[1] = after(pair_grad[1], cross_grad[0])
    far_grad = [send(x, across) for x in pair_grad]
    passed_grad = [send(x, outward) for x in cross_grad]
    helped_hidden = [send(after(rows_of(far, c), pair_grad[1]), inward) for c in chunks]

    m = carried + product(rows_of(me), out_grad)
    for c, pair_part, cross_part in zip(chunks, pair_grad, cross_grad):
        m = m + product(rows_of(me ^ 1, c), pair_part) + product(rows_of(cross, c), cross_part)
    late = jnp.where(middle, far, cross)
    m = m + product(rows_of(late, chunks[0]), far_grad[0] + passed_grad[0])
    helped = product(helped_hidden[0], far_grad[0])
    far_grad[1] = after(far_grad[1], passed_grad[1], m, helped, tables, end_tables)

    full = jax.ShapeDtypeStruct(m.shape, jnp.float32)
    folded = jax.ShapeDtypeStruct((m.shape[0] // steps, m.shape[1] // steps), jnp.float32)
    helped, helped_bands = call(
        last_rows_kernel, (full, folded), helped, helped_hidden[1], far_grad[1], *end_tables
    )
    helped_bands = send(helped_bands, outward)
    helped = send(after(helped, helped_bands), outward)
    m, bands = call(
        last_rows_kernel, (full, folded), m, rows_of(late, chunks[1]), far_grad[1], passed_grad[1], *tables
    )
    return [m, helped], [bands, helped_bands]


def local(hidden, out_grad, momentum, band_rows, band_start_columns):
    row_count = hidden.shape[1]
    col_count = out_grad.shape[1]
    matrices = tuple(
        jnp.asarray(x) for x in (fold_matrix(col_count), diagonal_blocks(row_count), diagonal_blocks(col_count))
    )

    def make_tables(*places):
        return tuple(jnp.repeat(x.astype(jnp.int32) // band, order, axis=1) for x in places) + matrices

    tables = make_tables(band_rows, band_start_columns)
    form = lined if lax.axis_size("tp") == 4 else gathered
    m_parts, band_parts = form(
        hidden, out_grad, decay_rate * momentum[0], tables, make_tables, band_rows, band_start_columns
    )
    parts = spread_sum(pair_sum(band_parts), "rep")
    shape = (row_count, col_count)
    momentum_out = call(
        functools.partial(remove_kernel, len(m_parts)),
        jax.ShapeDtypeStruct(shape, jnp.float32),
        *m_parts,
        *band_parts,
        *tables,
    )
    update = call(update_kernel, jax.ShapeDtypeStruct(shape, jnp.bfloat16), *parts, *tables)
    return (momentum_out[None], update)


def solution(mesh):
    return jax.shard_map(
        local,
        mesh=mesh,
        in_specs=(
            P("rep", "tp"),
            P(("rep", "tp"), None),
            P("rep", "tp", None),
            P("tp", None),
            P("tp", None),
        ),
        out_specs=(P("rep", "tp", None), P("tp", None)),
        check_vma=False,
    )
```

```python
import functools

import jax
import jax.numpy as jnp
import numpy as np
from jax import lax
from jax.experimental import pallas as pl
from jax.experimental.pallas import tpu as pltpu
from jax.sharding import PartitionSpec as P

decay_rate = 0.9
order = 64
band = 16
steps = order // band


def basis_matrix():
    frequency = np.arange(order, dtype=np.float64)[:, None]
    sample_pos = np.arange(order, dtype=np.float64)[None, :]
    norm_scale = np.where(frequency == 0, np.sqrt(1.0 / order), np.sqrt(2.0 / order))
    return norm_scale * np.cos(np.pi * (sample_pos + 0.5) * frequency / order)


def halves_of(matrix):
    high = matrix.astype(jnp.bfloat16)
    low = (matrix - high.astype(matrix.dtype)).astype(jnp.bfloat16)
    return np.stack([high, low])


def diagonal_blocks(width):
    count = next(c for c in (4, 2, 1) if width % (c * order) == 0)
    return halves_of(np.kron(np.eye(count), basis_matrix()))


def fold_matrix(width):
    return np.kron(np.eye(width // order), np.kron(np.ones((steps, 1)), np.eye(band))).astype(jnp.bfloat16)


def split2(x):
    high = x.astype(jnp.bfloat16)
    return high, (x - high.astype(jnp.float32)).astype(jnp.bfloat16)


def split3(x):
    high, low = split2(x)
    rest = x - high.astype(jnp.float32) - low.astype(jnp.float32)
    return high, low, rest.astype(jnp.bfloat16)


def dot(a, b, dims=((1,), (0,))):
    return lax.dot_general(a, b, (dims, ((), ())), preferred_element_type=jnp.float32)


def dot3(a, b, dims=((1,), (0,))):
    return dot(a[0], b[0], dims) + (dot(a[0], b[1], dims) + dot(a[1], b[0], dims))


def on_rows(basis_ref, x, transposed):
    basis = basis_ref[0], basis_ref[1]
    side = basis[0].shape[0]
    dims = ((0,), (0,)) if transposed else ((1,), (0,))
    parts = [dot3(basis, split2(x[i : i + side]), dims) for i in range(0, x.shape[0], side)]
    return parts[0] if len(parts) == 1 else jnp.concatenate(parts, axis=0)


def on_columns(basis_ref, x, transposed):
    basis = basis_ref[0], basis_ref[1]
    side = basis[0].shape[0]
    dims = ((1,), (0,)) if transposed else ((1,), (1,))
    parts = [dot3(split2(x[:, i : i + side]), basis, dims) for i in range(0, x.shape[1], side)]
    return parts[0] if len(parts) == 1 else jnp.concatenate(parts, axis=1)


def column_mask(row, cols_ref, width):
    group = lax.rem(lax.broadcasted_iota(jnp.int32, (band, width), 1), order) // band
    return group == cols_ref[row : row + 1, :]


def lifted(folded, rows_ref, cols_ref, fold_ref, row_basis_ref, column_basis_ref):
    width = cols_ref.shape[1]
    spread = sum(dot(part, fold_ref[...], ((1,), (1,))) for part in split3(folded))
    pieces = []
    for row in range(rows_ref.shape[0]):
        inside = jnp.where(column_mask(row, cols_ref, width), spread[row * band : (row + 1) * band], 0.0)
        for step in range(steps):
            pieces.append(jnp.where(rows_ref[row : row + 1, :] == step, inside, 0.0))
    coefficients = jnp.concatenate(pieces, axis=0)
    return on_columns(column_basis_ref, on_rows(row_basis_ref, coefficients, True), True)


def bands_of(x, rows_ref, cols_ref, fold_ref, row_basis_ref, column_basis_ref):
    width = cols_ref.shape[1]
    coefficients = on_columns(column_basis_ref, on_rows(row_basis_ref, x, False), False)
    pieces = []
    for row in range(rows_ref.shape[0]):
        taken = jnp.zeros((band, width), jnp.float32)
        for step in range(steps):
            at = row * order + step * band
            taken = jnp.where(rows_ref[row : row + 1, :] == step, coefficients[at : at + band], taken)
        pieces.append(jnp.where(column_mask(row, cols_ref, width), taken, 0.0))
    taken = jnp.concatenate(pieces, axis=0)
    return sum(dot(part, fold_ref[...]) for part in split3(taken))


def bands_kernel(m_ref, *refs):
    *table_refs, bands_ref = refs
    bands_ref[...] = bands_of(m_ref[...], *table_refs)


def last_rows_kernel(m_ref, hidden_ref, grad_ref, *refs):
    *table_refs, out_ref, bands_ref = refs
    hidden = hidden_ref[hidden_ref.shape[0] - grad_ref.shape[0] :]
    out_ref[...] = m_ref[...] + dot(hidden, grad_ref[...], ((0,), (0,)))
    bands_ref[...] = bands_of(out_ref[...], *table_refs)


def remove_kernel(count, *refs):
    m_refs, band_refs, (*table_refs, out_ref) = refs[:count], refs[count : 2 * count], refs[2 * count :]
    bands = pair_sum([ref[...] for ref in band_refs])
    out_ref[...] = pair_sum([ref[...] for ref in m_refs]) - lifted(bands, *table_refs)


def update_kernel(*refs):
    *part_refs, rows_ref, cols_ref, fold_ref, row_basis_ref, column_basis_ref, out_ref = refs
    parts = [ref[...] for ref in part_refs]
    out_ref[...] = lifted(
        pair_sum(parts), rows_ref, cols_ref, fold_ref, row_basis_ref, column_basis_ref
    ).astype(out_ref.dtype)


def pair_sum(parts):
    while len(parts) > 1:
        parts = [sum(parts[i + 1 : i + 2], parts[i]) for i in range(0, len(parts), 2)]
    return parts[0]


def call(kernel, out_shapes, *operands):
    return pl.pallas_call(
        kernel,
        out_shape=out_shapes,
        compiler_params=pltpu.CompilerParams(vmem_limit_bytes=32 * 2**20),
        cost_estimate=pl.CostEstimate(flops=4 * 10**8, bytes_accessed=4 * 10**6, transcendentals=0),
    )(*operands)


def spread_sum(x, axis):
    size = lax.axis_size(axis)
    if size & (size - 1):
        return [lax.psum(x, axis)]
    stride, parts = 1, [x]
    while stride < size:
        count = min(8, size // stride)
        x = pair_sum(parts)
        parts = [x] + [
            lax.ppermute(x, axis, [(i, i ^ (stride * k)) for i in range(size)]) for k in range(1, count)
        ]
        stride *= count
    return parts


def product(hidden_rows, grad_rows):
    return dot(hidden_rows, grad_rows, ((0,), (0,)))


def after(x, *others):
    return lax.optimization_barrier((x, *others))[0]


def gathered(hidden, out_grad, carried, tables, make_tables, band_rows, band_start_columns):
    m = carried + product(hidden, lax.all_gather(out_grad, "tp", axis=0, tiled=True))
    folded = jax.ShapeDtypeStruct((m.shape[0] // steps, m.shape[1] // steps), jnp.float32)
    return [m], [call(bands_kernel, folded, m, *tables)]


def lined(hidden, out_grad, carried, tables, make_tables, band_rows, band_start_columns):
    tok = out_grad.shape[0]
    me = lax.axis_index("tp")
    left = me < 2
    cross = jnp.where(left, 2, 1)
    far = jnp.where(left, 3, 0)
    first = max(tok // 3 // 128 * 128, 16)
    handed = tok - first

    def rows_of(part, start=0, stop=tok):
        return lax.dynamic_slice_in_dim(hidden, part * tok + start, stop - start, 0)

    def send(x, perm):
        return lax.ppermute(x, "tp", perm)

    both_ways = [(0, 1), (1, 0), (2, 3), (3, 2)]
    across = [(1, 2), (2, 1)]
    outward = [(1, 0), (2, 3)]
    inward = [(0, 1), (3, 2)]

    cross_grad = send(out_grad, across)
    pair_head = send(out_grad[:first], both_ways)
    m = carried + product(rows_of(me), out_grad)
    pair_rest = send(after(out_grad, m)[first:], both_ways)

    far_head = send(pair_head, across)
    places = jnp.concatenate([band_rows, band_start_columns], axis=0)
    places = send(after(places, pair_head), inward)
    end_tables = make_tables(*(places[i * band_rows.shape[0] :][: band_rows.shape[0]] for i in range(2)))
    pair_rest = after(pair_rest, pair_head)
    far_rest = send(pair_rest, across)
    helped_hidden = jnp.concatenate([rows_of(cross, handed), rows_of(far)], axis=0)
    helped_hidden = send(after(helped_hidden, pair_rest), inward)
    cross_grad = after(cross_grad, pair_rest)
    passed_grad = send(cross_grad[:handed], outward)

    m = m + product(rows_of(me ^ 1, 0, first), pair_head) + product(rows_of(me ^ 1, first), pair_rest)
    m = m + product(rows_of(cross), cross_grad)
    m = m + product(rows_of(cross, 0, handed), passed_grad) + product(rows_of(far, 0, first), far_head)
    helped = product(helped_hidden[: tok - handed], cross_grad[handed:])
    helped = helped + product(helped_hidden[tok - handed :][:first], far_head)
    far_rest = after(far_rest, m, helped, tables, end_tables)

    full = jax.ShapeDtypeStruct(m.shape, jnp.float32)
    folded = jax.ShapeDtypeStruct((m.shape[0] // steps, m.shape[1] // steps), jnp.float32)
    helped, helped_bands = call(
        last_rows_kernel, (full, folded), helped, helped_hidden, far_rest, *end_tables
    )
    helped_bands = send(helped_bands, outward)
    m, bands = call(last_rows_kernel, (full, folded), m, rows_of(far, first), far_rest, *tables)
    helped_bands, bands = lax.optimization_barrier((helped_bands, bands))
    helped = send(after(helped, helped_bands), outward)
    return [m, helped], [bands, helped_bands]


def local(hidden, out_grad, momentum, band_rows, band_start_columns):
    row_count = hidden.shape[1]
    col_count = out_grad.shape[1]
    matrices = tuple(
        jnp.asarray(x) for x in (fold_matrix(col_count), diagonal_blocks(row_count), diagonal_blocks(col_count))
    )

    def make_tables(*places):
        return tuple(jnp.repeat(x.astype(jnp.int32) // band, order, axis=1) for x in places) + matrices

    tables = make_tables(band_rows, band_start_columns)
    form = lined if lax.axis_size("tp") == 4 else gathered
    m_parts, band_parts = form(
        hidden, out_grad, decay_rate * momentum[0], tables, make_tables, band_rows, band_start_columns
    )
    parts = spread_sum(pair_sum(band_parts), "rep")
    shape = (row_count, col_count)
    momentum_out = call(
        functools.partial(remove_kernel, len(m_parts)),
        jax.ShapeDtypeStruct(shape, jnp.float32),
        *m_parts,
        *band_parts,
        *tables,
    )
    update = call(update_kernel, jax.ShapeDtypeStruct(shape, jnp.bfloat16), *parts, *tables)
    return (momentum_out[None], update)


def solution(mesh):
    return jax.shard_map(
        local,
        mesh=mesh,
        in_specs=(
            P("rep", "tp"),
            P(("rep", "tp"), None),
            P("rep", "tp", None),
            P("tp", None),
            P("tp", None),
        ),
        out_specs=(P("rep", "tp", None), P("tp", None)),
        check_vma=False,
    )
```

```python
import functools

import jax
import jax.numpy as jnp
import numpy as np
from jax import lax
from jax.experimental import pallas as pl
from jax.experimental.pallas import tpu as pltpu
from jax.sharding import PartitionSpec as P

decay_rate = 0.9
order = 64
band = 16
steps = order // band


def basis_matrix():
    frequency = np.arange(order, dtype=np.float64)[:, None]
    sample_pos = np.arange(order, dtype=np.float64)[None, :]
    norm_scale = np.where(frequency == 0, np.sqrt(1.0 / order), np.sqrt(2.0 / order))
    return norm_scale * np.cos(np.pi * (sample_pos + 0.5) * frequency / order)


def halves_of(matrix):
    high = matrix.astype(jnp.bfloat16)
    low = (matrix - high.astype(matrix.dtype)).astype(jnp.bfloat16)
    return np.stack([high, low])


def diagonal_blocks(width):
    count = next(c for c in (4, 2, 1) if width % (c * order) == 0)
    return halves_of(np.kron(np.eye(count), basis_matrix()))


def fold_matrix(width):
    return np.kron(np.eye(width // order), np.kron(np.ones((steps, 1)), np.eye(band))).astype(jnp.bfloat16)


def split2(x):
    high = x.astype(jnp.bfloat16)
    return high, (x - high.astype(jnp.float32)).astype(jnp.bfloat16)


def split3(x):
    high, low = split2(x)
    rest = x - high.astype(jnp.float32) - low.astype(jnp.float32)
    return high, low, rest.astype(jnp.bfloat16)


def dot(a, b, dims=((1,), (0,))):
    return lax.dot_general(a, b, (dims, ((), ())), preferred_element_type=jnp.float32)


def dot3(a, b, dims=((1,), (0,))):
    return dot(a[0], b[0], dims) + (dot(a[0], b[1], dims) + dot(a[1], b[0], dims))


def on_rows(basis_ref, x, transposed):
    basis = basis_ref[0], basis_ref[1]
    side = basis[0].shape[0]
    dims = ((0,), (0,)) if transposed else ((1,), (0,))
    parts = [dot3(basis, split2(x[i : i + side]), dims) for i in range(0, x.shape[0], side)]
    return parts[0] if len(parts) == 1 else jnp.concatenate(parts, axis=0)


def on_columns(basis_ref, x, transposed):
    basis = basis_ref[0], basis_ref[1]
    side = basis[0].shape[0]
    dims = ((1,), (0,)) if transposed else ((1,), (1,))
    parts = [dot3(split2(x[:, i : i + side]), basis, dims) for i in range(0, x.shape[1], side)]
    return parts[0] if len(parts) == 1 else jnp.concatenate(parts, axis=1)


def place_of_blocks(places_ref, row, width):
    block = lax.broadcasted_iota(jnp.int32, (1, width), 1) // order
    out = jnp.zeros((1, width), jnp.int32)
    for column in range(width // order):
        out = jnp.where(block == column, places_ref[row, column], out)
    return out


def masks_of(places_ref, width):
    count = places_ref.shape[0] // 2
    group = lax.rem(lax.broadcasted_iota(jnp.int32, (band, width), 1), order) // band * band
    rows = [place_of_blocks(places_ref, row, width) for row in range(count)]
    return [(at, group == place_of_blocks(places_ref, count + row, width)) for row, at in enumerate(rows)]


def lifted(folded, places_ref, fold_ref, row_basis_ref, column_basis_ref):
    spread = sum(dot(part, fold_ref[...], ((1,), (1,))) for part in split3(folded))
    pieces = []
    for row, (at, inside) in enumerate(masks_of(places_ref, fold_ref.shape[0])):
        part = jnp.where(inside, spread[row * band : (row + 1) * band], 0.0)
        pieces += [jnp.where(at == step * band, part, 0.0) for step in range(steps)]
    coefficients = jnp.concatenate(pieces, axis=0)
    return on_columns(column_basis_ref, on_rows(row_basis_ref, coefficients, True), True)


def bands_of(x, places_ref, fold_ref, row_basis_ref, column_basis_ref):
    coefficients = on_columns(column_basis_ref, on_rows(row_basis_ref, x, False), False)
    pieces = []
    for row, (at, inside) in enumerate(masks_of(places_ref, fold_ref.shape[0])):
        taken = jnp.zeros(inside.shape, jnp.float32)
        for step in range(steps):
            start = row * order + step * band
            taken = jnp.where(at == step * band, coefficients[start : start + band], taken)
        pieces.append(jnp.where(inside, taken, 0.0))
    taken = jnp.concatenate(pieces, axis=0)
    return sum(dot(part, fold_ref[...]) for part in split3(taken))


def bands_kernel(m_ref, *refs):
    *table_refs, bands_ref = refs
    bands_ref[...] = bands_of(m_ref[...], *table_refs)


def last_rows_kernel(m_ref, hidden_ref, grad_ref, *refs):
    *table_refs, out_ref, bands_ref = refs
    hidden = hidden_ref[hidden_ref.shape[0] - grad_ref.shape[0] :]
    out_ref[...] = m_ref[...] + dot(hidden, grad_ref[...], ((0,), (0,)))
    bands_ref[...] = bands_of(out_ref[...], *table_refs)


def remove_kernel(count, *refs):
    m_refs, band_refs, (*table_refs, out_ref) = refs[:count], refs[count : 2 * count], refs[2 * count :]
    bands = pair_sum([ref[...] for ref in band_refs])
    out_ref[...] = pair_sum([ref[...] for ref in m_refs]) - lifted(bands, *table_refs)


def update_kernel(*refs):
    *part_refs, places_ref, fold_ref, row_basis_ref, column_basis_ref, out_ref = refs
    parts = [ref[...] for ref in part_refs]
    bands = pair_sum(parts)
    out_ref[...] = lifted(bands, places_ref, fold_ref, row_basis_ref, column_basis_ref).astype(out_ref.dtype)


def pair_sum(parts):
    while len(parts) > 1:
        parts = [sum(parts[i + 1 : i + 2], parts[i]) for i in range(0, len(parts), 2)]
    return parts[0]


def call(kernel, out_shapes, *operands):
    spaces = [pltpu.SMEM if x.dtype == jnp.int32 else pltpu.VMEM for x in operands]
    return pl.pallas_call(
        kernel,
        out_shape=out_shapes,
        in_specs=[pl.BlockSpec(memory_space=space) for space in spaces],
        compiler_params=pltpu.CompilerParams(vmem_limit_bytes=32 * 2**20),
        cost_estimate=pl.CostEstimate(flops=4 * 10**8, bytes_accessed=4 * 10**6, transcendentals=0),
    )(*operands)


def spread_sum(x, axis):
    size = lax.axis_size(axis)
    if size & (size - 1):
        return [lax.psum(x, axis)]
    stride, parts = 1, [x]
    while stride < size:
        count = min(4, size // stride)
        x = pair_sum(parts)
        parts = [x] + [
            lax.ppermute(x, axis, [(i, i ^ (stride * k)) for i in range(size)]) for k in range(1, count)
        ]
        stride *= count
    return parts


def product(hidden_rows, grad_rows):
    return dot(hidden_rows, grad_rows, ((0,), (0,)))


def after(x, *others):
    return lax.optimization_barrier((x, *others))[0]


def gathered(hidden, out_grad, carried, places, matrices):
    m = carried + product(hidden, lax.all_gather(out_grad, "tp", axis=0, tiled=True))
    folded = jax.ShapeDtypeStruct((m.shape[0] // steps, m.shape[1] // steps), jnp.float32)
    return [m], [call(bands_kernel, folded, m, places, *matrices)]


def lined(hidden, out_grad, carried, places, matrices):
    tok = out_grad.shape[0]
    me = lax.axis_index("tp")
    left = me < 2
    cross = jnp.where(left, 2, 1)
    far = jnp.where(left, 3, 0)
    first = max(tok // 4 // 128 * 128, 16)
    handed = tok - max(tok // 3 // 128 * 128, 16)

    def rows_of(part, start=0, stop=tok):
        return lax.dynamic_slice_in_dim(hidden, part * tok + start, stop - start, 0)

    def send(x, perm):
        return lax.ppermute(x, "tp", perm)

    both_ways = [(0, 1), (1, 0), (2, 3), (3, 2)]
    across = [(1, 2), (2, 1)]
    over_one = [(0, 2), (3, 1)]
    outward = [(1, 0), (2, 3)]
    inward = [(0, 1), (3, 2)]

    head, rest = out_grad[:first], out_grad[first:]
    cross_grad = send(out_grad, across)
    far_head = send(head, over_one)
    pair_rest = send(rest, both_ways)
    m = carried + product(rows_of(me), out_grad)
    helped_hidden = jnp.concatenate([rows_of(cross, handed), rows_of(far)], axis=0)
    pair_rest, m, head, helped_hidden = lax.optimization_barrier((pair_rest, m, head, helped_hidden))
    far_rest = send(pair_rest, across)
    pair_head = send(head, both_ways)
    helped_hidden = send(helped_hidden, inward)
    end_places = send(after(places, pair_head), inward)
    passed_grad = send(cross_grad[:handed], outward)

    m = m + product(rows_of(me ^ 1, 0, first), pair_head) + product(rows_of(me ^ 1, first), pair_rest)
    m = m + product(rows_of(cross), cross_grad) + product(rows_of(far, 0, first), far_head)
    m = m + product(rows_of(cross, 0, handed), passed_grad)
    helped = product(helped_hidden[: tok - handed], cross_grad[handed:])
    helped = helped + product(helped_hidden[tok - handed :][:first], far_head)
    far_rest = after(far_rest, m, helped)

    full = jax.ShapeDtypeStruct(m.shape, jnp.float32)
    folded = jax.ShapeDtypeStruct((m.shape[0] // steps, m.shape[1] // steps), jnp.float32)
    helped, helped_bands = call(
        last_rows_kernel, (full, folded), helped, helped_hidden, far_rest, end_places, *matrices
    )
    m, helped_bands = lax.optimization_barrier((m, helped_bands))
    sent_bands = send(helped_bands, outward)
    m, bands = call(last_rows_kernel, (full, folded), m, rows_of(far, first), far_rest, places, *matrices)
    helped_bands, bands = lax.optimization_barrier((sent_bands, bands))
    helped = send(after(helped, helped_bands), outward)
    return [m, helped], [bands, helped_bands]


def local(hidden, out_grad, momentum, band_rows, band_start_columns):
    row_count = hidden.shape[1]
    col_count = out_grad.shape[1]
    matrices = tuple(
        jnp.asarray(x) for x in (fold_matrix(col_count), diagonal_blocks(row_count), diagonal_blocks(col_count))
    )
    places = jnp.concatenate([band_rows, band_start_columns], axis=0).astype(jnp.int32)
    form = lined if lax.axis_size("tp") == 4 else gathered
    m_parts, band_parts = form(hidden, out_grad, decay_rate * momentum[0], places, matrices)
    parts = spread_sum(pair_sum(band_parts), "rep")
    shape = (row_count, col_count)
    momentum_out = call(
        functools.partial(remove_kernel, len(m_parts)),
        jax.ShapeDtypeStruct(shape, jnp.float32),
        *m_parts,
        *band_parts,
        places,
        *matrices,
    )
    update = call(update_kernel, jax.ShapeDtypeStruct(shape, jnp.bfloat16), *parts, places, *matrices)
    return (momentum_out[None], update)


def solution(mesh):
    return jax.shard_map(
        local,
        mesh=mesh,
        in_specs=(
            P("rep", "tp"),
            P(("rep", "tp"), None),
            P("rep", "tp", None),
            P("tp", None),
            P("tp", None),
        ),
        out_specs=(P("rep", "tp", None), P("tp", None)),
        check_vma=False,
    )
```

```python
import functools

import jax
import jax.numpy as jnp
import numpy as np
from jax import lax
from jax.experimental import pallas as pl
from jax.experimental.pallas import tpu as pltpu
from jax.sharding import PartitionSpec as P

decay_rate = 0.9
order = 64
band = 16
steps = order // band
place_rows = 16


def basis_matrix():
    frequency = np.arange(order, dtype=np.float64)[:, None]
    sample_pos = np.arange(order, dtype=np.float64)[None, :]
    norm_scale = np.where(frequency == 0, np.sqrt(1.0 / order), np.sqrt(2.0 / order))
    return norm_scale * np.cos(np.pi * (sample_pos + 0.5) * frequency / order)


def halves_of(matrix):
    high = matrix.astype(jnp.bfloat16)
    low = (matrix - high.astype(matrix.dtype)).astype(jnp.bfloat16)
    return np.stack([high, low])


def diagonal_blocks(width):
    count = next(c for c in (4, 2, 1) if width % (c * order) == 0)
    return halves_of(np.kron(np.eye(count), basis_matrix()))


def fold_matrix(width):
    return np.kron(np.eye(width // order), np.kron(np.ones((steps, 1)), np.eye(band))).astype(jnp.bfloat16)


def split2(x):
    high = x.astype(jnp.bfloat16)
    return high, (x - high.astype(jnp.float32)).astype(jnp.bfloat16)


def split3(x):
    high, low = split2(x)
    rest = x - high.astype(jnp.float32) - low.astype(jnp.float32)
    return high, low, rest.astype(jnp.bfloat16)


def dot(a, b, dims=((1,), (0,))):
    return lax.dot_general(a, b, (dims, ((), ())), preferred_element_type=jnp.float32)


def dot3(a, b, dims=((1,), (0,))):
    return dot(a[0], b[0], dims) + (dot(a[0], b[1], dims) + dot(a[1], b[0], dims))


def on_rows(basis_ref, x, transposed):
    basis = basis_ref[0], basis_ref[1]
    side = basis[0].shape[0]
    dims = ((0,), (0,)) if transposed else ((1,), (0,))
    parts = [dot3(basis, split2(x[i : i + side]), dims) for i in range(0, x.shape[0], side)]
    return parts[0] if len(parts) == 1 else jnp.concatenate(parts, axis=0)


def on_columns(basis_ref, x, transposed):
    basis = basis_ref[0], basis_ref[1]
    side = basis[0].shape[0]
    dims = ((1,), (0,)) if transposed else ((1,), (1,))
    parts = [dot3(split2(x[:, i : i + side]), basis, dims) for i in range(0, x.shape[1], side)]
    return parts[0] if len(parts) == 1 else jnp.concatenate(parts, axis=1)


def masks_of(places, count):
    width = places.shape[1]
    column = lax.rem(lax.broadcasted_iota(jnp.int32, (band, width), 1), order).astype(jnp.float32)
    masks = []
    for row in range(count):
        start = places[count + row : count + row + 1, :]
        masks.append((places[row : row + 1, :], (column >= start) & (column < start + band)))
    return masks


def lifted(folded, places, fold_ref, row_basis_ref, column_basis_ref):
    spread = sum(dot(part, fold_ref[...], ((1,), (1,))) for part in split3(folded))
    pieces = []
    for row, (at, inside) in enumerate(masks_of(places, folded.shape[0] // band)):
        part = jnp.where(inside, spread[row * band : (row + 1) * band], 0.0)
        pieces += [jnp.where(at == step * band, part, 0.0) for step in range(steps)]
    coefficients = jnp.concatenate(pieces, axis=0)
    return on_columns(column_basis_ref, on_rows(row_basis_ref, coefficients, True), True)


def bands_of(x, places, fold_ref, row_basis_ref, column_basis_ref):
    coefficients = on_columns(column_basis_ref, on_rows(row_basis_ref, x, False), False)
    pieces = []
    for row, (at, inside) in enumerate(masks_of(places, x.shape[0] // order)):
        taken = jnp.zeros(inside.shape, jnp.float32)
        for step in range(steps):
            start = row * order + step * band
            taken = jnp.where(at == step * band, coefficients[start : start + band], taken)
        pieces.append(jnp.where(inside, taken, 0.0))
    taken = jnp.concatenate(pieces, axis=0)
    return sum(dot(part, fold_ref[...]) for part in split3(taken))


def bands_kernel(m_ref, places_ref, *refs):
    *matrix_refs, bands_ref = refs
    bands_ref[...] = bands_of(m_ref[...], places_ref[...], *matrix_refs)


def helped_kernel(swapped_ref, cross_ref, far_ref, *refs):
    *matrix_refs, out_ref, bands_ref = refs
    handed, side = swapped_ref.shape[0] - place_rows, out_ref.shape[0]
    alone = cross_ref.shape[0] - handed
    out_ref[...] = (
        dot(swapped_ref[:alone, :side], cross_ref[handed:], ((0,), (0,)))
        + dot(swapped_ref[alone:handed, :side], far_ref[: handed - alone], ((0,), (0,)))
        + dot(swapped_ref[:handed, side:], far_ref[handed - alone :], ((0,), (0,)))
    )
    bands_ref[...] = bands_of(out_ref[...], swapped_ref[handed:].astype(jnp.float32), *matrix_refs)


def last_rows_kernel(m_ref, far_hidden_ref, far_ref, cross_hidden_ref, swapped_ref, places_ref, *refs):
    *matrix_refs, out_ref, bands_ref = refs
    out_ref[...] = (
        m_ref[...]
        + dot(far_hidden_ref[...], far_ref[...], ((0,), (0,)))
        + dot(cross_hidden_ref[...], swapped_ref[: cross_hidden_ref.shape[0]], ((0,), (0,)))
    )
    bands_ref[...] = bands_of(out_ref[...], places_ref[...], *matrix_refs)


def remove_kernel(count, *refs):
    m_refs, band_refs = refs[:count], refs[count : 2 * count]
    places_ref, *matrix_refs, out_ref = refs[2 * count :]
    bands = pair_sum([ref[...] for ref in band_refs])
    out_ref[...] = pair_sum([ref[...] for ref in m_refs]) - lifted(bands, places_ref[...], *matrix_refs)


def update_kernel(*refs):
    *part_refs, places_ref, fold_ref, row_basis_ref, column_basis_ref, out_ref = refs
    parts = [ref[...] for ref in part_refs]
    bands = pair_sum(parts)
    out_ref[...] = lifted(bands, places_ref[...], fold_ref, row_basis_ref, column_basis_ref).astype(out_ref.dtype)


def pair_sum(parts):
    while len(parts) > 1:
        parts = [sum(parts[i + 1 : i + 2], parts[i]) for i in range(0, len(parts), 2)]
    return parts[0]


def call(kernel, out_shapes, *operands):
    return pl.pallas_call(
        kernel,
        out_shape=out_shapes,
        compiler_params=pltpu.CompilerParams(vmem_limit_bytes=32 * 2**20),
        cost_estimate=pl.CostEstimate(flops=4 * 10**8, bytes_accessed=4 * 10**6, transcendentals=0),
    )(*operands)


def spread_sum(x, axis):
    size = lax.axis_size(axis)
    if size & (size - 1):
        return [lax.psum(x, axis)]
    stride, parts = 1, [x]
    while stride < size:
        count = min(4, size // stride)
        x = pair_sum(parts)
        parts = [x] + [
            lax.ppermute(x, axis, [(i, i ^ (stride * k)) for i in range(size)]) for k in range(1, count)
        ]
        stride *= count
    return parts


def product(hidden_rows, grad_rows):
    return dot(hidden_rows, grad_rows, ((0,), (0,)))


def after(x, *others):
    return lax.optimization_barrier((x, *others))[0]


def gathered(hidden, out_grad, carried, places, matrices):
    m = carried + product(hidden, lax.all_gather(out_grad, "tp", axis=0, tiled=True))
    folded = jax.ShapeDtypeStruct((m.shape[0] // steps, m.shape[1] // steps), jnp.float32)
    return [m], [call(bands_kernel, folded, m, places, *matrices)]


def lined(hidden, out_grad, carried, places, matrices):
    tok = out_grad.shape[0]
    me = lax.axis_index("tp")
    left = me < 2
    end = (me == 0) | (me == 3)
    cross = jnp.where(left, 2, 1)
    far = jnp.where(left, 3, 0)
    handed = tok * 2 // 3
    alone = tok - handed

    def rows_of(part, start=0, stop=tok):
        return lax.dynamic_slice_in_dim(hidden, part * tok + start, stop - start, 0)

    def send(x, perm):
        return lax.ppermute(x, "tp", perm)

    both_ways = [(0, 1), (1, 0), (2, 3), (3, 2)]
    across = [(1, 2), (2, 1)]
    outward = [(1, 0), (2, 3)]

    pair_grad = send(out_grad, both_ways)
    cross_grad = send(out_grad, across)
    m = carried + product(rows_of(me), out_grad)
    far_hidden = rows_of(far)
    helped_hidden = jnp.concatenate(
        [
            jnp.concatenate([rows_of(cross, handed), far_hidden[: handed - alone]], axis=0),
            far_hidden[handed - alone :],
        ],
        axis=1,
    )
    place_part = jnp.pad(places.astype(hidden.dtype), ((0, place_rows - places.shape[0]), (0, 0)))
    helped_hidden = jnp.concatenate([helped_hidden, place_part], axis=0)
    cross_hidden = jnp.where(end, rows_of(cross, 0, handed), 0)
    helped_hidden, cross_hidden, m = lax.optimization_barrier((helped_hidden, cross_hidden, m))

    far_grad = send(pair_grad, across)
    cross_grad = after(cross_grad, pair_grad, m)
    swapped = send(jnp.where(end, helped_hidden, cross_grad[: handed + place_rows]), both_ways)
    m = m + product(rows_of(me ^ 1), pair_grad) + product(rows_of(cross), cross_grad)
    far_grad = after(far_grad, m)
    swapped = after(swapped, far_grad)

    full = jax.ShapeDtypeStruct(m.shape, jnp.float32)
    folded = jax.ShapeDtypeStruct((m.shape[0] // steps, m.shape[1] // steps), jnp.float32)
    helped, helped_bands = call(helped_kernel, (full, folded), swapped, cross_grad, far_grad, *matrices)
    m, helped_bands = lax.optimization_barrier((m, helped_bands))
    sent_bands = send(helped_bands, outward)
    m, bands = call(
        last_rows_kernel, (full, folded), m, far_hidden, far_grad, cross_hidden, swapped, places, *matrices
    )
    helped_bands, bands = lax.optimization_barrier((sent_bands, bands))
    helped = send(after(helped, helped_bands), outward)
    return [m, helped], [bands, helped_bands]


def local(hidden, out_grad, momentum, band_rows, band_start_columns):
    row_count = hidden.shape[1]
    col_count = out_grad.shape[1]
    one_hot = jnp.asarray(np.kron(np.eye(col_count // order), np.ones((1, order))), jnp.float32)
    matrices = tuple(
        jnp.asarray(x) for x in (fold_matrix(col_count), diagonal_blocks(row_count), diagonal_blocks(col_count))
    )
    places = jnp.concatenate([band_rows, band_start_columns], axis=0).astype(jnp.float32)
    places = dot(places, one_hot)
    fits = out_grad.shape[0] % 48 == 0 and 2 * row_count == col_count and places.shape[0] <= place_rows
    form = lined if fits and lax.axis_size("tp") == 4 else gathered
    m_parts, band_parts = form(hidden, out_grad, decay_rate * momentum[0], places, matrices)
    parts = spread_sum(pair_sum(band_parts), "rep")
    shape = (row_count, col_count)
    momentum_out = call(
        functools.partial(remove_kernel, len(m_parts)),
        jax.ShapeDtypeStruct(shape, jnp.float32),
        *m_parts,
        *band_parts,
        places,
        *matrices,
    )
    update = call(update_kernel, jax.ShapeDtypeStruct(shape, jnp.bfloat16), *parts, places, *matrices)
    return (momentum_out[None], update)


def solution(mesh):
    return jax.shard_map(
        local,
        mesh=mesh,
        in_specs=(
            P("rep", "tp"),
            P(("rep", "tp"), None),
            P("rep", "tp", None),
            P("tp", None),
            P("tp", None),
        ),
        out_specs=(P("rep", "tp", None), P("tp", None)),
        check_vma=False,
    )
```

```python
import functools

import jax
import jax.numpy as jnp
import numpy as np
from jax import lax
from jax.experimental import pallas as pl
from jax.experimental.pallas import tpu as pltpu
from jax.sharding import PartitionSpec as P

decay_rate = 0.9
order = 64
band = 16
steps = order // band
place_rows = 16
code_rows = 16


def basis_matrix():
    frequency = np.arange(order, dtype=np.float64)[:, None]
    sample_pos = np.arange(order, dtype=np.float64)[None, :]
    norm_scale = np.where(frequency == 0, np.sqrt(1.0 / order), np.sqrt(2.0 / order))
    return norm_scale * np.cos(np.pi * (sample_pos + 0.5) * frequency / order)


def halves_of(matrix):
    high = matrix.astype(jnp.bfloat16)
    low = (matrix - high.astype(matrix.dtype)).astype(jnp.bfloat16)
    return np.stack([high, low])


def diagonal_blocks(width):
    count = next(c for c in (4, 2, 1) if width % (c * order) == 0)
    return halves_of(np.kron(np.eye(count), basis_matrix()))


def fold_matrix(width):
    return np.kron(np.eye(width // order), np.kron(np.ones((steps, 1)), np.eye(band))).astype(jnp.bfloat16)


def split2(x):
    high = x.astype(jnp.bfloat16)
    return high, (x - high.astype(jnp.float32)).astype(jnp.bfloat16)


def split3(x):
    high, low = split2(x)
    rest = x - high.astype(jnp.float32) - low.astype(jnp.float32)
    return high, low, rest.astype(jnp.bfloat16)


def dot(a, b, dims=((1,), (0,))):
    return lax.dot_general(a, b, (dims, ((), ())), preferred_element_type=jnp.float32)


def dot3(a, b, dims=((1,), (0,))):
    return dot(a[0], b[0], dims) + (dot(a[0], b[1], dims) + dot(a[1], b[0], dims))


def on_rows(basis_ref, x, transposed):
    basis = basis_ref[0], basis_ref[1]
    side = basis[0].shape[0]
    dims = ((0,), (0,)) if transposed else ((1,), (0,))
    parts = [dot3(basis, split2(x[i : i + side]), dims) for i in range(0, x.shape[0], side)]
    return parts[0] if len(parts) == 1 else jnp.concatenate(parts, axis=0)


def on_columns(basis_ref, x, transposed):
    basis = basis_ref[0], basis_ref[1]
    side = basis[0].shape[0]
    dims = ((1,), (0,)) if transposed else ((1,), (1,))
    parts = [dot3(split2(x[:, i : i + side]), basis, dims) for i in range(0, x.shape[1], side)]
    return parts[0] if len(parts) == 1 else jnp.concatenate(parts, axis=1)


def masks_of(places, count):
    width = places.shape[1]
    column = lax.rem(lax.broadcasted_iota(jnp.int32, (band, width), 1), order).astype(jnp.float32)
    masks = []
    for row in range(count):
        start = places[count + row : count + row + 1, :]
        masks.append((places[row : row + 1, :], (column >= start) & (column < start + band)))
    return masks


def selected(x, masks, row_basis_ref, column_basis_ref):
    by_rows = on_rows(row_basis_ref, x, False)
    pieces = []
    for row, (at, _) in enumerate(masks):
        taken = jnp.zeros((band, x.shape[1]), jnp.float32)
        for step in range(steps):
            start = row * order + step * band
            taken = jnp.where(at == step * band, by_rows[start : start + band], taken)
        pieces.append(taken)
    coefficients = on_columns(column_basis_ref, jnp.concatenate(pieces, axis=0), False)
    return within(coefficients, masks)


def within(x, masks):
    return jnp.concatenate(
        [jnp.where(inside, x[i * band : (i + 1) * band], 0.0) for i, (_, inside) in enumerate(masks)], axis=0
    )


def restored(x, masks, row_basis_ref, column_basis_ref):
    by_columns = on_columns(column_basis_ref, x, True)
    pieces = []
    for row, (at, _) in enumerate(masks):
        part = by_columns[row * band : (row + 1) * band]
        pieces += [jnp.where(at == step * band, part, 0.0) for step in range(steps)]
    return on_rows(row_basis_ref, jnp.concatenate(pieces, axis=0), True)


def bands_of(x, places, fold_ref, *basis_refs):
    taken = selected(x, masks_of(places, x.shape[0] // order), *basis_refs)
    return sum(dot(part, fold_ref[...]) for part in split3(taken))


def bands_kernel(m_ref, places_ref, fold_ref, row_basis_ref, column_basis_ref, bands_ref):
    bands_ref[...] = bands_of(m_ref[...], places_ref[...], fold_ref, row_basis_ref, column_basis_ref)


def coded(x):
    top = jnp.max(jnp.abs(x), axis=0, keepdims=True)
    exponent = jnp.ceil(jnp.log2(jnp.maximum(top, 1e-30)) + 0.01)
    scaled = x * jnp.exp2(15.0 - exponent)
    values = jnp.clip(jnp.round(scaled), -32767.0, 32767.0).astype(jnp.int32).astype(jnp.int16)
    row = jnp.broadcast_to(exponent, (code_rows, x.shape[1])).astype(jnp.int32).astype(jnp.int16)
    return values, row


def decoded(ref):
    values = ref[: ref.shape[0] - code_rows].astype(jnp.int32).astype(jnp.float32)
    row = ref[ref.shape[0] - code_rows :].astype(jnp.int32).astype(jnp.float32)
    return values * jnp.exp2(row[:1] - 15.0)


def last_rows_kernel(m_ref, far_hidden_ref, far_ref, cross_hidden_ref, cross_ref, swapped_ref, places_ref, *refs):
    *matrix_refs, out_ref, code_ref, bands_ref = refs
    handed, side = swapped_ref.shape[0] - place_rows, out_ref.shape[0]
    alone, count = cross_ref.shape[0] - handed, bands_ref.shape[0] // 2
    helped = (
        dot(swapped_ref[:alone, :side], cross_ref[handed:], ((0,), (0,)))
        + dot(swapped_ref[alone:handed, :side], far_ref[: handed - alone], ((0,), (0,)))
        + dot(swapped_ref[:handed, side:], far_ref[handed - alone :], ((0,), (0,)))
    )
    code_ref[:side], code_ref[side:] = coded(helped)
    bands_ref[count:] = bands_of(helped, swapped_ref[handed:].astype(jnp.float32), *matrix_refs)
    out_ref[...] = (
        m_ref[...]
        + dot(far_hidden_ref[...], far_ref[...], ((0,), (0,)))
        + dot(cross_hidden_ref[...], swapped_ref[:handed], ((0,), (0,)))
    )
    bands_ref[:count] = bands_of(out_ref[...], places_ref[...], *matrix_refs)


def remove_kernel(m_ref, *refs):
    *code_refs, places_ref, row_basis_ref, column_basis_ref, out_ref = refs
    m = m_ref[...]
    for ref in code_refs:
        m = m + decoded(ref)
    masks = masks_of(places_ref[...], m.shape[0] // order)
    taken = selected(m, masks, row_basis_ref, column_basis_ref)
    out_ref[...] = m - restored(taken, masks, row_basis_ref, column_basis_ref)


def update_kernel(*refs):
    *part_refs, places_ref, fold_ref, row_basis_ref, column_basis_ref, out_ref = refs
    folded = pair_sum([ref[...] for ref in part_refs])
    masks = masks_of(places_ref[...], out_ref.shape[0] // order)
    spread = sum(dot(part, fold_ref[...], ((1,), (1,))) for part in split3(folded))
    out_ref[...] = restored(within(spread, masks), masks, row_basis_ref, column_basis_ref).astype(out_ref.dtype)


def pair_sum(parts):
    while len(parts) > 1:
        parts = [sum(parts[i + 1 : i + 2], parts[i]) for i in range(0, len(parts), 2)]
    return parts[0]


def call(kernel, out_shapes, *operands):
    return pl.pallas_call(
        kernel,
        out_shape=out_shapes,
        compiler_params=pltpu.CompilerParams(vmem_limit_bytes=32 * 2**20),
        cost_estimate=pl.CostEstimate(flops=4 * 10**8, bytes_accessed=4 * 10**6, transcendentals=0),
    )(*operands)


def stages_of(axis):
    size, stride, stages = lax.axis_size(axis), 1, []
    while stride < size:
        stages.append((stride, min(4, size // stride)))
        stride *= stages[-1][1]
    return stages


def exchanged(x, axis, stride, count):
    size = lax.axis_size(axis)
    return [lax.ppermute(x, axis, [(i, i ^ (stride * k)) for i in range(size)]) for k in range(1, count)]


def summed_but_last(x, axis, form):
    size = lax.axis_size(axis)
    if size & (size - 1):
        return form(lax.psum(x, axis)), (1, 1)
    *stages, last = stages_of(axis) or [(1, 1)]
    for stride, count in stages:
        x = pair_sum([x] + exchanged(x, axis, stride, count))
    return form(x), last


def product(hidden_rows, grad_rows):
    return dot(hidden_rows, grad_rows, ((0,), (0,)))


def after(x, *others):
    return lax.optimization_barrier((x, *others))[0]


def gathered(hidden, out_grad, carried, places, matrices):
    m = carried + product(hidden, lax.all_gather(out_grad, "tp", axis=0, tiled=True))
    folded = jax.ShapeDtypeStruct((m.shape[0] // steps, m.shape[1] // steps), jnp.float32)
    bands, last = summed_but_last(call(bands_kernel, folded, m, places, *matrices), "rep", lambda x: x)
    return [m], [bands] + exchanged(bands, "rep", *last)


def lined(hidden, out_grad, carried, places, matrices):
    tok = out_grad.shape[0]
    me = lax.axis_index("tp")
    left = me < 2
    end = (me == 0) | (me == 3)
    cross = jnp.where(left, 2, 1)
    far = jnp.where(left, 3, 0)
    handed = tok * 2 // 3
    alone = tok - handed

    def rows_of(part, start=0, stop=tok):
        return lax.dynamic_slice_in_dim(hidden, part * tok + start, stop - start, 0)

    def send(x, perm):
        return lax.ppermute(x, "tp", perm)

    both_ways = [(0, 1), (1, 0), (2, 3), (3, 2)]
    across = [(1, 2), (2, 1)]
    outward = [(1, 0), (2, 3)]

    pair_grad = send(out_grad, both_ways)
    cross_grad = send(out_grad, across)
    m = carried + product(rows_of(me), out_grad)
    far_hidden = rows_of(far)
    helped_hidden = jnp.concatenate(
        [
            jnp.concatenate([rows_of(cross, handed), far_hidden[: handed - alone]], axis=0),
            far_hidden[handed - alone :],
        ],
        axis=1,
    )
    place_part = jnp.pad(places.astype(hidden.dtype), ((0, place_rows - places.shape[0]), (0, 0)))
    helped_hidden = jnp.concatenate([helped_hidden, place_part], axis=0)
    cross_hidden = jnp.where(end, rows_of(cross, 0, handed), 0)
    helped_hidden, cross_hidden, m = lax.optimization_barrier((helped_hidden, cross_hidden, m))

    far_grad = send(pair_grad, across)
    cross_grad = after(cross_grad, pair_grad, m)
    swapped = send(jnp.where(end, helped_hidden, cross_grad[: handed + place_rows]), both_ways)
    m = m + product(rows_of(me ^ 1), pair_grad) + product(rows_of(cross), cross_grad)
    far_grad = after(far_grad, m)
    swapped = after(swapped, far_grad)

    height, width = m.shape[0] // steps, m.shape[1] // steps
    m, code, bands = call(
        last_rows_kernel,
        (
            jax.ShapeDtypeStruct(m.shape, jnp.float32),
            jax.ShapeDtypeStruct((m.shape[0] + code_rows, m.shape[1]), jnp.int16),
            jax.ShapeDtypeStruct((2 * height, width), jnp.float32),
        ),
        m,
        far_hidden,
        far_grad,
        cross_hidden,
        cross_grad,
        swapped,
        places,
        *matrices,
    )
    code = send(code, outward)
    (bands, end_bands), (stride, count) = summed_but_last(bands, "rep", lambda x: (x[:height], x[height:]))
    parts = [bands] + exchanged(bands, "rep", stride, count)
    for k in range(count):
        perm = [
            (i * 4 + a, (i ^ (stride * k)) * 4 + b) for i in range(lax.axis_size("rep")) for a, b in outward
        ]
        parts.append(lax.ppermute(end_bands, ("rep", "tp"), perm))
    return [m, code], parts


def local(hidden, out_grad, momentum, band_rows, band_start_columns):
    row_count = hidden.shape[1]
    col_count = out_grad.shape[1]
    one_hot = jnp.asarray(np.kron(np.eye(col_count // order), np.ones((1, order))), jnp.float32)
    matrices = tuple(
        jnp.asarray(x) for x in (fold_matrix(col_count), diagonal_blocks(row_count), diagonal_blocks(col_count))
    )
    places = jnp.concatenate([band_rows, band_start_columns], axis=0).astype(jnp.float32)
    places = dot(places, one_hot)
    fits = out_grad.shape[0] % 48 == 0 and 2 * row_count == col_count and places.shape[0] <= place_rows
    form = lined if fits and lax.axis_size("tp") == 4 else gathered
    m_parts, band_parts = form(hidden, out_grad, decay_rate * momentum[0], places, matrices)
    shape = (row_count, col_count)
    momentum_out = call(
        remove_kernel, jax.ShapeDtypeStruct(shape, jnp.float32), *m_parts, places, *matrices[1:]
    )
    update = call(update_kernel, jax.ShapeDtypeStruct(shape, jnp.bfloat16), *band_parts, places, *matrices)
    return (momentum_out[None], update)


def solution(mesh):
    return jax.shard_map(
        local,
        mesh=mesh,
        in_specs=(
            P("rep", "tp"),
            P(("rep", "tp"), None),
            P("rep", "tp", None),
            P("tp", None),
            P("tp", None),
        ),
        out_specs=(P("rep", "tp", None), P("tp", None)),
        check_vma=False,
    )
```

```python
import functools

import jax
import jax.numpy as jnp
import numpy as np
from jax import lax
from jax.experimental import pallas as pl
from jax.experimental.pallas import tpu as pltpu
from jax.sharding import PartitionSpec as P

decay_rate = 0.9
order = 64
band = 16
steps = order // band
place_rows = 16
code_rows = 16


def basis_matrix():
    frequency = np.arange(order, dtype=np.float64)[:, None]
    sample_pos = np.arange(order, dtype=np.float64)[None, :]
    norm_scale = np.where(frequency == 0, np.sqrt(1.0 / order), np.sqrt(2.0 / order))
    return norm_scale * np.cos(np.pi * (sample_pos + 0.5) * frequency / order)


def halves_of(matrix):
    high = matrix.astype(jnp.bfloat16)
    low = (matrix - high.astype(matrix.dtype)).astype(jnp.bfloat16)
    return np.stack([high, low])


def diagonal_blocks(width):
    count = next(c for c in (4, 2, 1) if width % (c * order) == 0)
    return halves_of(np.kron(np.eye(count), basis_matrix()))


def fold_matrix(width):
    return np.kron(np.eye(width // order), np.kron(np.ones((steps, 1)), np.eye(band))).astype(jnp.bfloat16)


def split2(x):
    high = x.astype(jnp.bfloat16)
    return high, (x - high.astype(jnp.float32)).astype(jnp.bfloat16)


def split3(x):
    high, low = split2(x)
    rest = x - high.astype(jnp.float32) - low.astype(jnp.float32)
    return high, low, rest.astype(jnp.bfloat16)


def dot(a, b, dims=((1,), (0,))):
    return lax.dot_general(a, b, (dims, ((), ())), preferred_element_type=jnp.float32)


def dot3(a, b, dims=((1,), (0,))):
    return dot(a[0], b[0], dims) + (dot(a[0], b[1], dims) + dot(a[1], b[0], dims))


def on_rows(basis_ref, x, transposed):
    basis = basis_ref[0], basis_ref[1]
    side = basis[0].shape[0]
    dims = ((0,), (0,)) if transposed else ((1,), (0,))
    parts = [dot3(basis, split2(x[i : i + side]), dims) for i in range(0, x.shape[0], side)]
    return parts[0] if len(parts) == 1 else jnp.concatenate(parts, axis=0)


def on_columns(basis_ref, x, transposed):
    basis = basis_ref[0], basis_ref[1]
    side = basis[0].shape[0]
    dims = ((1,), (0,)) if transposed else ((1,), (1,))
    parts = [dot3(split2(x[:, i : i + side]), basis, dims) for i in range(0, x.shape[1], side)]
    return parts[0] if len(parts) == 1 else jnp.concatenate(parts, axis=1)


def masks_of(places, count):
    width = places.shape[1]
    column = lax.rem(lax.broadcasted_iota(jnp.int32, (band, width), 1), order).astype(jnp.float32)
    masks = []
    for row in range(count):
        start = places[count + row : count + row + 1, :]
        masks.append((places[row : row + 1, :], (column >= start) & (column < start + band)))
    return masks


def selected(x, masks, row_basis_ref, column_basis_ref):
    by_rows = on_rows(row_basis_ref, x, False)
    pieces = []
    for row, (at, _) in enumerate(masks):
        taken = jnp.zeros((band, x.shape[1]), jnp.float32)
        for step in range(steps):
            start = row * order + step * band
            taken = jnp.where(at == step * band, by_rows[start : start + band], taken)
        pieces.append(taken)
    coefficients = on_columns(column_basis_ref, jnp.concatenate(pieces, axis=0), False)
    return within(coefficients, masks)


def within(x, masks):
    return jnp.concatenate(
        [jnp.where(inside, x[i * band : (i + 1) * band], 0.0) for i, (_, inside) in enumerate(masks)], axis=0
    )


def restored(x, masks, row_basis_ref, column_basis_ref):
    by_columns = on_columns(column_basis_ref, x, True)
    pieces = []
    for row, (at, _) in enumerate(masks):
        part = by_columns[row * band : (row + 1) * band]
        pieces += [jnp.where(at == step * band, part, 0.0) for step in range(steps)]
    return on_rows(row_basis_ref, jnp.concatenate(pieces, axis=0), True)


def bands_of(x, places, fold_ref, *basis_refs):
    taken = selected(x, masks_of(places, x.shape[0] // order), *basis_refs)
    return sum(dot(part, fold_ref[...]) for part in split3(taken))


def bands_kernel(m_ref, places_ref, fold_ref, row_basis_ref, column_basis_ref, bands_ref):
    bands_ref[...] = bands_of(m_ref[...], places_ref[...], fold_ref, row_basis_ref, column_basis_ref)


def coded(x):
    top = jnp.max(jnp.abs(x), axis=0, keepdims=True)
    exponent = jnp.ceil(jnp.log2(jnp.maximum(top, 1e-30)) + 0.01)
    scaled = x * jnp.exp2(15.0 - exponent)
    values = jnp.clip(jnp.round(scaled), -32767.0, 32767.0).astype(jnp.int32).astype(jnp.int16)
    row = jnp.broadcast_to(exponent, (code_rows, x.shape[1])).astype(jnp.int32).astype(jnp.int16)
    return values, row


def decoded(ref):
    values = ref[: ref.shape[0] - code_rows].astype(jnp.int32).astype(jnp.float32)
    row = ref[ref.shape[0] - code_rows :].astype(jnp.int32).astype(jnp.float32)
    return values * jnp.exp2(row[:1] - 15.0)


def swapped_kernel(m_ref, far_hidden_ref, cross_hidden_ref, cross_ref, swapped_ref, *out_refs):
    out_ref, helped_ref, own_turned_ref, end_turned_ref, end_places_ref = out_refs
    handed, side = swapped_ref.shape[0] - place_rows, out_ref.shape[0]
    alone = cross_ref.shape[0] - handed
    out_ref[...] = m_ref[...] + dot(cross_hidden_ref[...], swapped_ref[:handed], ((0,), (0,)))
    helped_ref[...] = dot(swapped_ref[:alone, :side], cross_ref[handed:], ((0,), (0,)))
    own_turned_ref[...] = far_hidden_ref[...].T
    end_turned_ref[:, : handed - alone] = swapped_ref[alone:handed, :side].T
    end_turned_ref[:, handed - alone :] = swapped_ref[:handed, side:].T
    end_places_ref[...] = swapped_ref[handed:].astype(jnp.float32)


def helped_kernel(helped_ref, end_turned_ref, far_ref, out_ref, code_ref):
    out_ref[...] = helped_ref[...] + dot(end_turned_ref[...], far_ref[...])
    side = out_ref.shape[0]
    code_ref[:side], code_ref[side:] = coded(out_ref[...])


def last_rows_kernel(m_ref, own_turned_ref, far_ref, helped_ref, places_ref, end_places_ref, *refs):
    *matrix_refs, out_ref, bands_ref = refs
    count = bands_ref.shape[0] // 2
    bands_ref[count:] = bands_of(helped_ref[...], end_places_ref[...], *matrix_refs)
    out_ref[...] = m_ref[...] + dot(own_turned_ref[...], far_ref[...])
    bands_ref[:count] = bands_of(out_ref[...], places_ref[...], *matrix_refs)


def remove_kernel(m_ref, *refs):
    *code_refs, places_ref, row_basis_ref, column_basis_ref, out_ref = refs
    m = m_ref[...]
    for ref in code_refs:
        m = m + decoded(ref)
    masks = masks_of(places_ref[...], m.shape[0] // order)
    taken = selected(m, masks, row_basis_ref, column_basis_ref)
    out_ref[...] = m - restored(taken, masks, row_basis_ref, column_basis_ref)


def update_kernel(*refs):
    *part_refs, places_ref, fold_ref, row_basis_ref, column_basis_ref, out_ref = refs
    folded = pair_sum([ref[...] for ref in part_refs])
    masks = masks_of(places_ref[...], out_ref.shape[0] // order)
    spread = sum(dot(part, fold_ref[...], ((1,), (1,))) for part in split3(folded))
    out_ref[...] = restored(within(spread, masks), masks, row_basis_ref, column_basis_ref).astype(out_ref.dtype)


def pair_sum(parts):
    while len(parts) > 1:
        parts = [sum(parts[i + 1 : i + 2], parts[i]) for i in range(0, len(parts), 2)]
    return parts[0]


def call(kernel, out_shapes, *operands):
    return pl.pallas_call(
        kernel,
        out_shape=out_shapes,
        compiler_params=pltpu.CompilerParams(vmem_limit_bytes=32 * 2**20),
        cost_estimate=pl.CostEstimate(flops=4 * 10**8, bytes_accessed=4 * 10**6, transcendentals=0),
    )(*operands)


def stages_of(axis):
    size, stride, stages = lax.axis_size(axis), 1, []
    while stride < size:
        stages.append((stride, min(4, size // stride)))
        stride *= stages[-1][1]
    return stages


def exchanged(x, axis, stride, count):
    size = lax.axis_size(axis)
    return [lax.ppermute(x, axis, [(i, i ^ (stride * k)) for i in range(size)]) for k in range(1, count)]


def summed_but_last(x, axis, form):
    size = lax.axis_size(axis)
    if size & (size - 1):
        return form(lax.psum(x, axis)), (1, 1)
    *stages, last = stages_of(axis) or [(1, 1)]
    for stride, count in stages:
        x = pair_sum([x] + exchanged(x, axis, stride, count))
    return form(x), last


def product(hidden_rows, grad_rows):
    return dot(hidden_rows, grad_rows, ((0,), (0,)))


def after(x, *others):
    return lax.optimization_barrier((x, *others))[0]


def gathered(hidden, out_grad, carried, places, matrices):
    m = carried + product(hidden, lax.all_gather(out_grad, "tp", axis=0, tiled=True))
    folded = jax.ShapeDtypeStruct((m.shape[0] // steps, m.shape[1] // steps), jnp.float32)
    bands, last = summed_but_last(call(bands_kernel, folded, m, places, *matrices), "rep", lambda x: x)
    return [m], [bands] + exchanged(bands, "rep", *last)


def lined(hidden, out_grad, carried, places, matrices):
    tok = out_grad.shape[0]
    me = lax.axis_index("tp")
    left = me < 2
    end = (me == 0) | (me == 3)
    cross = jnp.where(left, 2, 1)
    far = jnp.where(left, 3, 0)
    handed = tok * 2 // 3
    alone = tok - handed

    def rows_of(part, start=0, stop=tok):
        return lax.dynamic_slice_in_dim(hidden, part * tok + start, stop - start, 0)

    def send(x, perm):
        return lax.ppermute(x, "tp", perm)

    both_ways = [(0, 1), (1, 0), (2, 3), (3, 2)]
    across = [(1, 2), (2, 1)]
    outward = [(1, 0), (2, 3)]

    pair_grad = send(out_grad, both_ways)
    cross_grad = send(out_grad, across)
    m = carried + product(rows_of(me), out_grad)
    far_hidden = rows_of(far)
    helped_hidden = jnp.concatenate(
        [
            jnp.concatenate([rows_of(cross, handed), far_hidden[: handed - alone]], axis=0),
            far_hidden[handed - alone :],
        ],
        axis=1,
    )
    place_part = jnp.pad(places.astype(hidden.dtype), ((0, place_rows - places.shape[0]), (0, 0)))
    helped_hidden = jnp.concatenate([helped_hidden, place_part], axis=0)
    cross_hidden = jnp.where(end, rows_of(cross, 0, handed), 0)
    helped_hidden, cross_hidden, m = lax.optimization_barrier((helped_hidden, cross_hidden, m))

    far_grad = send(pair_grad, across)
    cross_grad = after(cross_grad, pair_grad, m)
    swapped = send(jnp.where(end, helped_hidden, cross_grad[: handed + place_rows]), both_ways)
    m = m + product(rows_of(me ^ 1), pair_grad) + product(rows_of(cross), cross_grad)

    height, width = m.shape[0] // steps, m.shape[1] // steps
    full = jax.ShapeDtypeStruct(m.shape, jnp.float32)
    turned = jax.ShapeDtypeStruct((m.shape[0], tok), hidden.dtype)
    table = jax.ShapeDtypeStruct((place_rows, m.shape[1]), jnp.float32)
    m, helped, own_turned, end_turned, end_places = call(
        swapped_kernel, (full, full, turned, turned, table), m, far_hidden, cross_hidden, cross_grad, swapped
    )
    far_grad = after(far_grad, m)
    code_shape = jax.ShapeDtypeStruct((m.shape[0] + code_rows, m.shape[1]), jnp.int16)
    helped, code = call(helped_kernel, (full, code_shape), helped, end_turned, far_grad)
    code = send(code, outward)
    folded = jax.ShapeDtypeStruct((2 * height, width), jnp.float32)
    m, bands = call(
        last_rows_kernel, (full, folded), m, own_turned, far_grad, helped, places, end_places, *matrices
    )
    (bands, end_bands), (stride, count) = summed_but_last(bands, "rep", lambda x: (x[:height], x[height:]))
    parts = [bands] + exchanged(bands, "rep", stride, count)
    for k in range(count):
        perm = [
            (i * 4 + a, (i ^ (stride * k)) * 4 + b) for i in range(lax.axis_size("rep")) for a, b in outward
        ]
        parts.append(lax.ppermute(end_bands, ("rep", "tp"), perm))
    return [m, code], parts


def local(hidden, out_grad, momentum, band_rows, band_start_columns):
    row_count = hidden.shape[1]
    col_count = out_grad.shape[1]
    one_hot = jnp.asarray(np.kron(np.eye(col_count // order), np.ones((1, order))), jnp.float32)
    matrices = tuple(
        jnp.asarray(x) for x in (fold_matrix(col_count), diagonal_blocks(row_count), diagonal_blocks(col_count))
    )
    places = jnp.concatenate([band_rows, band_start_columns], axis=0).astype(jnp.float32)
    places = dot(places, one_hot)
    fits = out_grad.shape[0] % 48 == 0 and 2 * row_count == col_count and places.shape[0] <= place_rows
    form = lined if fits and lax.axis_size("tp") == 4 else gathered
    m_parts, band_parts = form(hidden, out_grad, decay_rate * momentum[0], places, matrices)
    shape = (row_count, col_count)
    momentum_out = call(
        remove_kernel, jax.ShapeDtypeStruct(shape, jnp.float32), *m_parts, places, *matrices[1:]
    )
    *band_parts, momentum_out = lax.optimization_barrier((*band_parts, momentum_out))
    update = call(update_kernel, jax.ShapeDtypeStruct(shape, jnp.bfloat16), *band_parts, places, *matrices)
    return (momentum_out[None], update)


def solution(mesh):
    return jax.shard_map(
        local,
        mesh=mesh,
        in_specs=(
            P("rep", "tp"),
            P(("rep", "tp"), None),
            P("rep", "tp", None),
            P("tp", None),
            P("tp", None),
        ),
        out_specs=(P("rep", "tp", None), P("tp", None)),
        check_vma=False,
    )
```

```python
import functools

import jax
import jax.numpy as jnp
import numpy as np
from jax import lax
from jax.experimental import pallas as pl
from jax.experimental.pallas import tpu as pltpu
from jax.sharding import PartitionSpec as P

decay_rate = 0.9
order = 64
band = 16
steps = order // band
place_rows = 16
code_rows = 16


def basis_matrix():
    frequency = np.arange(order, dtype=np.float64)[:, None]
    sample_pos = np.arange(order, dtype=np.float64)[None, :]
    norm_scale = np.where(frequency == 0, np.sqrt(1.0 / order), np.sqrt(2.0 / order))
    return norm_scale * np.cos(np.pi * (sample_pos + 0.5) * frequency / order)


def diagonal_blocks(width):
    count = next(c for c in (4, 2, 1) if width % (c * order) == 0)
    return np.kron(np.eye(count), basis_matrix()).astype(np.float32)


def fold_matrix(width):
    return np.kron(np.eye(width // order), np.kron(np.ones((steps, 1)), np.eye(band))).astype(jnp.bfloat16)


def split2(x):
    high = x.astype(jnp.bfloat16)
    return high, (x - high.astype(jnp.float32)).astype(jnp.bfloat16)


def split3(x):
    high, low = split2(x)
    rest = x - high.astype(jnp.float32) - low.astype(jnp.float32)
    return high, low, rest.astype(jnp.bfloat16)


def dot(a, b, dims=((1,), (0,))):
    return lax.dot_general(a, b, (dims, ((), ())), preferred_element_type=jnp.float32)


def dot3(a, b, dims=((1,), (0,))):
    return dot(a[0], b[0], dims) + (dot(a[0], b[1], dims) + dot(a[1], b[0], dims))


def on_rows(basis_ref, x, transposed):
    basis, side = split2(basis_ref[...]), basis_ref.shape[0]
    dims = ((0,), (0,)) if transposed else ((1,), (0,))
    parts = [dot3(basis, split2(x[i : i + side]), dims) for i in range(0, x.shape[0], side)]
    return parts[0] if len(parts) == 1 else jnp.concatenate(parts, axis=0)


def on_columns(basis_ref, x, transposed):
    basis, side = split2(basis_ref[...]), basis_ref.shape[0]
    dims = ((1,), (0,)) if transposed else ((1,), (1,))
    parts = [dot3(split2(x[:, i : i + side]), basis, dims) for i in range(0, x.shape[1], side)]
    return parts[0] if len(parts) == 1 else jnp.concatenate(parts, axis=1)


def masks_of(places, count):
    width = places.shape[1]
    column = lax.rem(lax.broadcasted_iota(jnp.int32, (band, width), 1), order).astype(jnp.float32)
    masks = []
    for row in range(count):
        start = places[count + row : count + row + 1, :]
        masks.append((places[row : row + 1, :], (column >= start) & (column < start + band)))
    return masks


def selected(x, masks, *basis_refs):
    by_rows = on_rows(basis_refs[0], x, False)
    pieces = []
    for row, (at, _) in enumerate(masks):
        taken = jnp.zeros((band, x.shape[1]), jnp.float32)
        for step in range(steps):
            start = row * order + step * band
            taken = jnp.where(at == step * band, by_rows[start : start + band], taken)
        pieces.append(taken)
    coefficients = on_columns(basis_refs[-1], jnp.concatenate(pieces, axis=0), False)
    return within(coefficients, masks)


def within(x, masks):
    return jnp.concatenate(
        [jnp.where(inside, x[i * band : (i + 1) * band], 0.0) for i, (_, inside) in enumerate(masks)], axis=0
    )


def restored(x, masks, *basis_refs):
    by_columns = on_columns(basis_refs[-1], x, True)
    pieces = []
    for row, (at, _) in enumerate(masks):
        part = by_columns[row * band : (row + 1) * band]
        pieces += [jnp.where(at == step * band, part, 0.0) for step in range(steps)]
    return on_rows(basis_refs[0], jnp.concatenate(pieces, axis=0), True)


def bands_of(x, places, fold_ref, *basis_refs):
    taken = selected(x, masks_of(places, x.shape[0] // order), *basis_refs)
    return sum(dot(part, fold_ref[...]) for part in split3(taken))


def bands_kernel(m_ref, places_ref, *refs):
    *matrix_refs, bands_ref = refs
    bands_ref[...] = bands_of(m_ref[...], places_ref[...], *matrix_refs)


def coded(x):
    top = jnp.max(jnp.abs(x), axis=0, keepdims=True)
    exponent = jnp.ceil(jnp.log2(jnp.maximum(top, 1e-30)) + 0.01)
    scaled = x * jnp.exp2(15.0 - exponent)
    values = jnp.clip(jnp.round(scaled), -32767.0, 32767.0).astype(jnp.int32).astype(jnp.int16)
    row = jnp.broadcast_to(exponent, (code_rows, x.shape[1])).astype(jnp.int32).astype(jnp.int16)
    return values, row


def decoded(code_ref, exponents_ref):
    values = code_ref[: code_ref.shape[0] - code_rows].astype(jnp.int32).astype(jnp.float32)
    exponents = exponents_ref[...].astype(jnp.int32).astype(jnp.float32)
    return values * jnp.exp2(exponents[:1] - 15.0)


def swapped_kernel(m_ref, far_hidden_ref, cross_hidden_ref, head_ref, cross_ref, swapped_ref, *out_refs):
    out_ref, helped_ref, own_turned_ref, end_turned_ref, end_places_ref = out_refs
    handed, side = swapped_ref.shape[0] - place_rows, out_ref.shape[0]
    alone, first = cross_ref.shape[0] - handed, head_ref.shape[0]
    own_turned_ref[...] = far_hidden_ref[...].T
    end_turned_ref[:, : handed - alone] = swapped_ref[alone:handed, :side].T
    end_turned_ref[:, handed - alone :] = swapped_ref[:handed, side:].T
    out_ref[...] = (
        m_ref[...]
        + dot(cross_hidden_ref[...], swapped_ref[:handed], ((0,), (0,)))
        + dot(own_turned_ref[:, :first], head_ref[...])
    )
    helped_ref[...] = dot(swapped_ref[:alone, :side], cross_ref[handed:], ((0,), (0,))) + dot(
        end_turned_ref[:, :first], head_ref[...]
    )
    end_places_ref[...] = swapped_ref[handed:].astype(jnp.float32)


def helped_kernel(helped_ref, end_turned_ref, far_ref, out_ref, code_ref):
    out_ref[...] = helped_ref[...] + dot(end_turned_ref[:, -far_ref.shape[0] :], far_ref[...])
    side = out_ref.shape[0]
    code_ref[:side], code_ref[side:] = coded(out_ref[...])


def last_rows_kernel(m_ref, own_turned_ref, far_ref, helped_ref, places_ref, end_places_ref, *refs):
    *matrix_refs, out_ref, bands_ref = refs
    count = bands_ref.shape[0] // 2
    bands_ref[count:] = bands_of(helped_ref[...], end_places_ref[...], *matrix_refs)
    out_ref[...] = m_ref[...] + dot(own_turned_ref[:, -far_ref.shape[0] :], far_ref[...])
    bands_ref[:count] = bands_of(out_ref[...], places_ref[...], *matrix_refs)


def remove_kernel(count, *refs):
    (m_ref, *code_refs), (places_ref, *basis_refs, out_ref) = refs[:count], refs[count:]
    m = m_ref[...]
    if code_refs:
        m = m + decoded(*code_refs)
    masks = masks_of(places_ref[...], m.shape[0] // order)
    out_ref[...] = m - restored(selected(m, masks, *basis_refs), masks, *basis_refs)


def update_kernel(count, *refs):
    part_refs, (places_ref, fold_ref, *basis_refs, out_ref) = refs[:count], refs[count:]
    folded = pair_sum([ref[...] for ref in part_refs])
    masks = masks_of(places_ref[...], out_ref.shape[0] // order)
    spread = sum(dot(part, fold_ref[...], ((1,), (1,))) for part in split3(folded))
    out_ref[...] = restored(within(spread, masks), masks, *basis_refs).astype(out_ref.dtype)


def pair_sum(parts):
    while len(parts) > 1:
        parts = [sum(parts[i + 1 : i + 2], parts[i]) for i in range(0, len(parts), 2)]
    return parts[0]


def call(kernel, out_shapes, *operands):
    return pl.pallas_call(
        kernel,
        out_shape=out_shapes,
        compiler_params=pltpu.CompilerParams(vmem_limit_bytes=32 * 2**20),
        cost_estimate=pl.CostEstimate(flops=4 * 10**8, bytes_accessed=4 * 10**6, transcendentals=0),
    )(*operands)


def stages_of(axis):
    size, stride, stages = lax.axis_size(axis), 1, []
    while stride < size:
        stages.append((stride, min(4, size // stride)))
        stride *= stages[-1][1]
    return stages


def exchanged(x, axis, stride, count):
    size = lax.axis_size(axis)
    return [lax.ppermute(x, axis, [(i, i ^ (stride * k)) for i in range(size)]) for k in range(1, count)]


def summed_but_last(x, axis, form, then=lambda x: x):
    size = lax.axis_size(axis)
    if size & (size - 1):
        return form(lax.psum(x, axis)), (1, 1)
    *stages, last = stages_of(axis) or [(1, 1)]
    for stride, count in stages:
        x = pair_sum([x] + then(exchanged(x, axis, stride, count)))
    return form(x), last


def product(hidden_rows, grad_rows):
    return dot(hidden_rows, grad_rows, ((0,), (0,)))


def after(x, *others):
    return lax.optimization_barrier((x, *others))[0]


def gathered(hidden, out_grad, carried, places, matrices):
    m = carried + product(hidden, lax.all_gather(out_grad, "tp", axis=0, tiled=True))
    folded = jax.ShapeDtypeStruct((m.shape[0] // steps, m.shape[1] // steps), jnp.float32)
    bands, last = summed_but_last(call(bands_kernel, folded, m, places, *matrices), "rep", lambda x: x)
    return [m], [bands] + exchanged(bands, "rep", *last), places, matrices


def lined(hidden, out_grad, carried, places, matrices):
    tok = out_grad.shape[0]
    me = lax.axis_index("tp")
    left = me < 2
    end = (me == 0) | (me == 3)
    cross = jnp.where(left, 2, 1)
    far = jnp.where(left, 3, 0)
    handed = tok * 2 // 3
    alone = tok - handed
    first = tok // 4 // 128 * 128

    def rows_of(part, start=0, stop=tok):
        return lax.dynamic_slice_in_dim(hidden, part * tok + start, stop - start, 0)

    def send(x, perm):
        return lax.ppermute(x, "tp", perm)

    both_ways = [(0, 1), (1, 0), (2, 3), (3, 2)]
    across = [(1, 2), (2, 1)]
    outward = [(1, 0), (2, 3)]
    over_one = [(0, 2), (3, 1)]

    pair_grad = send(out_grad, both_ways)
    cross_grad = send(out_grad, across)
    m = carried + product(rows_of(me), out_grad)
    far_hidden = rows_of(far)
    helped_hidden = jnp.concatenate(
        [
            jnp.concatenate([rows_of(cross, handed), far_hidden[: handed - alone]], axis=0),
            far_hidden[handed - alone :],
        ],
        axis=1,
    )
    place_part = jnp.pad(places.astype(hidden.dtype), ((0, place_rows - places.shape[0]), (0, 0)))
    helped_hidden = jnp.concatenate([helped_hidden, place_part], axis=0)
    cross_hidden = jnp.where(end, rows_of(cross, 0, handed), 0)
    helped_hidden, cross_hidden, m = lax.optimization_barrier((helped_hidden, cross_hidden, m))

    far_head = send(out_grad[:first], over_one)
    far_grad = send(pair_grad[first:], across)
    cross_grad, matrices, places = after((cross_grad, matrices, places), pair_grad, far_head, m)
    swapped = send(jnp.where(end, helped_hidden, cross_grad[: handed + place_rows]), both_ways)
    m = m + product(rows_of(me ^ 1), pair_grad) + product(rows_of(cross), cross_grad)

    height, width = m.shape[0] // steps, m.shape[1] // steps
    full = jax.ShapeDtypeStruct(m.shape, jnp.float32)
    turned = jax.ShapeDtypeStruct((m.shape[0], tok), hidden.dtype)
    table = jax.ShapeDtypeStruct((place_rows, m.shape[1]), jnp.float32)
    m, helped, own_turned, end_turned, end_places = call(
        swapped_kernel, (full, full, turned, turned, table), m, far_hidden, cross_hidden, far_head, cross_grad, swapped
    )
    far_grad = after(far_grad, m)
    code_shape = jax.ShapeDtypeStruct((m.shape[0] + code_rows, m.shape[1]), jnp.int16)
    helped, code = call(helped_kernel, (full, code_shape), helped, end_turned, far_grad)
    code = send(code, outward)
    folded = jax.ShapeDtypeStruct((2 * height, width), jnp.float32)
    m, bands = call(
        last_rows_kernel, (full, folded), m, own_turned, far_grad, helped, places, end_places, *matrices
    )
    exponents = code[m.shape[0] :]

    def behind_code(x):
        nonlocal exponents
        x, exponents = lax.optimization_barrier((x, exponents))
        return x

    (bands, end_bands), (stride, count) = summed_but_last(
        bands, "rep", lambda x: (x[:height], x[height:]), behind_code
    )
    parts = [bands] + exchanged(bands, "rep", stride, count)
    for k in range(count):
        perm = [
            (i * 4 + a, (i ^ (stride * k)) * 4 + b) for i in range(lax.axis_size("rep")) for a, b in outward
        ]
        parts.append(lax.ppermute(end_bands, ("rep", "tp"), perm))
    return [m, code, exponents], parts, places, matrices


def local(hidden, out_grad, momentum, band_rows, band_start_columns):
    row_count = hidden.shape[1]
    col_count = out_grad.shape[1]
    one_hot = jnp.asarray(np.kron(np.eye(col_count // order), np.ones((1, order))), jnp.float32)
    bases = [diagonal_blocks(row_count), diagonal_blocks(col_count)]
    if bases[0].shape == bases[1].shape:
        bases = bases[:1]
    matrices = tuple(jnp.asarray(x) for x in (fold_matrix(col_count), *bases))
    places = jnp.concatenate([band_rows, band_start_columns], axis=0).astype(jnp.float32)
    places = dot(places, one_hot)
    fits = out_grad.shape[0] % 384 == 0 and out_grad.shape[0] >= 768 and 2 * row_count == col_count and places.shape[0] <= place_rows
    form = lined if fits and lax.axis_size("tp") == 4 else gathered
    m_parts, band_parts, places, matrices = form(hidden, out_grad, decay_rate * momentum[0], places, matrices)
    shape = (row_count, col_count)
    momentum_out = call(
        functools.partial(remove_kernel, len(m_parts)),
        jax.ShapeDtypeStruct(shape, jnp.float32),
        *m_parts,
        places,
        *matrices[1:],
    )
    *band_parts, momentum_out = lax.optimization_barrier((*band_parts, momentum_out))
    update = call(
        functools.partial(update_kernel, len(band_parts)),
        jax.ShapeDtypeStruct(shape, jnp.bfloat16),
        *band_parts,
        places,
        *matrices,
    )
    return (momentum_out[None], update)


def solution(mesh):
    return jax.shard_map(
        local,
        mesh=mesh,
        in_specs=(
            P("rep", "tp"),
            P(("rep", "tp"), None),
            P("rep", "tp", None),
            P("tp", None),
            P("tp", None),
        ),
        out_specs=(P("rep", "tp", None), P("tp", None)),
        check_vma=False,
    )
```

```python
import functools

import jax
import jax.numpy as jnp
import numpy as np
from jax import lax
from jax.experimental import pallas as pl
from jax.experimental.pallas import tpu as pltpu
from jax.sharding import PartitionSpec as P

decay_rate = 0.9
order = 64
band = 16
steps = order // band
place_rows = 16
code_rows = 16


def basis_matrix():
    frequency = np.arange(order, dtype=np.float64)[:, None]
    sample_pos = np.arange(order, dtype=np.float64)[None, :]
    norm_scale = np.where(frequency == 0, np.sqrt(1.0 / order), np.sqrt(2.0 / order))
    return norm_scale * np.cos(np.pi * (sample_pos + 0.5) * frequency / order)


def diagonal_blocks(width):
    count = next(c for c in (4, 2, 1) if width % (c * order) == 0)
    return np.kron(np.eye(count), basis_matrix()).astype(np.float32)


def fold_matrix(width):
    return np.kron(np.eye(width // order), np.kron(np.ones((steps, 1)), np.eye(band))).astype(jnp.bfloat16)


def split2(x):
    high = x.astype(jnp.bfloat16)
    return high, (x - high.astype(jnp.float32)).astype(jnp.bfloat16)


def split3(x):
    high, low = split2(x)
    rest = x - high.astype(jnp.float32) - low.astype(jnp.float32)
    return high, low, rest.astype(jnp.bfloat16)


def dot(a, b, dims=((1,), (0,))):
    return lax.dot_general(a, b, (dims, ((), ())), preferred_element_type=jnp.float32)


def dot3(a, b, dims=((1,), (0,))):
    (a_high, a_low), (b_high, b_low) = a, b
    left = jnp.concatenate([a_high, a_low, a_high], axis=dims[0][0])
    right = jnp.concatenate([b_high, b_high, b_low], axis=dims[1][0])
    return dot(left, right, dims)


def on_rows(basis_ref, x, transposed):
    basis, side = split2(basis_ref[...]), basis_ref.shape[0]
    dims = ((0,), (0,)) if transposed else ((1,), (0,))
    parts = [dot3(basis, split2(x[i : i + side]), dims) for i in range(0, x.shape[0], side)]
    return parts[0] if len(parts) == 1 else jnp.concatenate(parts, axis=0)


def on_columns(basis_ref, x, transposed):
    basis, side = split2(basis_ref[...]), basis_ref.shape[0]
    dims = ((1,), (0,)) if transposed else ((1,), (1,))
    parts = [dot3(split2(x[:, i : i + side]), basis, dims) for i in range(0, x.shape[1], side)]
    return parts[0] if len(parts) == 1 else jnp.concatenate(parts, axis=1)


def masks_of(places, count):
    width = places.shape[1]
    column = lax.rem(lax.broadcasted_iota(jnp.int32, (band, width), 1), order).astype(jnp.float32)
    masks = []
    for row in range(count):
        start = places[count + row : count + row + 1, :]
        masks.append((places[row : row + 1, :], (column >= start) & (column < start + band)))
    return masks


def rows_taken(x, masks):
    pieces = []
    for row, (at, _) in enumerate(masks):
        taken = jnp.zeros((band, x.shape[1]), jnp.float32)
        for step in range(steps):
            start = row * order + step * band
            taken = jnp.where(at == step * band, x[start : start + band], taken)
        pieces.append(taken)
    return jnp.concatenate(pieces, axis=0)


def selected(x, masks, *basis_refs):
    taken = rows_taken(on_rows(basis_refs[0], x, False), masks)
    return within(on_columns(basis_refs[-1], taken, False), masks)


def within(x, masks):
    return jnp.concatenate(
        [jnp.where(inside, x[i * band : (i + 1) * band], 0.0) for i, (_, inside) in enumerate(masks)], axis=0
    )


def restored(x, masks, *basis_refs):
    by_columns = on_columns(basis_refs[-1], x, True)
    pieces = []
    for row, (at, _) in enumerate(masks):
        part = by_columns[row * band : (row + 1) * band]
        pieces += [jnp.where(at == step * band, part, 0.0) for step in range(steps)]
    return on_rows(basis_refs[0], jnp.concatenate(pieces, axis=0), True)


def bands_of(x, places, fold_ref, *basis_refs):
    return folded(selected(x, masks_of(places, x.shape[0] // order), *basis_refs), fold_ref[...])


def folded(x, fold):
    return dot(jnp.concatenate(split3(x), axis=1), jnp.concatenate([fold] * 3, axis=0))


def spread(x, fold):
    return dot(jnp.concatenate(split3(x), axis=1), jnp.concatenate([fold] * 3, axis=1), ((1,), (1,)))


def bands_kernel(m_ref, places_ref, *refs):
    *matrix_refs, bands_ref = refs
    bands_ref[...] = bands_of(m_ref[...], places_ref[...], *matrix_refs)


def coded(x):
    top = jnp.max(jnp.abs(x), axis=0, keepdims=True)
    exponent = jnp.ceil(jnp.log2(jnp.maximum(top, 1e-30)) + 0.01)
    scaled = x * jnp.exp2(15.0 - exponent)
    values = jnp.clip(jnp.round(scaled), -32767.0, 32767.0).astype(jnp.int32).astype(jnp.int16)
    row = jnp.broadcast_to(exponent, (code_rows, x.shape[1])).astype(jnp.int32).astype(jnp.int16)
    return values, row


def decoded(code_ref, exponents_ref):
    values = code_ref[: code_ref.shape[0] - code_rows].astype(jnp.int32).astype(jnp.float32)
    exponents = exponents_ref[...].astype(jnp.int32).astype(jnp.float32)
    return values * jnp.exp2(exponents[:1] - 15.0)


def swapped_kernel(m_ref, far_hidden_ref, cross_hidden_ref, head_ref, cross_ref, swapped_ref, *out_refs):
    out_ref, helped_ref, own_turned_ref, end_turned_ref, end_places_ref = out_refs
    handed, side = swapped_ref.shape[0] - place_rows, out_ref.shape[0]
    alone, first = cross_ref.shape[0] - handed, head_ref.shape[0]
    own_turned_ref[...] = far_hidden_ref[...].T
    end_turned_ref[:, : handed - alone] = swapped_ref[alone:handed, :side].T
    end_turned_ref[:, handed - alone :] = swapped_ref[:handed, side:].T
    out_ref[...] = (
        m_ref[...]
        + dot(cross_hidden_ref[...], swapped_ref[:handed], ((0,), (0,)))
        + dot(own_turned_ref[:, :first], head_ref[...])
    )
    helped_ref[...] = dot(swapped_ref[:alone, :side], cross_ref[handed:], ((0,), (0,))) + dot(
        end_turned_ref[:, :first], head_ref[...]
    )
    end_places_ref[...] = swapped_ref[handed:].astype(jnp.float32)


def helped_kernel(helped_ref, end_turned_ref, far_ref, out_ref, code_ref):
    out_ref[...] = helped_ref[...] + dot(end_turned_ref[:, -far_ref.shape[0] :], far_ref[...])
    side = out_ref.shape[0]
    code_ref[:side], code_ref[side:] = coded(out_ref[...])


def last_rows_kernel(m_ref, own_turned_ref, far_ref, helped_ref, places_ref, end_places_ref, *refs):
    fold_ref, *basis_refs, out_ref, bands_ref = refs
    out_ref[...] = m_ref[...] + dot(own_turned_ref[:, -far_ref.shape[0] :], far_ref[...])
    rows, width = out_ref.shape
    by_rows = on_rows(basis_refs[0], jnp.concatenate([out_ref[...], helped_ref[...]], axis=1), False)
    masks = [masks_of(places[...], rows // order) for places in (places_ref, end_places_ref)]
    taken = [rows_taken(by_rows[:, i * width :][:, :width], masks[i]) for i in range(2)]
    coefficients = on_columns(basis_refs[-1], jnp.concatenate(taken, axis=0), False)
    bands_ref[...] = folded(within(coefficients, masks[0] + masks[1]), fold_ref[...])


def remove_kernel(count, *refs):
    (m_ref, *code_refs), (end_ref, places_ref, *basis_refs, out_ref) = refs[:count], refs[count:]
    m = m_ref[...]
    if code_refs:
        m = m + jnp.where(end_ref[:1, :] > 0, decoded(*code_refs), 0.0)
    masks = masks_of(places_ref[...], m.shape[0] // order)
    out_ref[...] = m - restored(selected(m, masks, *basis_refs), masks, *basis_refs)


def update_kernel(own_count, count, *refs):
    part_refs, (end_ref, places_ref, fold_ref, *basis_refs, out_ref) = refs[:count], refs[count:]
    parts = [ref[...] for ref in part_refs]
    bands = pair_sum(parts[:own_count])
    if own_count < count:
        bands = bands + jnp.where(end_ref[:1, : bands.shape[1]] > 0, pair_sum(parts[own_count:]), 0.0)
    masks = masks_of(places_ref[...], out_ref.shape[0] // order)
    coefficients = within(spread(bands, fold_ref[...]), masks)
    out_ref[...] = restored(coefficients, masks, *basis_refs).astype(out_ref.dtype)


def pair_sum(parts):
    while len(parts) > 1:
        parts = [sum(parts[i + 1 : i + 2], parts[i]) for i in range(0, len(parts), 2)]
    return parts[0]


def call(kernel, out_shapes, *operands):
    return pl.pallas_call(
        kernel,
        out_shape=out_shapes,
        compiler_params=pltpu.CompilerParams(vmem_limit_bytes=32 * 2**20),
        cost_estimate=pl.CostEstimate(flops=4 * 10**8, bytes_accessed=4 * 10**6, transcendentals=0),
    )(*operands)


def stages_of(axis):
    size, stride, stages = lax.axis_size(axis), 1, []
    while stride < size:
        stages.append((stride, min(4, size // stride)))
        stride *= stages[-1][1]
    return stages


def exchanged(x, axis, stride, count):
    size = lax.axis_size(axis)
    return [lax.ppermute(x, axis, [(i, i ^ (stride * k)) for i in range(size)]) for k in range(1, count)]


def summed_but_last(x, axis, form, then=lambda x: x):
    size = lax.axis_size(axis)
    if size & (size - 1):
        return form(lax.psum(x, axis)), (1, 1)
    *stages, last = stages_of(axis) or [(1, 1)]
    for stride, count in stages:
        x = pair_sum([x] + then(exchanged(x, axis, stride, count)))
    return form(x), last


def product(hidden_rows, grad_rows):
    return dot(hidden_rows, grad_rows, ((0,), (0,)))


def after(x, *others):
    return lax.optimization_barrier((x, *others))[0]


def gathered(hidden, out_grad, carried, places, matrices):
    m = carried + product(hidden, lax.all_gather(out_grad, "tp", axis=0, tiled=True))
    folded = jax.ShapeDtypeStruct((m.shape[0] // steps, m.shape[1] // steps), jnp.float32)
    bands, last = summed_but_last(call(bands_kernel, folded, m, places, *matrices), "rep", lambda x: x)
    parts = [bands] + exchanged(bands, "rep", *last)
    return [m], parts, len(parts), jnp.zeros((8, m.shape[1]), jnp.float32), places, matrices


def lined(hidden, out_grad, carried, places, matrices):
    tok = out_grad.shape[0]
    me = lax.axis_index("tp")
    left = me < 2
    end = (me == 0) | (me == 3)
    cross = jnp.where(left, 2, 1)
    far = jnp.where(left, 3, 0)
    handed = tok * 2 // 3
    alone = tok - handed
    first = tok // 4 // 128 * 128

    def rows_of(part, start=0, stop=tok):
        return lax.dynamic_slice_in_dim(hidden, part * tok + start, stop - start, 0)

    def send(x, perm):
        return lax.ppermute(x, "tp", perm)

    both_ways = [(0, 1), (1, 0), (2, 3), (3, 2)]
    across = [(1, 2), (2, 1)]
    over_one = [(0, 2), (3, 1)]

    pair_grad = send(out_grad, both_ways)
    cross_grad = send(out_grad, across)
    m = carried + product(rows_of(me), out_grad)
    far_hidden = rows_of(far)
    helped_hidden = jnp.concatenate(
        [
            jnp.concatenate([rows_of(cross, handed), far_hidden[: handed - alone]], axis=0),
            far_hidden[handed - alone :],
        ],
        axis=1,
    )
    place_part = jnp.pad(places.astype(hidden.dtype), ((0, place_rows - places.shape[0]), (0, 0)))
    helped_hidden = jnp.concatenate([helped_hidden, place_part], axis=0)
    cross_hidden = jnp.where(end, rows_of(cross, 0, handed), 0)
    helped_hidden, cross_hidden, m = lax.optimization_barrier((helped_hidden, cross_hidden, m))

    far_head = send(out_grad[:first], over_one)
    cross_grad, matrices, places = after((cross_grad, matrices, places), m)
    to_swap = jnp.where(end, helped_hidden, cross_grad[: handed + place_rows])
    pair_grad, to_swap = lax.optimization_barrier((pair_grad, to_swap))
    far_grad = send(pair_grad[first:], across)
    far_head, to_swap = lax.optimization_barrier((far_head, to_swap))
    swapped = send(to_swap, both_ways)
    m = m + product(rows_of(me ^ 1), pair_grad) + product(rows_of(cross), cross_grad)

    height, width = m.shape[0] // steps, m.shape[1] // steps
    full = jax.ShapeDtypeStruct(m.shape, jnp.float32)
    turned = jax.ShapeDtypeStruct((m.shape[0], tok), hidden.dtype)
    table = jax.ShapeDtypeStruct((place_rows, m.shape[1]), jnp.float32)
    m, helped, own_turned, end_turned, end_places = call(
        swapped_kernel, (full, full, turned, turned, table), m, far_hidden, cross_hidden, far_head, cross_grad, swapped
    )
    far_grad = after(far_grad, m)
    code_shape = jax.ShapeDtypeStruct((m.shape[0] + code_rows, m.shape[1]), jnp.int16)
    helped, code = call(helped_kernel, (full, code_shape), helped, end_turned, far_grad)
    code = send(code, both_ways)
    folded = jax.ShapeDtypeStruct((2 * height, width), jnp.float32)
    m, bands = call(
        last_rows_kernel, (full, folded), m, own_turned, far_grad, helped, places, end_places, *matrices
    )
    exponents = code[m.shape[0] :]

    def behind_code(x):
        nonlocal exponents
        x, exponents = lax.optimization_barrier((x, exponents))
        return x

    (bands, end_bands), (stride, count) = summed_but_last(
        bands, "rep", lambda x: (x[:height], x[height:]), behind_code
    )
    parts = [bands] + exchanged(bands, "rep", stride, count)
    end_flag = jnp.full((8, m.shape[1]), end, jnp.float32)
    for k in range(count):
        perm = [
            (i * 4 + a, (i ^ (stride * k)) * 4 + b) for i in range(lax.axis_size("rep")) for a, b in both_ways
        ]
        parts.append(lax.ppermute(end_bands, ("rep", "tp"), perm))
    return [m, code, exponents], parts, count, end_flag, places, matrices


def local(hidden, out_grad, momentum, band_rows, band_start_columns):
    row_count = hidden.shape[1]
    col_count = out_grad.shape[1]
    one_hot = jnp.asarray(np.kron(np.eye(col_count // order), np.ones((1, order))), jnp.float32)
    bases = [diagonal_blocks(row_count), diagonal_blocks(col_count)]
    if bases[0].shape == bases[1].shape:
        bases = bases[:1]
    matrices = tuple(jnp.asarray(x) for x in (fold_matrix(col_count), *bases))
    places = jnp.concatenate([band_rows, band_start_columns], axis=0).astype(jnp.float32)
    places = dot(places, one_hot)
    fits = out_grad.shape[0] % 384 == 0 and out_grad.shape[0] >= 768 and 2 * row_count == col_count and places.shape[0] <= place_rows
    form = lined if fits and lax.axis_size("tp") == 4 else gathered
    m_parts, band_parts, own_count, end_flag, places, matrices = form(
        hidden, out_grad, decay_rate * momentum[0], places, matrices
    )
    shape = (row_count, col_count)
    momentum_out = call(
        functools.partial(remove_kernel, len(m_parts)),
        jax.ShapeDtypeStruct(shape, jnp.float32),
        *m_parts,
        end_flag,
        places,
        *matrices[1:],
    )
    *band_parts, momentum_out = lax.optimization_barrier((*band_parts, momentum_out))
    update = call(
        functools.partial(update_kernel, own_count, len(band_parts)),
        jax.ShapeDtypeStruct(shape, jnp.bfloat16),
        *band_parts,
        end_flag,
        places,
        *matrices,
    )
    return (momentum_out[None], update)


def solution(mesh):
    return jax.shard_map(
        local,
        mesh=mesh,
        in_specs=(
            P("rep", "tp"),
            P(("rep", "tp"), None),
            P("rep", "tp", None),
            P("tp", None),
            P("tp", None),
        ),
        out_specs=(P("rep", "tp", None), P("tp", None)),
        check_vma=False,
    )
```

```python
import functools

import jax
import jax.numpy as jnp
import numpy as np
from jax import lax
from jax.experimental import pallas as pl
from jax.experimental.pallas import tpu as pltpu
from jax.sharding import PartitionSpec as P

decay_rate = 0.9
order = 64
band = 16
steps = order // band
place_rows = 16
code_rows = 16


def basis_matrix():
    frequency = np.arange(order, dtype=np.float64)[:, None]
    sample_pos = np.arange(order, dtype=np.float64)[None, :]
    norm_scale = np.where(frequency == 0, np.sqrt(1.0 / order), np.sqrt(2.0 / order))
    return norm_scale * np.cos(np.pi * (sample_pos + 0.5) * frequency / order)


def diagonal_blocks(width):
    count = next(c for c in (4, 2, 1) if width % (c * order) == 0)
    return np.kron(np.eye(count), basis_matrix()).astype(np.float32)


def fold_matrix(width):
    return np.kron(np.eye(width // order), np.kron(np.ones((steps, 1)), np.eye(band))).astype(jnp.bfloat16)


def split2(x):
    high = x.astype(jnp.bfloat16)
    return high, (x - high.astype(jnp.float32)).astype(jnp.bfloat16)


def split3(x):
    high, low = split2(x)
    rest = x - high.astype(jnp.float32) - low.astype(jnp.float32)
    return high, low, rest.astype(jnp.bfloat16)


def dot(a, b, dims=((1,), (0,))):
    return lax.dot_general(a, b, (dims, ((), ())), preferred_element_type=jnp.float32)


def dot3(a, b, dims=((1,), (0,))):
    (a_high, a_low), (b_high, b_low) = a, b
    left = jnp.concatenate([a_high, a_low, a_high], axis=dims[0][0])
    right = jnp.concatenate([b_high, b_high, b_low], axis=dims[1][0])
    return dot(left, right, dims)


def on_rows(basis_ref, x, transposed):
    basis, side = split2(basis_ref[...]), basis_ref.shape[0]
    dims = ((0,), (0,)) if transposed else ((1,), (0,))
    parts = [dot3(basis, split2(x[i : i + side]), dims) for i in range(0, x.shape[0], side)]
    return parts[0] if len(parts) == 1 else jnp.concatenate(parts, axis=0)


def on_columns(basis_ref, x, transposed):
    basis, side = split2(basis_ref[...]), basis_ref.shape[0]
    dims = ((1,), (0,)) if transposed else ((1,), (1,))
    parts = [dot3(split2(x[:, i : i + side]), basis, dims) for i in range(0, x.shape[1], side)]
    return parts[0] if len(parts) == 1 else jnp.concatenate(parts, axis=1)


def masks_of(places, count):
    width = places.shape[1]
    column = lax.rem(lax.broadcasted_iota(jnp.int32, (band, width), 1), order).astype(jnp.float32)
    masks = []
    for row in range(count):
        start = places[count + row : count + row + 1, :]
        masks.append((places[row : row + 1, :], (column >= start) & (column < start + band)))
    return masks


def rows_taken(x, masks):
    pieces = []
    for row, (at, _) in enumerate(masks):
        taken = jnp.zeros((band, x.shape[1]), jnp.float32)
        for step in range(steps):
            start = row * order + step * band
            taken = jnp.where(at == step * band, x[start : start + band], taken)
        pieces.append(taken)
    return jnp.concatenate(pieces, axis=0)


def selected(x, masks, *basis_refs):
    taken = rows_taken(on_rows(basis_refs[0], x, False), masks)
    return within(on_columns(basis_refs[-1], taken, False), masks)


def within(x, masks):
    return jnp.concatenate(
        [jnp.where(inside, x[i * band : (i + 1) * band], 0.0) for i, (_, inside) in enumerate(masks)], axis=0
    )


def restored(x, masks, *basis_refs):
    by_columns = on_columns(basis_refs[-1], x, True)
    pieces = []
    for row, (at, _) in enumerate(masks):
        part = by_columns[row * band : (row + 1) * band]
        pieces += [jnp.where(at == step * band, part, 0.0) for step in range(steps)]
    return on_rows(basis_refs[0], jnp.concatenate(pieces, axis=0), True)


def bands_of(x, places, fold_ref, *basis_refs):
    return folded(selected(x, masks_of(places, x.shape[0] // order), *basis_refs), fold_ref[...])


def folded(x, fold):
    return dot(jnp.concatenate(split3(x), axis=1), jnp.concatenate([fold] * 3, axis=0))


def spread(x, fold):
    return dot(jnp.concatenate(split3(x), axis=1), jnp.concatenate([fold] * 3, axis=1), ((1,), (1,)))


def bands_kernel(m_ref, places_ref, *refs):
    *matrix_refs, bands_ref = refs
    bands_ref[...] = bands_of(m_ref[...], places_ref[...], *matrix_refs)


def coded(x):
    top = jnp.max(jnp.abs(x), axis=0, keepdims=True)
    exponent = jnp.ceil(jnp.log2(jnp.maximum(top, 1e-30)) + 0.01)
    scaled = x * jnp.exp2(15.0 - exponent)
    values = jnp.clip(jnp.round(scaled), -32767.0, 32767.0).astype(jnp.int32).astype(jnp.int16)
    row = jnp.broadcast_to(exponent, (code_rows, x.shape[1])).astype(jnp.int32).astype(jnp.int16)
    return values, row


def decoded(code_ref, exponents_ref):
    values = code_ref[: code_ref.shape[0] - code_rows].astype(jnp.int32).astype(jnp.float32)
    exponents = exponents_ref[...].astype(jnp.int32).astype(jnp.float32)
    return values * jnp.exp2(exponents[:1] - 15.0)


def swapped_kernel(m_ref, far_hidden_ref, cross_hidden_ref, cross_ref, swapped_ref, *out_refs):
    out_ref, helped_ref, own_turned_ref, end_turned_ref, end_places_ref = out_refs
    handed, side = swapped_ref.shape[0] - place_rows, out_ref.shape[0]
    alone = cross_ref.shape[0] - handed
    out_ref[...] = m_ref[...] + dot(cross_hidden_ref[...], swapped_ref[:handed], ((0,), (0,)))
    helped_ref[...] = dot(swapped_ref[:alone, :side], cross_ref[handed:], ((0,), (0,)))
    own_turned_ref[...] = far_hidden_ref[...].T
    end_turned_ref[:, : handed - alone] = swapped_ref[alone:handed, :side].T
    end_turned_ref[:, handed - alone :] = swapped_ref[:handed, side:].T
    end_places_ref[...] = swapped_ref[handed:].astype(jnp.float32)


def helped_kernel(helped_ref, end_turned_ref, far_ref, out_ref, code_ref):
    out_ref[...] = helped_ref[...] + dot(end_turned_ref[...], far_ref[...])
    side = out_ref.shape[0]
    code_ref[:side], code_ref[side:] = coded(out_ref[...])


def last_rows_kernel(m_ref, own_turned_ref, far_ref, helped_ref, places_ref, end_places_ref, *refs):
    fold_ref, *basis_refs, out_ref, bands_ref = refs
    out_ref[...] = m_ref[...] + dot(own_turned_ref[...], far_ref[...])
    rows, width = out_ref.shape
    by_rows = on_rows(basis_refs[0], jnp.concatenate([out_ref[...], helped_ref[...]], axis=1), False)
    masks = [masks_of(places[...], rows // order) for places in (places_ref, end_places_ref)]
    taken = [rows_taken(by_rows[:, i * width :][:, :width], masks[i]) for i in range(2)]
    coefficients = on_columns(basis_refs[-1], jnp.concatenate(taken, axis=0), False)
    bands_ref[...] = folded(within(coefficients, masks[0] + masks[1]), fold_ref[...])


def remove_kernel(count, *refs):
    (m_ref, *code_refs), (end_ref, places_ref, *basis_refs, out_ref) = refs[:count], refs[count:]
    m = m_ref[...]
    if code_refs:
        m = m + jnp.where(end_ref[:1, :] > 0, decoded(*code_refs), 0.0)
    masks = masks_of(places_ref[...], m.shape[0] // order)
    out_ref[...] = m - restored(selected(m, masks, *basis_refs), masks, *basis_refs)


def update_kernel(own_count, count, *refs):
    part_refs, (end_ref, places_ref, fold_ref, *basis_refs, out_ref) = refs[:count], refs[count:]
    parts = [ref[...] for ref in part_refs]
    bands = pair_sum(parts[:own_count])
    if own_count < count:
        bands = bands + jnp.where(end_ref[:1, : bands.shape[1]] > 0, pair_sum(parts[own_count:]), 0.0)
    masks = masks_of(places_ref[...], out_ref.shape[0] // order)
    coefficients = within(spread(bands, fold_ref[...]), masks)
    out_ref[...] = restored(coefficients, masks, *basis_refs).astype(out_ref.dtype)


def pair_sum(parts):
    while len(parts) > 1:
        parts = [sum(parts[i + 1 : i + 2], parts[i]) for i in range(0, len(parts), 2)]
    return parts[0]


def call(kernel, out_shapes, *operands):
    return pl.pallas_call(
        kernel,
        out_shape=out_shapes,
        compiler_params=pltpu.CompilerParams(vmem_limit_bytes=32 * 2**20),
        cost_estimate=pl.CostEstimate(flops=4 * 10**8, bytes_accessed=4 * 10**6, transcendentals=0),
    )(*operands)


def stages_of(axis):
    size, stride, stages = lax.axis_size(axis), 1, []
    while stride < size:
        stages.append((stride, min(4, size // stride)))
        stride *= stages[-1][1]
    return stages


def exchanged(x, axis, stride, count):
    size = lax.axis_size(axis)
    return [lax.ppermute(x, axis, [(i, i ^ (stride * k)) for i in range(size)]) for k in range(1, count)]


def summed_but_last(x, axis, form, then=lambda x: x):
    size = lax.axis_size(axis)
    if size & (size - 1):
        return form(lax.psum(x, axis)), (1, 1)
    *stages, last = stages_of(axis) or [(1, 1)]
    for stride, count in stages:
        x = pair_sum([x] + then(exchanged(x, axis, stride, count)))
    return form(x), last


def product(hidden_rows, grad_rows):
    return dot(hidden_rows, grad_rows, ((0,), (0,)))


def after(x, *others):
    return lax.optimization_barrier((x, *others))[0]


def gathered(hidden, out_grad, carried, places, matrices):
    m = carried + product(hidden, lax.all_gather(out_grad, "tp", axis=0, tiled=True))
    folded = jax.ShapeDtypeStruct((m.shape[0] // steps, m.shape[1] // steps), jnp.float32)
    bands, last = summed_but_last(call(bands_kernel, folded, m, places, *matrices), "rep", lambda x: x)
    parts = [bands] + exchanged(bands, "rep", *last)
    return [m], parts, len(parts), jnp.zeros((8, m.shape[1]), jnp.float32), places, matrices


def lined(hidden, out_grad, carried, places, matrices):
    tok = out_grad.shape[0]
    me = lax.axis_index("tp")
    left = me < 2
    end = (me == 0) | (me == 3)
    cross = jnp.where(left, 2, 1)
    far = jnp.where(left, 3, 0)
    handed = tok * 2 // 3
    alone = tok - handed

    def rows_of(part, start=0, stop=tok):
        return lax.dynamic_slice_in_dim(hidden, part * tok + start, stop - start, 0)

    def send(x, perm):
        return lax.ppermute(x, "tp", perm)

    both_ways = [(0, 1), (1, 0), (2, 3), (3, 2)]
    across = [(1, 2), (2, 1)]

    pair_grad = send(out_grad, both_ways)
    cross_grad = send(out_grad, across)
    m = carried + product(rows_of(me), out_grad)
    far_hidden = rows_of(far)
    helped_hidden = jnp.concatenate(
        [
            jnp.concatenate([rows_of(cross, handed), far_hidden[: handed - alone]], axis=0),
            far_hidden[handed - alone :],
        ],
        axis=1,
    )
    place_part = jnp.pad(places.astype(hidden.dtype), ((0, place_rows - places.shape[0]), (0, 0)))
    helped_hidden = jnp.concatenate([helped_hidden, place_part], axis=0)
    cross_hidden = jnp.where(end, rows_of(cross, 0, handed), 0)
    helped_hidden, cross_hidden, m = lax.optimization_barrier((helped_hidden, cross_hidden, m))

    far_grad = send(pair_grad, across)
    cross_grad, matrices, places = after((cross_grad, matrices, places), pair_grad, m)
    swapped = send(jnp.where(end, helped_hidden, cross_grad[: handed + place_rows]), both_ways)
    m = m + product(rows_of(me ^ 1), pair_grad) + product(rows_of(cross), cross_grad)

    height, width = m.shape[0] // steps, m.shape[1] // steps
    full = jax.ShapeDtypeStruct(m.shape, jnp.float32)
    turned = jax.ShapeDtypeStruct((m.shape[0], tok), hidden.dtype)
    table = jax.ShapeDtypeStruct((place_rows, m.shape[1]), jnp.float32)
    m, helped, own_turned, end_turned, end_places = call(
        swapped_kernel, (full, full, turned, turned, table), m, far_hidden, cross_hidden, cross_grad, swapped
    )
    far_grad = after(far_grad, m)
    code_shape = jax.ShapeDtypeStruct((m.shape[0] + code_rows, m.shape[1]), jnp.int16)
    helped, code = call(helped_kernel, (full, code_shape), helped, end_turned, far_grad)
    code = send(code, both_ways)
    folded = jax.ShapeDtypeStruct((2 * height, width), jnp.float32)
    m, bands = call(
        last_rows_kernel, (full, folded), m, own_turned, far_grad, helped, places, end_places, *matrices
    )
    exponents = code[m.shape[0] :]

    def behind_code(x):
        nonlocal exponents
        x, exponents = lax.optimization_barrier((x, exponents))
        return x

    (bands, end_bands), (stride, count) = summed_but_last(
        bands, "rep", lambda x: (x[:height], x[height:]), behind_code
    )
    parts = [bands] + exchanged(bands, "rep", stride, count)
    end_flag = jnp.full((8, m.shape[1]), end, jnp.float32)
    for k in range(count):
        perm = [
            (i * 4 + a, (i ^ (stride * k)) * 4 + b) for i in range(lax.axis_size("rep")) for a, b in both_ways
        ]
        parts.append(lax.ppermute(end_bands, ("rep", "tp"), perm))
    return [m, code, exponents], parts, count, end_flag, places, matrices


def local(hidden, out_grad, momentum, band_rows, band_start_columns):
    row_count = hidden.shape[1]
    col_count = out_grad.shape[1]
    one_hot = jnp.asarray(np.kron(np.eye(col_count // order), np.ones((1, order))), jnp.float32)
    bases = [diagonal_blocks(row_count), diagonal_blocks(col_count)]
    if bases[0].shape == bases[1].shape:
        bases = bases[:1]
    matrices = tuple(jnp.asarray(x) for x in (fold_matrix(col_count), *bases))
    places = jnp.concatenate([band_rows, band_start_columns], axis=0).astype(jnp.float32)
    places = dot(places, one_hot)
    fits = out_grad.shape[0] % 384 == 0 and 2 * row_count == col_count and places.shape[0] <= place_rows
    form = lined if fits and lax.axis_size("tp") == 4 else gathered
    m_parts, band_parts, own_count, end_flag, places, matrices = form(
        hidden, out_grad, decay_rate * momentum[0], places, matrices
    )
    shape = (row_count, col_count)
    momentum_out = call(
        functools.partial(remove_kernel, len(m_parts)),
        jax.ShapeDtypeStruct(shape, jnp.float32),
        *m_parts,
        end_flag,
        places,
        *matrices[1:],
    )
    *band_parts, momentum_out = lax.optimization_barrier((*band_parts, momentum_out))
    update = call(
        functools.partial(update_kernel, own_count, len(band_parts)),
        jax.ShapeDtypeStruct(shape, jnp.bfloat16),
        *band_parts,
        end_flag,
        places,
        *matrices,
    )
    return (momentum_out[None], update)


def solution(mesh):
    return jax.shard_map(
        local,
        mesh=mesh,
        in_specs=(
            P("rep", "tp"),
            P(("rep", "tp"), None),
            P("rep", "tp", None),
            P("tp", None),
            P("tp", None),
        ),
        out_specs=(P("rep", "tp", None), P("tp", None)),
        check_vma=False,
    )
```

```python
import functools

import jax
import jax.numpy as jnp
import numpy as np
from jax import lax
from jax.experimental import pallas as pl
from jax.experimental.pallas import tpu as pltpu
from jax.sharding import PartitionSpec as P

decay_rate = 0.9
order = 64
band = 16
steps = order // band
place_rows = 16
code_rows = 16


def basis_matrix():
    frequency = np.arange(order, dtype=np.float64)[:, None]
    sample_pos = np.arange(order, dtype=np.float64)[None, :]
    norm_scale = np.where(frequency == 0, np.sqrt(1.0 / order), np.sqrt(2.0 / order))
    return norm_scale * np.cos(np.pi * (sample_pos + 0.5) * frequency / order)


def diagonal_blocks(width):
    count = next(c for c in (4, 2, 1) if width % (c * order) == 0)
    return np.kron(np.eye(count), basis_matrix()).astype(np.float32)


def fold_matrix(width):
    return np.kron(np.eye(width // order), np.kron(np.ones((steps, 1)), np.eye(band))).astype(jnp.bfloat16)


def split2(x):
    high = x.astype(jnp.bfloat16)
    return high, (x - high.astype(jnp.float32)).astype(jnp.bfloat16)


def split3(x):
    high, low = split2(x)
    rest = x - high.astype(jnp.float32) - low.astype(jnp.float32)
    return high, low, rest.astype(jnp.bfloat16)


def dot(a, b, dims=((1,), (0,))):
    return lax.dot_general(a, b, (dims, ((), ())), preferred_element_type=jnp.float32)


def dot3(a, b, dims=((1,), (0,))):
    (a_high, a_low), (b_high, b_low) = a, b
    left = jnp.concatenate([a_high, a_low, a_high], axis=dims[0][0])
    right = jnp.concatenate([b_high, b_high, b_low], axis=dims[1][0])
    return dot(left, right, dims)


def on_rows(basis_ref, x, transposed):
    basis, side = split2(basis_ref[...]), basis_ref.shape[0]
    dims = ((0,), (0,)) if transposed else ((1,), (0,))
    parts = [dot3(basis, split2(x[i : i + side]), dims) for i in range(0, x.shape[0], side)]
    return parts[0] if len(parts) == 1 else jnp.concatenate(parts, axis=0)


def on_columns(basis_ref, x, transposed):
    basis, side = split2(basis_ref[...]), basis_ref.shape[0]
    dims = ((1,), (0,)) if transposed else ((1,), (1,))
    parts = [dot3(split2(x[:, i : i + side]), basis, dims) for i in range(0, x.shape[1], side)]
    return parts[0] if len(parts) == 1 else jnp.concatenate(parts, axis=1)


def masks_of(places, count):
    width = places.shape[1]
    column = lax.rem(lax.broadcasted_iota(jnp.int32, (band, width), 1), order).astype(jnp.float32)
    masks = []
    for row in range(count):
        start = places[count + row : count + row + 1, :]
        masks.append((places[row : row + 1, :], (column >= start) & (column < start + band)))
    return masks


def rows_taken(x, masks):
    pieces = []
    for row, (at, _) in enumerate(masks):
        taken = jnp.zeros((band, x.shape[1]), jnp.float32)
        for step in range(steps):
            start = row * order + step * band
            taken = jnp.where(at == step * band, x[start : start + band], taken)
        pieces.append(taken)
    return jnp.concatenate(pieces, axis=0)


def selected(x, masks, *basis_refs):
    taken = rows_taken(on_rows(basis_refs[0], x, False), masks)
    return within(on_columns(basis_refs[-1], taken, False), masks)


def within(x, masks):
    return jnp.concatenate(
        [jnp.where(inside, x[i * band : (i + 1) * band], 0.0) for i, (_, inside) in enumerate(masks)], axis=0
    )


def restored(x, masks, *basis_refs):
    by_columns = on_columns(basis_refs[-1], x, True)
    pieces = []
    for row, (at, _) in enumerate(masks):
        part = by_columns[row * band : (row + 1) * band]
        pieces += [jnp.where(at == step * band, part, 0.0) for step in range(steps)]
    return on_rows(basis_refs[0], jnp.concatenate(pieces, axis=0), True)


def bands_of(x, places, fold_ref, *basis_refs):
    return folded(selected(x, masks_of(places, x.shape[0] // order), *basis_refs), fold_ref[...])


def folded(x, fold):
    return dot(jnp.concatenate(split3(x), axis=1), jnp.concatenate([fold] * 3, axis=0))


def spread(x, fold):
    return dot(jnp.concatenate(split3(x), axis=1), jnp.concatenate([fold] * 3, axis=1), ((1,), (1,)))


def bands_kernel(m_ref, places_ref, *refs):
    *matrix_refs, bands_ref = refs
    bands_ref[...] = bands_of(m_ref[...], places_ref[...], *matrix_refs)


def coded(x):
    top = jnp.max(jnp.abs(x), axis=0, keepdims=True)
    exponent = jnp.ceil(jnp.log2(jnp.maximum(top, 1e-30)) + 0.01)
    scaled = x * jnp.exp2(15.0 - exponent)
    values = jnp.clip(jnp.round(scaled), -32767.0, 32767.0).astype(jnp.int32).astype(jnp.int16)
    row = jnp.broadcast_to(exponent, (code_rows, x.shape[1])).astype(jnp.int32).astype(jnp.int16)
    return values, row


def decoded(code_ref, exponents_ref):
    values = code_ref[: code_ref.shape[0] - code_rows].astype(jnp.int32).astype(jnp.float32)
    exponents = exponents_ref[...].astype(jnp.int32).astype(jnp.float32)
    return values * jnp.exp2(exponents[:1] - 15.0)


def swapped_kernel(m_ref, far_hidden_ref, cross_hidden_ref, cross_ref, swapped_ref, places_ref, *refs):
    *matrix_refs, out_ref, helped_ref, own_turned_ref, end_turned_ref, end_places_ref, bands_ref = refs
    handed, side = swapped_ref.shape[0] - place_rows, out_ref.shape[0]
    alone = cross_ref.shape[0] - handed
    out_ref[...] = m_ref[...] + dot(cross_hidden_ref[...], swapped_ref[:handed], ((0,), (0,)))
    helped_ref[...] = dot(swapped_ref[:alone, :side], cross_ref[handed:], ((0,), (0,)))
    own_turned_ref[...] = far_hidden_ref[...].T
    end_turned_ref[:, : handed - alone] = swapped_ref[alone:handed, :side].T
    end_turned_ref[:, handed - alone :] = swapped_ref[:handed, side:].T
    end_places_ref[...] = swapped_ref[handed:].astype(jnp.float32)
    bands_ref[...] = bands_of(out_ref[...], places_ref[...], *matrix_refs)


def helped_kernel(helped_ref, end_turned_ref, far_ref, out_ref, code_ref):
    out_ref[...] = helped_ref[...] + dot(end_turned_ref[...], far_ref[...])
    side = out_ref.shape[0]
    code_ref[:side], code_ref[side:] = coded(out_ref[...])


def last_rows_kernel(end_ref, m_ref, own_bands_ref, own_turned_ref, far_ref, helped_ref, *refs):
    places_ref, end_places_ref, fold_ref, *basis_refs, out_ref, bands_ref = refs
    rows, width = out_ref.shape
    count = own_bands_ref.shape[0]

    @pl.when(end_ref[0] == 1)
    def _():
        out_ref[...] = m_ref[...]
        bands_ref[:count] = own_bands_ref[...]
        bands_ref[count:] = jnp.zeros_like(own_bands_ref)

    @pl.when(end_ref[0] == 0)
    def _():
        out_ref[...] = m_ref[...] + dot(own_turned_ref[...], far_ref[...])
        both = jnp.concatenate([out_ref[...], helped_ref[...]], axis=1)
        by_rows = on_rows(basis_refs[0], both, False)
        masks = [masks_of(places[...], rows // order) for places in (places_ref, end_places_ref)]
        taken = [rows_taken(by_rows[:, i * width :][:, :width], masks[i]) for i in range(2)]
        coefficients = on_columns(basis_refs[-1], jnp.concatenate(taken, axis=0), False)
        bands_ref[...] = folded(within(coefficients, masks[0] + masks[1]), fold_ref[...])


def remove_kernel(count, *refs):
    (m_ref, *code_refs), (end_ref, places_ref, *basis_refs, out_ref) = refs[:count], refs[count:]
    m = m_ref[...]
    if code_refs:
        m = m + jnp.where(end_ref[:1, :] > 0, decoded(*code_refs), 0.0)
    masks = masks_of(places_ref[...], m.shape[0] // order)
    out_ref[...] = m - restored(selected(m, masks, *basis_refs), masks, *basis_refs)


def update_kernel(own_count, count, *refs):
    part_refs, (end_ref, places_ref, fold_ref, *basis_refs, out_ref) = refs[:count], refs[count:]
    parts = [ref[...] for ref in part_refs]
    bands = pair_sum(parts[:own_count])
    if own_count < count:
        bands = bands + jnp.where(end_ref[:1, : bands.shape[1]] > 0, pair_sum(parts[own_count:]), 0.0)
    masks = masks_of(places_ref[...], out_ref.shape[0] // order)
    coefficients = within(spread(bands, fold_ref[...]), masks)
    out_ref[...] = restored(coefficients, masks, *basis_refs).astype(out_ref.dtype)


def pair_sum(parts):
    while len(parts) > 1:
        parts = [sum(parts[i + 1 : i + 2], parts[i]) for i in range(0, len(parts), 2)]
    return parts[0]


def call(kernel, out_shapes, *operands):
    spaces = [pltpu.SMEM if x.dtype == jnp.int32 else pltpu.VMEM for x in operands]
    return pl.pallas_call(
        kernel,
        out_shape=out_shapes,
        in_specs=[pl.BlockSpec(memory_space=space) for space in spaces],
        compiler_params=pltpu.CompilerParams(vmem_limit_bytes=32 * 2**20),
        cost_estimate=pl.CostEstimate(flops=4 * 10**8, bytes_accessed=4 * 10**6, transcendentals=0),
    )(*operands)


def stages_of(axis):
    size, stride, stages = lax.axis_size(axis), 1, []
    while stride < size:
        stages.append((stride, min(4, size // stride)))
        stride *= stages[-1][1]
    return stages


def exchanged(x, axis, stride, count):
    size = lax.axis_size(axis)
    return [lax.ppermute(x, axis, [(i, i ^ (stride * k)) for i in range(size)]) for k in range(1, count)]


def summed_but_last(x, axis, form, then=lambda x: x):
    size = lax.axis_size(axis)
    if size & (size - 1):
        return form(lax.psum(x, axis)), (1, 1)
    *stages, last = stages_of(axis) or [(1, 1)]
    for stride, count in stages:
        x = pair_sum([x] + then(exchanged(x, axis, stride, count)))
    return form(x), last


def product(hidden_rows, grad_rows):
    return dot(hidden_rows, grad_rows, ((0,), (0,)))


def after(x, *others):
    return lax.optimization_barrier((x, *others))[0]


def gathered(hidden, out_grad, carried, places, matrices):
    m = carried + product(hidden, lax.all_gather(out_grad, "tp", axis=0, tiled=True))
    folded = jax.ShapeDtypeStruct((m.shape[0] // steps, m.shape[1] // steps), jnp.float32)
    bands, last = summed_but_last(call(bands_kernel, folded, m, places, *matrices), "rep", lambda x: x)
    parts = [bands] + exchanged(bands, "rep", *last)
    return [m], parts, len(parts), jnp.zeros((8, m.shape[1]), jnp.float32), places, matrices


def lined(hidden, out_grad, carried, places, matrices):
    tok = out_grad.shape[0]
    me = lax.axis_index("tp")
    left = me < 2
    end = (me == 0) | (me == 3)
    cross = jnp.where(left, 2, 1)
    far = jnp.where(left, 3, 0)
    handed = tok * 2 // 3
    alone = tok - handed

    def rows_of(part, start=0, stop=tok):
        return lax.dynamic_slice_in_dim(hidden, part * tok + start, stop - start, 0)

    def send(x, perm):
        return lax.ppermute(x, "tp", perm)

    both_ways = [(0, 1), (1, 0), (2, 3), (3, 2)]
    across = [(1, 2), (2, 1)]

    pair_grad = send(out_grad, both_ways)
    cross_grad = send(out_grad, across)
    m = carried + product(rows_of(me), out_grad)
    far_hidden = rows_of(far)
    helped_hidden = jnp.concatenate(
        [
            jnp.concatenate([rows_of(cross, handed), far_hidden[: handed - alone]], axis=0),
            far_hidden[handed - alone :],
        ],
        axis=1,
    )
    place_part = jnp.pad(places.astype(hidden.dtype), ((0, place_rows - places.shape[0]), (0, 0)))
    helped_hidden = jnp.concatenate([helped_hidden, place_part], axis=0)
    cross_hidden = jnp.where(end, rows_of(cross, 0, handed), 0)
    helped_hidden, cross_hidden, m = lax.optimization_barrier((helped_hidden, cross_hidden, m))

    far_grad = send(pair_grad, across)
    cross_grad, matrices, places = after((cross_grad, matrices, places), pair_grad, m)
    swapped = send(jnp.where(end, helped_hidden, cross_grad[: handed + place_rows]), both_ways)
    m = m + product(rows_of(me ^ 1), pair_grad) + product(rows_of(cross), cross_grad)

    height, width = m.shape[0] // steps, m.shape[1] // steps
    full = jax.ShapeDtypeStruct(m.shape, jnp.float32)
    turned = jax.ShapeDtypeStruct((m.shape[0], tok), hidden.dtype)
    table = jax.ShapeDtypeStruct((place_rows, m.shape[1]), jnp.float32)
    own_bands = jax.ShapeDtypeStruct((height, width), jnp.float32)
    m, helped, own_turned, end_turned, end_places, own_bands = call(
        swapped_kernel,
        (full, full, turned, turned, table, own_bands),
        m,
        far_hidden,
        cross_hidden,
        cross_grad,
        swapped,
        places,
        *matrices,
    )
    far_grad = after(far_grad, m)
    code_shape = jax.ShapeDtypeStruct((m.shape[0] + code_rows, m.shape[1]), jnp.int16)
    helped, code = call(helped_kernel, (full, code_shape), helped, end_turned, far_grad)
    code = send(code, both_ways)
    m, bands = call(
        last_rows_kernel,
        (full, jax.ShapeDtypeStruct((2 * height, width), jnp.float32)),
        end.astype(jnp.int32).reshape(1),
        m,
        own_bands,
        own_turned,
        far_grad,
        helped,
        places,
        end_places,
        *matrices,
    )
    exponents = code[m.shape[0] :]

    def behind_code(x):
        nonlocal exponents
        x, exponents = lax.optimization_barrier((x, exponents))
        return x

    (bands, end_bands), (stride, count) = summed_but_last(
        bands, "rep", lambda x: lax.optimization_barrier((x[:height], x[height:])), behind_code
    )
    own_sum = pair_sum([bands] + exchanged(bands, "rep", stride, count))
    to_ends = []
    for k in range(count):
        perm = [
            (i * 4 + a, (i ^ (stride * k)) * 4 + b) for i in range(lax.axis_size("rep")) for a, b in both_ways
        ]
        to_ends.append(lax.ppermute(end_bands, ("rep", "tp"), perm))
    m, own_sum = lax.optimization_barrier((m, own_sum))
    end_flag = jnp.full((8, m.shape[1]), end, jnp.float32)
    return [m, code, exponents], [own_sum] + to_ends, 1, end_flag, places, matrices


def local(hidden, out_grad, momentum, band_rows, band_start_columns):
    row_count = hidden.shape[1]
    col_count = out_grad.shape[1]
    one_hot = jnp.asarray(np.kron(np.eye(col_count // order), np.ones((1, order))), jnp.float32)
    bases = [diagonal_blocks(row_count), diagonal_blocks(col_count)]
    if bases[0].shape == bases[1].shape:
        bases = bases[:1]
    matrices = tuple(jnp.asarray(x) for x in (fold_matrix(col_count), *bases))
    places = jnp.concatenate([band_rows, band_start_columns], axis=0).astype(jnp.float32)
    places = dot(places, one_hot)
    fits = out_grad.shape[0] % 384 == 0 and 2 * row_count == col_count and places.shape[0] <= place_rows
    form = lined if fits and lax.axis_size("tp") == 4 else gathered
    m_parts, band_parts, own_count, end_flag, places, matrices = form(
        hidden, out_grad, decay_rate * momentum[0], places, matrices
    )
    shape = (row_count, col_count)
    momentum_out = call(
        functools.partial(remove_kernel, len(m_parts)),
        jax.ShapeDtypeStruct(shape, jnp.float32),
        *m_parts,
        end_flag,
        places,
        *matrices[1:],
    )
    *band_parts, momentum_out = lax.optimization_barrier((*band_parts, momentum_out))
    update = call(
        functools.partial(update_kernel, own_count, len(band_parts)),
        jax.ShapeDtypeStruct(shape, jnp.bfloat16),
        *band_parts,
        end_flag,
        places,
        *matrices,
    )
    return (momentum_out[None], update)


def solution(mesh):
    return jax.shard_map(
        local,
        mesh=mesh,
        in_specs=(
            P("rep", "tp"),
            P(("rep", "tp"), None),
            P("rep", "tp", None),
            P("tp", None),
            P("tp", None),
        ),
        out_specs=(P("rep", "tp", None), P("tp", None)),
        check_vma=False,
    )
```

```python
import functools

import jax
import jax.numpy as jnp
import numpy as np
from jax import lax
from jax.experimental import pallas as pl
from jax.experimental.pallas import tpu as pltpu
from jax.sharding import PartitionSpec as P

decay_rate = 0.9
order = 64
band = 16
steps = order // band
place_rows = 16
code_rows = 16


def basis_matrix():
    frequency = np.arange(order, dtype=np.float64)[:, None]
    sample_pos = np.arange(order, dtype=np.float64)[None, :]
    norm_scale = np.where(frequency == 0, np.sqrt(1.0 / order), np.sqrt(2.0 / order))
    return norm_scale * np.cos(np.pi * (sample_pos + 0.5) * frequency / order)


def diagonal_blocks(width):
    count = next(c for c in (4, 2, 1) if width % (c * order) == 0)
    return np.kron(np.eye(count), basis_matrix()).astype(np.float32)


def fold_matrix(width):
    return np.kron(np.eye(width // order), np.kron(np.ones((steps, 1)), np.eye(band))).astype(jnp.bfloat16)


def split2(x):
    high = x.astype(jnp.bfloat16)
    return high, (x - high.astype(jnp.float32)).astype(jnp.bfloat16)


def split3(x):
    high, low = split2(x)
    rest = x - high.astype(jnp.float32) - low.astype(jnp.float32)
    return high, low, rest.astype(jnp.bfloat16)


def dot(a, b, dims=((1,), (0,))):
    return lax.dot_general(a, b, (dims, ((), ())), preferred_element_type=jnp.float32)


def dot3(a, b, dims=((1,), (0,))):
    (a_high, a_low), (b_high, b_low) = a, b
    left = jnp.concatenate([a_high, a_low, a_high], axis=dims[0][0])
    right = jnp.concatenate([b_high, b_high, b_low], axis=dims[1][0])
    return dot(left, right, dims)


def on_rows(basis_ref, x, transposed):
    basis, side = split2(basis_ref[...]), basis_ref.shape[0]
    dims = ((0,), (0,)) if transposed else ((1,), (0,))
    parts = [dot3(basis, split2(x[i : i + side]), dims) for i in range(0, x.shape[0], side)]
    return parts[0] if len(parts) == 1 else jnp.concatenate(parts, axis=0)


def on_columns(basis_ref, x, transposed):
    basis, side = split2(basis_ref[...]), basis_ref.shape[0]
    dims = ((1,), (0,)) if transposed else ((1,), (1,))
    parts = [dot3(split2(x[:, i : i + side]), basis, dims) for i in range(0, x.shape[1], side)]
    return parts[0] if len(parts) == 1 else jnp.concatenate(parts, axis=1)


def masks_of(places, count):
    width = places.shape[1]
    column = lax.rem(lax.broadcasted_iota(jnp.int32, (band, width), 1), order).astype(jnp.float32)
    masks = []
    for row in range(count):
        start = places[count + row : count + row + 1, :]
        masks.append((places[row : row + 1, :], (column >= start) & (column < start + band)))
    return masks


def rows_taken(x, masks):
    pieces = []
    for row, (at, _) in enumerate(masks):
        taken = jnp.zeros((band, x.shape[1]), jnp.float32)
        for step in range(steps):
            start = row * order + step * band
            taken = jnp.where(at == step * band, x[start : start + band], taken)
        pieces.append(taken)
    return jnp.concatenate(pieces, axis=0)


def selected(x, masks, *basis_refs):
    taken = rows_taken(on_rows(basis_refs[0], x, False), masks)
    return within(on_columns(basis_refs[-1], taken, False), masks)


def within(x, masks):
    return jnp.concatenate(
        [jnp.where(inside, x[i * band : (i + 1) * band], 0.0) for i, (_, inside) in enumerate(masks)], axis=0
    )


def restored(x, masks, *basis_refs):
    by_columns = on_columns(basis_refs[-1], x, True)
    pieces = []
    for row, (at, _) in enumerate(masks):
        part = by_columns[row * band : (row + 1) * band]
        pieces += [jnp.where(at == step * band, part, 0.0) for step in range(steps)]
    return on_rows(basis_refs[0], jnp.concatenate(pieces, axis=0), True)


def bands_of(x, places, fold_ref, *basis_refs):
    return folded(selected(x, masks_of(places, x.shape[0] // order), *basis_refs), fold_ref[...])


def folded(x, fold):
    return dot(jnp.concatenate(split3(x), axis=1), jnp.concatenate([fold] * 3, axis=0))


def spread(x, fold):
    return dot(jnp.concatenate(split3(x), axis=1), jnp.concatenate([fold] * 3, axis=1), ((1,), (1,)))


def bands_kernel(m_ref, places_ref, *refs):
    *matrix_refs, bands_ref = refs
    bands_ref[...] = bands_of(m_ref[...], places_ref[...], *matrix_refs)


def coded(x):
    top = jnp.max(jnp.abs(x), axis=0, keepdims=True)
    exponent = jnp.ceil(jnp.log2(jnp.maximum(top, 1e-30)) + 0.01)
    scaled = x * jnp.exp2(15.0 - exponent)
    values = jnp.clip(jnp.round(scaled), -32767.0, 32767.0).astype(jnp.int32).astype(jnp.int16)
    row = jnp.broadcast_to(exponent, (code_rows, x.shape[1])).astype(jnp.int32).astype(jnp.int16)
    return values, row


def decoded(code_ref, exponents_ref):
    values = code_ref[: code_ref.shape[0] - code_rows].astype(jnp.int32).astype(jnp.float32)
    exponents = exponents_ref[...].astype(jnp.int32).astype(jnp.float32)
    return values * jnp.exp2(exponents[:1] - 15.0)


def swapped_kernel(m_ref, far_hidden_ref, cross_hidden_ref, cross_ref, swapped_ref, *out_refs):
    out_ref, helped_ref, own_turned_ref, end_turned_ref, end_places_ref = out_refs
    handed, side = swapped_ref.shape[0] - place_rows, out_ref.shape[0]
    alone = cross_ref.shape[0] - handed
    out_ref[...] = m_ref[...] + dot(cross_hidden_ref[...], swapped_ref[:handed], ((0,), (0,)))
    helped_ref[...] = dot(swapped_ref[:alone, :side], cross_ref[handed:], ((0,), (0,)))
    own_turned_ref[...] = far_hidden_ref[...].T
    end_turned_ref[:, : handed - alone] = swapped_ref[alone:handed, :side].T
    end_turned_ref[:, handed - alone :] = swapped_ref[:handed, side:].T
    end_places_ref[...] = swapped_ref[handed:].astype(jnp.float32)


def helped_kernel(helped_ref, end_turned_ref, far_ref, out_ref, code_ref):
    out_ref[...] = helped_ref[...] + dot(end_turned_ref[...], far_ref[...])
    side = out_ref.shape[0]
    code_ref[:side], code_ref[side:] = coded(out_ref[...])


def last_rows_kernel(m_ref, own_turned_ref, far_ref, helped_ref, places_ref, end_places_ref, *refs):
    fold_ref, *basis_refs, out_ref, bands_ref = refs
    out_ref[...] = m_ref[...] + dot(own_turned_ref[...], far_ref[...])
    rows, width = out_ref.shape
    by_rows = on_rows(basis_refs[0], jnp.concatenate([out_ref[...], helped_ref[...]], axis=1), False)
    masks = [masks_of(places[...], rows // order) for places in (places_ref, end_places_ref)]
    taken = [rows_taken(by_rows[:, i * width :][:, :width], masks[i]) for i in range(2)]
    coefficients = on_columns(basis_refs[-1], jnp.concatenate(taken, axis=0), False)
    bands_ref[...] = folded(within(coefficients, masks[0] + masks[1]), fold_ref[...])


def remove_kernel(count, *refs):
    (m_ref, *code_refs), (end_ref, places_ref, *basis_refs, out_ref) = refs[:count], refs[count:]
    m = m_ref[...]
    if code_refs:
        m = m + jnp.where(end_ref[:1, :] > 0, decoded(*code_refs), 0.0)
    masks = masks_of(places_ref[...], m.shape[0] // order)
    out_ref[...] = m - restored(selected(m, masks, *basis_refs), masks, *basis_refs)


def update_kernel(own_count, count, *refs):
    part_refs, (end_ref, places_ref, fold_ref, *basis_refs, out_ref) = refs[:count], refs[count:]
    parts = [ref[...] for ref in part_refs]
    bands = pair_sum(parts[:own_count])
    if own_count < count:
        bands = bands + jnp.where(end_ref[:1, : bands.shape[1]] > 0, pair_sum(parts[own_count:]), 0.0)
    masks = masks_of(places_ref[...], out_ref.shape[0] // order)
    coefficients = within(spread(bands, fold_ref[...]), masks)
    out_ref[...] = restored(coefficients, masks, *basis_refs).astype(out_ref.dtype)


def pair_sum(parts):
    while len(parts) > 1:
        parts = [sum(parts[i + 1 : i + 2], parts[i]) for i in range(0, len(parts), 2)]
    return parts[0]


def call(kernel, out_shapes, *operands):
    return pl.pallas_call(
        kernel,
        out_shape=out_shapes,
        compiler_params=pltpu.CompilerParams(vmem_limit_bytes=16 * 2**20),
        cost_estimate=pl.CostEstimate(flops=4 * 10**8, bytes_accessed=4 * 10**6, transcendentals=0),
    )(*operands)


def stages_of(axis):
    size, stride, stages = lax.axis_size(axis), 2, []
    while stride < size:
        stages.append((stride, min(4, size // stride)))
        stride *= stages[-1][1]
    return stages + [(1, min(2, size))]


def exchanged(x, axis, stride, count):
    size = lax.axis_size(axis)
    return [lax.ppermute(x, axis, [(i, i ^ (stride * k)) for i in range(size)]) for k in range(1, count)]


def summed_but_last(x, axis, form, then=lambda x: x):
    size = lax.axis_size(axis)
    if size & (size - 1):
        return form(lax.psum(x, axis)), (1, 1)
    *stages, last = stages_of(axis)
    for stride, count in stages:
        x = pair_sum([x] + then(exchanged(x, axis, stride, count)))
    return form(x), last


def product(hidden_rows, grad_rows):
    return dot(hidden_rows, grad_rows, ((0,), (0,)))


def after(x, *others):
    return lax.optimization_barrier((x, *others))[0]


def gathered(hidden, out_grad, carried, places, matrices):
    m = carried + product(hidden, lax.all_gather(out_grad, "tp", axis=0, tiled=True))
    folded = jax.ShapeDtypeStruct((m.shape[0] // steps, m.shape[1] // steps), jnp.float32)
    bands, last = summed_but_last(call(bands_kernel, folded, m, places, *matrices), "rep", lambda x: x)
    parts = [bands] + exchanged(bands, "rep", *last)
    return [m], parts, len(parts), jnp.zeros((8, m.shape[1]), jnp.float32), places, matrices


def lined(hidden, out_grad, carried, places, matrices):
    tok = out_grad.shape[0]
    me = lax.axis_index("tp")
    left = me < 2
    end = (me == 0) | (me == 3)
    cross = jnp.where(left, 2, 1)
    far = jnp.where(left, 3, 0)
    handed = tok * 2 // 3
    alone = tok - handed

    def rows_of(part, start=0, stop=tok):
        return lax.dynamic_slice_in_dim(hidden, part * tok + start, stop - start, 0)

    def send(x, perm):
        return lax.ppermute(x, "tp", perm)

    both_ways = [(0, 1), (1, 0), (2, 3), (3, 2)]
    across = [(1, 2), (2, 1)]
    outward = [(1, 0), (2, 3)]

    pair_grad = send(out_grad, both_ways)
    cross_grad = send(out_grad, across)
    m = carried + product(rows_of(me), out_grad)
    far_hidden = rows_of(far)
    helped_hidden = jnp.concatenate(
        [
            jnp.concatenate([rows_of(cross, handed), far_hidden[: handed - alone]], axis=0),
            far_hidden[handed - alone :],
        ],
        axis=1,
    )
    place_part = jnp.pad(places.astype(hidden.dtype), ((0, place_rows - places.shape[0]), (0, 0)))
    helped_hidden = jnp.concatenate([helped_hidden, place_part], axis=0)
    cross_hidden = jnp.where(end, rows_of(cross, 0, handed), 0)
    helped_hidden, cross_hidden, m = lax.optimization_barrier((helped_hidden, cross_hidden, m))

    far_grad = send(pair_grad, across)
    cross_grad, matrices, places = after((cross_grad, matrices, places), pair_grad, m)
    swapped = send(jnp.where(end, helped_hidden, cross_grad[: handed + place_rows]), both_ways)
    m = m + product(rows_of(me ^ 1), pair_grad) + product(rows_of(cross), cross_grad)

    height, width = m.shape[0] // steps, m.shape[1] // steps
    full = jax.ShapeDtypeStruct(m.shape, jnp.float32)
    turned = jax.ShapeDtypeStruct((m.shape[0], tok), hidden.dtype)
    table = jax.ShapeDtypeStruct((place_rows, m.shape[1]), jnp.float32)
    m, helped, own_turned, end_turned, end_places = call(
        swapped_kernel, (full, full, turned, turned, table), m, far_hidden, cross_hidden, cross_grad, swapped
    )
    far_grad = after(far_grad, m)
    code_shape = jax.ShapeDtypeStruct((m.shape[0] + code_rows, m.shape[1]), jnp.int16)
    helped, code = call(helped_kernel, (full, code_shape), helped, end_turned, far_grad)
    code = send(code, outward)
    folded = jax.ShapeDtypeStruct((2 * height, width), jnp.float32)
    m, bands = call(
        last_rows_kernel, (full, folded), m, own_turned, far_grad, helped, places, end_places, *matrices
    )
    exponents = code[m.shape[0] :]

    def behind_code(x):
        nonlocal exponents
        x, exponents = lax.optimization_barrier((x, exponents))
        return x

    (bands, end_bands), (stride, count) = summed_but_last(
        bands, "rep", lambda x: lax.optimization_barrier((x[:height], x[height:])), behind_code
    )
    own_sum = pair_sum([bands] + exchanged(bands, "rep", stride, count))
    to_ends = []
    for k in range(count):
        perm = [
            (i * 4 + a, (i ^ (stride * k)) * 4 + b) for i in range(lax.axis_size("rep")) for a, b in both_ways
        ]
        to_ends.append(lax.ppermute(end_bands, ("rep", "tp"), perm))
    m, own_sum = lax.optimization_barrier((m, own_sum))
    end_flag = jnp.full((8, m.shape[1]), end, jnp.float32)
    return [m, code, exponents], [own_sum] + to_ends, 1, end_flag, places, matrices


def local(hidden, out_grad, momentum, band_rows, band_start_columns):
    row_count = hidden.shape[1]
    col_count = out_grad.shape[1]
    one_hot = jnp.asarray(np.kron(np.eye(col_count // order), np.ones((1, order))), jnp.float32)
    bases = [diagonal_blocks(row_count), diagonal_blocks(col_count)]
    if bases[0].shape == bases[1].shape:
        bases = bases[:1]
    matrices = tuple(jnp.asarray(x) for x in (fold_matrix(col_count), *bases))
    places = jnp.concatenate([band_rows, band_start_columns], axis=0).astype(jnp.float32)
    places = dot(places, one_hot)
    fits = out_grad.shape[0] % 384 == 0 and 2 * row_count == col_count and places.shape[0] <= place_rows
    form = lined if fits and lax.axis_size("tp") == 4 else gathered
    m_parts, band_parts, own_count, end_flag, places, matrices = form(
        hidden, out_grad, decay_rate * momentum[0], places, matrices
    )
    shape = (row_count, col_count)
    momentum_out = call(
        functools.partial(remove_kernel, len(m_parts)),
        jax.ShapeDtypeStruct(shape, jnp.float32),
        *m_parts,
        end_flag,
        places,
        *matrices[1:],
    )
    *band_parts, momentum_out = lax.optimization_barrier((*band_parts, momentum_out))
    update = call(
        functools.partial(update_kernel, own_count, len(band_parts)),
        jax.ShapeDtypeStruct(shape, jnp.bfloat16),
        *band_parts,
        end_flag,
        places,
        *matrices,
    )
    return (momentum_out[None], update)


def solution(mesh):
    return jax.shard_map(
        local,
        mesh=mesh,
        in_specs=(
            P("rep", "tp"),
            P(("rep", "tp"), None),
            P("rep", "tp", None),
            P("tp", None),
            P("tp", None),
        ),
        out_specs=(P("rep", "tp", None), P("tp", None)),
        check_vma=False,
    )
```

```python
import jax
import jax.numpy as jnp
import numpy as np
from jax import lax
from jax.experimental import pallas as pl
from jax.experimental.pallas import tpu as pltpu
from jax.sharding import PartitionSpec as P

decay_rate = 0.9
order = 64
band = 16
steps = order // band
place_rows = 16
code_rows = 16


def basis_matrix():
    frequency = np.arange(order, dtype=np.float64)[:, None]
    sample_pos = np.arange(order, dtype=np.float64)[None, :]
    norm_scale = np.where(frequency == 0, np.sqrt(1.0 / order), np.sqrt(2.0 / order))
    return norm_scale * np.cos(np.pi * (sample_pos + 0.5) * frequency / order)


def diagonal_blocks(*widths):
    count = next(c for c in (4, 2, 1) if all(width % (c * order) == 0 for width in widths))
    return np.kron(np.eye(count), basis_matrix()).astype(np.float32)


def fold_matrix(width):
    return np.kron(np.eye(width // order), np.kron(np.ones((steps, 1)), np.eye(band))).astype(jnp.bfloat16)


def split2(x):
    high = x.astype(jnp.bfloat16)
    return high, (x - high.astype(jnp.float32)).astype(jnp.bfloat16)


def split3(x):
    high, low = split2(x)
    rest = x - high.astype(jnp.float32) - low.astype(jnp.float32)
    return high, low, rest.astype(jnp.bfloat16)


def dot(a, b, dims=((1,), (0,))):
    return lax.dot_general(a, b, (dims, ((), ())), preferred_element_type=jnp.float32)


def dot3(a, b, dims=((1,), (0,))):
    (a_high, a_low), (b_high, b_low) = a, b
    left = jnp.concatenate([a_high, a_low, a_high], axis=dims[0][0])
    right = jnp.concatenate([b_high, b_high, b_low], axis=dims[1][0])
    return dot(left, right, dims)


def on_rows(basis_ref, x, transposed):
    basis, side = split2(basis_ref[...]), basis_ref.shape[0]
    dims = ((0,), (0,)) if transposed else ((1,), (0,))
    parts = [dot3(basis, split2(x[i : i + side]), dims) for i in range(0, x.shape[0], side)]
    return parts[0] if len(parts) == 1 else jnp.concatenate(parts, axis=0)


def on_columns(basis_ref, x, transposed):
    basis, side = split2(basis_ref[...]), basis_ref.shape[0]
    dims = ((1,), (0,)) if transposed else ((1,), (1,))
    parts = [dot3(split2(x[:, i : i + side]), basis, dims) for i in range(0, x.shape[1], side)]
    return parts[0] if len(parts) == 1 else jnp.concatenate(parts, axis=1)


def masks_of(places, count):
    width = places.shape[1]
    column = lax.rem(lax.broadcasted_iota(jnp.int32, (band, width), 1), order).astype(jnp.float32)
    masks = []
    for row in range(count):
        start = places[count + row : count + row + 1, :]
        masks.append((places[row : row + 1, :], (column >= start) & (column < start + band)))
    return masks


def rows_taken(x, masks):
    pieces = []
    for row, (at, _) in enumerate(masks):
        taken = jnp.zeros((band, x.shape[1]), jnp.float32)
        for step in range(steps):
            start = row * order + step * band
            taken = jnp.where(at == step * band, x[start : start + band], taken)
        pieces.append(taken)
    return jnp.concatenate(pieces, axis=0)


def selected(x, masks, basis_ref):
    taken = rows_taken(on_rows(basis_ref, x, False), masks)
    return within(on_columns(basis_ref, taken, False), masks)


def within(x, masks):
    return jnp.concatenate(
        [jnp.where(inside, x[i * band : (i + 1) * band], 0.0) for i, (_, inside) in enumerate(masks)], axis=0
    )


def restored(x, masks, basis_ref):
    by_columns = on_columns(basis_ref, x, True)
    pieces = []
    for row, (at, _) in enumerate(masks):
        part = by_columns[row * band : (row + 1) * band]
        pieces += [jnp.where(at == step * band, part, 0.0) for step in range(steps)]
    return on_rows(basis_ref, jnp.concatenate(pieces, axis=0), True)


def bands_of(x, places, fold_ref, basis_ref):
    return folded(selected(x, masks_of(places, x.shape[0] // order), basis_ref), fold_ref[...])


def folded(x, fold):
    return dot(jnp.concatenate(split3(x), axis=1), jnp.concatenate([fold] * 3, axis=0))


def spread(x, fold):
    return dot(jnp.concatenate(split3(x), axis=1), jnp.concatenate([fold] * 3, axis=1), ((1,), (1,)))


def bands_kernel(m_ref, places_ref, *refs):
    *matrix_refs, bands_ref = refs
    bands_ref[...] = bands_of(m_ref[...], places_ref[...], *matrix_refs)


def coded(x):
    top = jnp.max(jnp.abs(x), axis=0, keepdims=True)
    exponent = jnp.ceil(jnp.log2(jnp.maximum(top, 1e-30)) + 0.01)
    scaled = x * jnp.exp2(15.0 - exponent)
    values = jnp.clip(jnp.round(scaled), -32767.0, 32767.0).astype(jnp.int32).astype(jnp.int16)
    row = jnp.broadcast_to(exponent, (code_rows, x.shape[1])).astype(jnp.int32).astype(jnp.int16)
    return values, row


def decoded(code_ref, exponents_ref):
    values = code_ref[: code_ref.shape[0] - code_rows].astype(jnp.int32).astype(jnp.float32)
    exponents = exponents_ref[...].astype(jnp.int32).astype(jnp.float32)
    return values * jnp.exp2(exponents[:1] - 15.0)


def swapped_kernel(m_ref, far_hidden_ref, cross_hidden_ref, cross_ref, swapped_ref, places_ref, *refs):
    *matrix_refs, out_ref, helped_ref, own_turned_ref, end_turned_ref, end_places_ref, bands_ref = refs
    handed, side = swapped_ref.shape[0] - place_rows, out_ref.shape[0]
    alone = cross_ref.shape[0] - handed
    out_ref[...] = m_ref[...] + dot(cross_hidden_ref[...], swapped_ref[:handed], ((0,), (0,)))
    helped_ref[...] = dot(swapped_ref[:alone, :side], cross_ref[handed:], ((0,), (0,)))
    own_turned_ref[...] = far_hidden_ref[...].T
    end_turned_ref[:, : handed - alone] = swapped_ref[alone:handed, :side].T
    end_turned_ref[:, handed - alone :] = swapped_ref[:handed, side:].T
    end_places_ref[...] = swapped_ref[handed:].astype(jnp.float32)
    bands_ref[...] = bands_of(out_ref[...], places_ref[...], *matrix_refs)


def helped_kernel(helped_ref, turned_ref, far_ref, places_ref, *refs):
    *matrix_refs, code_ref, bands_ref = refs
    product = helped_ref[...] + dot(turned_ref[...], far_ref[...])
    bands_ref[...] = bands_of(product, places_ref[...], *matrix_refs)
    side = product.shape[0]
    code_ref[:side], code_ref[side:] = coded(product)


def last_rows_kernel(end_ref, m_ref, own_bands_ref, turned_ref, far_ref, places_ref, *refs):
    *matrix_refs, out_ref, bands_ref = refs

    @pl.when(end_ref[0] == 1)
    def _():
        out_ref[...] = m_ref[...]
        bands_ref[...] = own_bands_ref[...]

    @pl.when(end_ref[0] == 0)
    def _():
        out_ref[...] = m_ref[...] + dot(turned_ref[...], far_ref[...])
        bands_ref[...] = bands_of(out_ref[...], places_ref[...], *matrix_refs)


def remove_kernel(m_ref, *refs):
    *code_refs, places_ref, basis_ref, out_ref = refs
    m = m_ref[...]
    if code_refs:
        m = m + decoded(*code_refs)
    masks = masks_of(places_ref[...], m.shape[0] // order)
    out_ref[...] = m - restored(selected(m, masks, basis_ref), masks, basis_ref)


def update_kernel(*refs):
    *part_refs, places_ref, fold_ref, basis_ref, out_ref = refs
    bands = pair_sum([ref[...] for ref in part_refs])
    masks = masks_of(places_ref[...], out_ref.shape[0] // order)
    coefficients = within(spread(bands, fold_ref[...]), masks)
    out_ref[...] = restored(coefficients, masks, basis_ref).astype(out_ref.dtype)


def pair_sum(parts):
    while len(parts) > 1:
        parts = [sum(parts[i + 1 : i + 2], parts[i]) for i in range(0, len(parts), 2)]
    return parts[0]


def call(kernel, out_shapes, *operands):
    spaces = [pltpu.SMEM if x.dtype == jnp.int32 else pltpu.VMEM for x in operands]
    return pl.pallas_call(
        kernel,
        out_shape=out_shapes,
        in_specs=[pl.BlockSpec(memory_space=space) for space in spaces],
        compiler_params=pltpu.CompilerParams(vmem_limit_bytes=16 * 2**20),
        cost_estimate=pl.CostEstimate(flops=4 * 10**8, bytes_accessed=4 * 10**6, transcendentals=0),
    )(*operands)


def spread_sum(x, axis, behind=lambda x: x):
    size = lax.axis_size(axis)
    if size & (size - 1):
        return [lax.psum(x, axis)]
    stride, parts = 1, [x]
    while stride < size:
        count = min(4, size // stride)
        x = pair_sum(parts)
        received = [
            lax.ppermute(x, axis, [(i, i ^ (stride * k)) for i in range(size)]) for k in range(1, count)
        ]
        parts = [x] + (behind(received) if stride == 1 else received)
        stride *= count
    return parts


def product(hidden_rows, grad_rows):
    return dot(hidden_rows, grad_rows, ((0,), (0,)))


def after(x, *others):
    return lax.optimization_barrier((x, *others))[0]


def gathered(hidden, out_grad, carried, places, matrices):
    m = carried + product(hidden, lax.all_gather(out_grad, "tp", axis=0, tiled=True))
    folded = jax.ShapeDtypeStruct((m.shape[0] // steps, m.shape[1] // steps), jnp.float32)
    bands = call(bands_kernel, folded, m, places, *matrices)
    return [m], spread_sum(bands, "rep"), places, matrices


def lined(hidden, out_grad, carried, places, matrices):
    tok = out_grad.shape[0]
    me = lax.axis_index("tp")
    left = me < 2
    end = (me == 0) | (me == 3)
    cross = jnp.where(left, 2, 1)
    far = jnp.where(left, 3, 0)
    handed = tok * 2 // 3
    alone = tok - handed

    def rows_of(part, start=0, stop=tok):
        return lax.dynamic_slice_in_dim(hidden, part * tok + start, stop - start, 0)

    def send(x, perm):
        return lax.ppermute(x, "tp", perm)

    both_ways = [(0, 1), (1, 0), (2, 3), (3, 2)]
    across = [(1, 2), (2, 1)]
    outward = [(1, 0), (2, 3)]

    pair_grad = send(out_grad, both_ways)
    cross_grad = send(out_grad, across)
    m = carried + product(rows_of(me), out_grad)
    far_hidden = rows_of(far)
    helped_hidden = jnp.concatenate(
        [
            jnp.concatenate([rows_of(cross, handed), far_hidden[: handed - alone]], axis=0),
            far_hidden[handed - alone :],
        ],
        axis=1,
    )
    place_part = jnp.pad(places.astype(hidden.dtype), ((0, place_rows - places.shape[0]), (0, 0)))
    helped_hidden = jnp.concatenate([helped_hidden, place_part], axis=0)
    cross_hidden = jnp.where(end, rows_of(cross, 0, handed), 0)
    helped_hidden, cross_hidden, m = lax.optimization_barrier((helped_hidden, cross_hidden, m))

    far_grad = send(pair_grad, across)
    cross_grad, matrices, places = after((cross_grad, matrices, places), pair_grad, m)
    swapped = send(jnp.where(end, helped_hidden, cross_grad[: handed + place_rows]), both_ways)
    m = m + product(rows_of(me ^ 1), pair_grad) + product(rows_of(cross), cross_grad)

    height, width = m.shape[0] // steps, m.shape[1] // steps
    full = jax.ShapeDtypeStruct(m.shape, jnp.float32)
    turned = jax.ShapeDtypeStruct((m.shape[0], tok), hidden.dtype)
    table = jax.ShapeDtypeStruct((place_rows, m.shape[1]), jnp.float32)
    folded = jax.ShapeDtypeStruct((height, width), jnp.float32)
    m, helped, own_turned, end_turned, end_places, own_bands = call(
        swapped_kernel,
        (full, full, turned, turned, table, folded),
        m,
        far_hidden,
        cross_hidden,
        cross_grad,
        swapped,
        places,
        *matrices,
    )
    far_grad = after(far_grad, m)
    code_shape = jax.ShapeDtypeStruct((m.shape[0] + code_rows, m.shape[1]), jnp.int16)
    code, end_bands = call(
        helped_kernel, (code_shape, folded), helped, end_turned, far_grad, end_places, *matrices
    )
    m, end_bands, code = lax.optimization_barrier((m, end_bands, code))
    end_bands = send(end_bands, both_ways)
    code = send(code, outward)
    flag = end.astype(jnp.int32).reshape(1)
    m, bands = call(
        last_rows_kernel, (full, folded), flag, m, own_bands, own_turned, far_grad, places, *matrices
    )
    end_bands, bands = lax.optimization_barrier((end_bands, bands))
    bands = bands + jnp.where(end, end_bands, 0.0)
    exponents = code[m.shape[0] :]

    def behind_code(x):
        nonlocal exponents
        x, exponents = lax.optimization_barrier((x, exponents))
        return x

    parts = spread_sum(bands, "rep", behind_code)
    return [m, code, exponents], parts, places, matrices


def local(hidden, out_grad, momentum, band_rows, band_start_columns):
    row_count = hidden.shape[1]
    col_count = out_grad.shape[1]
    one_hot = jnp.asarray(np.kron(np.eye(col_count // order), np.ones((1, order))), jnp.float32)
    matrices = (jnp.asarray(fold_matrix(col_count)), jnp.asarray(diagonal_blocks(row_count, col_count)))
    places = jnp.concatenate([band_rows, band_start_columns], axis=0).astype(jnp.float32)
    places = dot(places, one_hot)
    fits = out_grad.shape[0] % 384 == 0 and 2 * row_count == col_count and places.shape[0] <= place_rows
    form = lined if fits and lax.axis_size("tp") == 4 else gathered
    m_parts, band_parts, places, matrices = form(
        hidden, out_grad, decay_rate * momentum[0], places, matrices
    )
    shape = (row_count, col_count)
    momentum_out = call(
        remove_kernel, jax.ShapeDtypeStruct(shape, jnp.float32), *m_parts, places, matrices[1]
    )
    *band_parts, momentum_out = lax.optimization_barrier((*band_parts, momentum_out))
    update = call(update_kernel, jax.ShapeDtypeStruct(shape, jnp.bfloat16), *band_parts, places, *matrices)
    return (momentum_out[None], update)


def solution(mesh):
    return jax.shard_map(
        local,
        mesh=mesh,
        in_specs=(
            P("rep", "tp"),
            P(("rep", "tp"), None),
            P("rep", "tp", None),
            P("tp", None),
            P("tp", None),
        ),
        out_specs=(P("rep", "tp", None), P("tp", None)),
        check_vma=False,
    )
```

```python
import jax
import jax.numpy as jnp
import numpy as np
from jax import lax
from jax.experimental import pallas as pl
from jax.experimental.pallas import tpu as pltpu
from jax.sharding import PartitionSpec as P

decay_rate = 0.9
order = 64
band = 16
steps = order // band
place_rows = 16
code_rows = 16


def basis_matrix():
    frequency = np.arange(order, dtype=np.float64)[:, None]
    sample_pos = np.arange(order, dtype=np.float64)[None, :]
    norm_scale = np.where(frequency == 0, np.sqrt(1.0 / order), np.sqrt(2.0 / order))
    return norm_scale * np.cos(np.pi * (sample_pos + 0.5) * frequency / order)


def diagonal_blocks(*widths):
    count = next(c for c in (4, 2, 1) if all(width % (c * order) == 0 for width in widths))
    return np.kron(np.eye(count), basis_matrix()).astype(np.float32)


def fold_matrix(width):
    return np.kron(np.eye(width // order), np.kron(np.ones((steps, 1)), np.eye(band))).astype(jnp.bfloat16)


def split2(x):
    high = x.astype(jnp.bfloat16)
    return high, (x - high.astype(jnp.float32)).astype(jnp.bfloat16)


def split3(x):
    high, low = split2(x)
    rest = x - high.astype(jnp.float32) - low.astype(jnp.float32)
    return high, low, rest.astype(jnp.bfloat16)


def dot(a, b, dims=((1,), (0,))):
    return lax.dot_general(a, b, (dims, ((), ())), preferred_element_type=jnp.float32)


def dot3(a, b, dims=((1,), (0,))):
    (a_high, a_low), (b_high, b_low) = a, b
    left = jnp.concatenate([a_high, a_low, a_high], axis=dims[0][0])
    right = jnp.concatenate([b_high, b_high, b_low], axis=dims[1][0])
    return dot(left, right, dims)


def on_rows(basis_ref, x, transposed):
    basis, side = split2(basis_ref[...]), basis_ref.shape[0]
    dims = ((0,), (0,)) if transposed else ((1,), (0,))
    parts = [dot3(basis, split2(x[i : i + side]), dims) for i in range(0, x.shape[0], side)]
    return parts[0] if len(parts) == 1 else jnp.concatenate(parts, axis=0)


def on_columns(basis_ref, x, transposed):
    basis, side = split2(basis_ref[...]), basis_ref.shape[0]
    dims = ((1,), (0,)) if transposed else ((1,), (1,))
    parts = [dot3(split2(x[:, i : i + side]), basis, dims) for i in range(0, x.shape[1], side)]
    return parts[0] if len(parts) == 1 else jnp.concatenate(parts, axis=1)


def masks_of(places, count):
    width = places.shape[1]
    column = lax.rem(lax.broadcasted_iota(jnp.int32, (band, width), 1), order).astype(jnp.float32)
    masks = []
    for row in range(count):
        start = places[count + row : count + row + 1, :]
        masks.append((places[row : row + 1, :], (column >= start) & (column < start + band)))
    return masks


def rows_taken(x, masks):
    pieces = []
    for row, (at, _) in enumerate(masks):
        taken = jnp.zeros((band, x.shape[1]), jnp.float32)
        for step in range(steps):
            start = row * order + step * band
            taken = jnp.where(at == step * band, x[start : start + band], taken)
        pieces.append(taken)
    return jnp.concatenate(pieces, axis=0)


def selected(x, masks, basis_ref):
    taken = rows_taken(on_rows(basis_ref, x, False), masks)
    return within(on_columns(basis_ref, taken, False), masks)


def within(x, masks):
    return jnp.concatenate(
        [jnp.where(inside, x[i * band : (i + 1) * band], 0.0) for i, (_, inside) in enumerate(masks)], axis=0
    )


def restored(x, masks, basis_ref):
    by_columns = on_columns(basis_ref, x, True)
    pieces = []
    for row, (at, _) in enumerate(masks):
        part = by_columns[row * band : (row + 1) * band]
        pieces += [jnp.where(at == step * band, part, 0.0) for step in range(steps)]
    return on_rows(basis_ref, jnp.concatenate(pieces, axis=0), True)


def bands_of(x, places, fold_ref, basis_ref):
    return folded(selected(x, masks_of(places, x.shape[0] // order), basis_ref), fold_ref[...])


def folded(x, fold):
    return dot(jnp.concatenate(split3(x), axis=1), jnp.concatenate([fold] * 3, axis=0))


def spread(x, fold):
    return dot(jnp.concatenate(split3(x), axis=1), jnp.concatenate([fold] * 3, axis=1), ((1,), (1,)))


def bands_kernel(m_ref, places_ref, *refs):
    *matrix_refs, bands_ref = refs
    bands_ref[...] = bands_of(m_ref[...], places_ref[...], *matrix_refs)


def coded(x):
    top = jnp.max(jnp.abs(x), axis=0, keepdims=True)
    exponent = jnp.ceil(jnp.log2(jnp.maximum(top, 1e-30)) + 0.01)
    scaled = x * jnp.exp2(15.0 - exponent)
    values = jnp.clip(jnp.round(scaled), -32767.0, 32767.0).astype(jnp.int32).astype(jnp.int16)
    row = jnp.broadcast_to(exponent, (code_rows, x.shape[1])).astype(jnp.int32).astype(jnp.int16)
    return values, row


def decoded(ref):
    values = ref[: ref.shape[0] - code_rows].astype(jnp.int32).astype(jnp.float32)
    exponents = ref[ref.shape[0] - code_rows :].astype(jnp.int32).astype(jnp.float32)
    return values * jnp.exp2(exponents[:1] - 15.0)


def swapped_kernel(m_ref, far_hidden_ref, cross_hidden_ref, cross_ref, swapped_ref, places_ref, *refs):
    *matrix_refs, out_ref, helped_ref, own_turned_ref, end_turned_ref, end_places_ref, bands_ref = refs
    handed, side = swapped_ref.shape[0] - place_rows, out_ref.shape[0]
    alone = cross_ref.shape[0] - handed
    out_ref[...] = m_ref[...] + dot(cross_hidden_ref[...], swapped_ref[:handed], ((0,), (0,)))
    helped_ref[...] = dot(swapped_ref[:alone, :side], cross_ref[handed:], ((0,), (0,)))
    own_turned_ref[...] = far_hidden_ref[...].T
    end_turned_ref[:, : handed - alone] = swapped_ref[alone:handed, :side].T
    end_turned_ref[:, handed - alone :] = swapped_ref[:handed, side:].T
    end_places_ref[...] = swapped_ref[handed:].astype(jnp.float32)
    bands_ref[...] = bands_of(out_ref[...], places_ref[...], *matrix_refs)


def helped_kernel(helped_ref, turned_ref, far_ref, places_ref, *refs):
    *matrix_refs, out_ref, bands_ref = refs
    out_ref[...] = helped_ref[...] + dot(turned_ref[...], far_ref[...])
    bands_ref[...] = bands_of(out_ref[...], places_ref[...], *matrix_refs)


def last_rows_kernel(end_ref, helped_ref, m_ref, own_bands_ref, turned_ref, far_ref, places_ref, *refs):
    *matrix_refs, out_ref, bands_ref, code_ref = refs

    @pl.when(end_ref[0] == 1)
    def _():
        out_ref[...] = m_ref[...]
        bands_ref[...] = own_bands_ref[...]
        code_ref[...] = jnp.zeros_like(code_ref)

    @pl.when(end_ref[0] == 0)
    def _():
        side = m_ref.shape[0]
        code_ref[:side], code_ref[side:] = coded(helped_ref[...])
        out_ref[...] = m_ref[...] + dot(turned_ref[...], far_ref[...])
        bands_ref[...] = bands_of(out_ref[...], places_ref[...], *matrix_refs)


def remove_kernel(m_ref, *refs):
    *code_refs, places_ref, basis_ref, out_ref = refs
    m = m_ref[...]
    for ref in code_refs:
        m = m + decoded(ref)
    masks = masks_of(places_ref[...], m.shape[0] // order)
    out_ref[...] = m - restored(selected(m, masks, basis_ref), masks, basis_ref)


def update_kernel(*refs):
    *part_refs, places_ref, fold_ref, basis_ref, out_ref = refs
    bands = pair_sum([ref[...] for ref in part_refs])
    masks = masks_of(places_ref[...], out_ref.shape[0] // order)
    coefficients = within(spread(bands, fold_ref[...]), masks)
    out_ref[...] = restored(coefficients, masks, basis_ref).astype(out_ref.dtype)


def pair_sum(parts):
    while len(parts) > 1:
        parts = [sum(parts[i + 1 : i + 2], parts[i]) for i in range(0, len(parts), 2)]
    return parts[0]


def call(kernel, out_shapes, *operands):
    spaces = [pltpu.SMEM if x.dtype == jnp.int32 else pltpu.VMEM for x in operands]
    return pl.pallas_call(
        kernel,
        out_shape=out_shapes,
        in_specs=[pl.BlockSpec(memory_space=space) for space in spaces],
        compiler_params=pltpu.CompilerParams(vmem_limit_bytes=16 * 2**20),
        cost_estimate=pl.CostEstimate(flops=300000000, bytes_accessed=4000000, transcendentals=0),
    )(*operands)


def spread_sum(x, axis):
    size = lax.axis_size(axis)
    if size & (size - 1):
        return [lax.psum(x, axis)]
    stride, parts = 1, [x]
    while stride < size:
        count = min(4, size // stride)
        x = pair_sum(parts)
        parts = [x] + [
            lax.ppermute(x, axis, [(i, i ^ (stride * k)) for i in range(size)]) for k in range(1, count)
        ]
        stride *= count
    return parts


def product(hidden_rows, grad_rows):
    return dot(hidden_rows, grad_rows, ((0,), (0,)))


def after(x, *others):
    return lax.optimization_barrier((x, *others))[0]


def gathered(hidden, out_grad, carried, places, matrices):
    m = carried + product(hidden, lax.all_gather(out_grad, "tp", axis=0, tiled=True))
    folded = jax.ShapeDtypeStruct((m.shape[0] // steps, m.shape[1] // steps), jnp.float32)
    bands = call(bands_kernel, folded, m, places, *matrices)
    return [m], spread_sum(bands, "rep"), places, matrices


def lined(hidden, out_grad, carried, places, matrices):
    tok = out_grad.shape[0]
    me = lax.axis_index("tp")
    left = me < 2
    end = (me == 0) | (me == 3)
    cross = jnp.where(left, 2, 1)
    far = jnp.where(left, 3, 0)
    handed = tok * 2 // 3
    alone = tok - handed

    def rows_of(part, start=0, stop=tok):
        return lax.dynamic_slice_in_dim(hidden, part * tok + start, stop - start, 0)

    def send(x, perm):
        return lax.ppermute(x, "tp", perm)

    both_ways = [(0, 1), (1, 0), (2, 3), (3, 2)]
    across = [(1, 2), (2, 1)]
    outward = [(1, 0), (2, 3)]

    pair_grad = send(out_grad, both_ways)
    cross_grad = send(out_grad, across)
    m = carried + product(rows_of(me), out_grad)
    far_hidden = rows_of(far)
    helped_hidden = jnp.concatenate(
        [
            jnp.concatenate([rows_of(cross, handed), far_hidden[: handed - alone]], axis=0),
            far_hidden[handed - alone :],
        ],
        axis=1,
    )
    place_part = jnp.pad(places.astype(hidden.dtype), ((0, place_rows - places.shape[0]), (0, 0)))
    helped_hidden = jnp.concatenate([helped_hidden, place_part], axis=0)
    cross_hidden = jnp.where(end, rows_of(cross, 0, handed), 0)
    helped_hidden, cross_hidden, m = lax.optimization_barrier((helped_hidden, cross_hidden, m))

    far_grad = send(pair_grad, across)
    cross_grad, matrices, places = after((cross_grad, matrices, places), pair_grad, m)
    swapped = send(jnp.where(end, helped_hidden, cross_grad[: handed + place_rows]), both_ways)
    m = m + product(rows_of(me ^ 1), pair_grad) + product(rows_of(cross), cross_grad)

    height, width = m.shape[0] // steps, m.shape[1] // steps
    full = jax.ShapeDtypeStruct(m.shape, jnp.float32)
    turned = jax.ShapeDtypeStruct((m.shape[0], tok), hidden.dtype)
    table = jax.ShapeDtypeStruct((place_rows, m.shape[1]), jnp.float32)
    folded = jax.ShapeDtypeStruct((height, width), jnp.float32)
    m, helped, own_turned, end_turned, end_places, own_bands = call(
        swapped_kernel,
        (full, full, turned, turned, table, folded),
        m,
        far_hidden,
        cross_hidden,
        cross_grad,
        swapped,
        places,
        *matrices,
    )
    far_grad = after(far_grad, m)
    helped, end_bands = call(
        helped_kernel, (full, folded), helped, end_turned, far_grad, end_places, *matrices
    )
    m, end_bands = lax.optimization_barrier((m, end_bands))
    end_bands = send(end_bands, both_ways)
    code_shape = jax.ShapeDtypeStruct((m.shape[0] + code_rows, m.shape[1]), jnp.int16)
    flag = end.astype(jnp.int32).reshape(1)
    m, bands, code = call(
        last_rows_kernel,
        (full, folded, code_shape),
        flag,
        helped,
        m,
        own_bands,
        own_turned,
        far_grad,
        places,
        *matrices,
    )
    code = send(code, outward)
    end_bands, bands = lax.optimization_barrier((end_bands, bands))
    bands = bands + jnp.where(end, end_bands, 0.0)
    parts = spread_sum(bands, "rep")
    return [m, code], parts, places, matrices


def local(hidden, out_grad, momentum, band_rows, band_start_columns):
    row_count = hidden.shape[1]
    col_count = out_grad.shape[1]
    one_hot = jnp.asarray(np.kron(np.eye(col_count // order), np.ones((1, order))), jnp.float32)
    matrices = (jnp.asarray(fold_matrix(col_count)), jnp.asarray(diagonal_blocks(row_count, col_count)))
    places = jnp.concatenate([band_rows, band_start_columns], axis=0).astype(jnp.float32)
    places = dot(places, one_hot)
    fits = out_grad.shape[0] % 384 == 0 and 2 * row_count == col_count and places.shape[0] <= place_rows
    form = lined if fits and lax.axis_size("tp") == 4 else gathered
    m_parts, band_parts, places, matrices = form(
        hidden, out_grad, decay_rate * momentum[0], places, matrices
    )
    shape = (row_count, col_count)
    momentum_out = call(
        remove_kernel, jax.ShapeDtypeStruct(shape, jnp.float32), *m_parts, places, matrices[1]
    )
    *band_parts, momentum_out = lax.optimization_barrier((*band_parts, momentum_out))
    update = call(update_kernel, jax.ShapeDtypeStruct(shape, jnp.bfloat16), *band_parts, places, *matrices)
    return (momentum_out[None], update)


def solution(mesh):
    return jax.shard_map(
        local,
        mesh=mesh,
        in_specs=(
            P("rep", "tp"),
            P(("rep", "tp"), None),
            P("rep", "tp", None),
            P("tp", None),
            P("tp", None),
        ),
        out_specs=(P("rep", "tp", None), P("tp", None)),
        check_vma=False,
    )
```

```python
import jax
import jax.numpy as jnp
import numpy as np
from jax import lax
from jax.experimental import pallas as pl
from jax.experimental.pallas import tpu as pltpu
from jax.sharding import PartitionSpec as P

decay_rate = 0.9
order = 64
band = 16
steps = order // band
place_rows = 16
code_rows = 16


def basis_matrix():
    frequency = np.arange(order, dtype=np.float64)[:, None]
    sample_pos = np.arange(order, dtype=np.float64)[None, :]
    norm_scale = np.where(frequency == 0, np.sqrt(1.0 / order), np.sqrt(2.0 / order))
    return norm_scale * np.cos(np.pi * (sample_pos + 0.5) * frequency / order)


def diagonal_blocks(*widths):
    count = next(c for c in (4, 2, 1) if all(width % (c * order) == 0 for width in widths))
    return np.kron(np.eye(count), basis_matrix()).astype(np.float32)


def fold_matrix(width):
    return np.kron(np.eye(width // order), np.kron(np.ones((steps, 1)), np.eye(band))).astype(jnp.bfloat16)


def split2(x):
    high = x.astype(jnp.bfloat16)
    return high, (x - high.astype(jnp.float32)).astype(jnp.bfloat16)


def split3(x):
    high, low = split2(x)
    rest = x - high.astype(jnp.float32) - low.astype(jnp.float32)
    return high, low, rest.astype(jnp.bfloat16)


def dot(a, b, dims=((1,), (0,))):
    return lax.dot_general(a, b, (dims, ((), ())), preferred_element_type=jnp.float32)


def dot3(a, b, dims=((1,), (0,))):
    (a_high, a_low), (b_high, b_low) = a, b
    left = jnp.concatenate([a_high, a_low, a_high], axis=dims[0][0])
    right = jnp.concatenate([b_high, b_high, b_low], axis=dims[1][0])
    return dot(left, right, dims)


def on_rows(basis_ref, x, transposed):
    basis, side = split2(basis_ref[...]), basis_ref.shape[0]
    dims = ((0,), (0,)) if transposed else ((1,), (0,))
    parts = [dot3(basis, split2(x[i : i + side]), dims) for i in range(0, x.shape[0], side)]
    return parts[0] if len(parts) == 1 else jnp.concatenate(parts, axis=0)


def on_columns(basis_ref, x, transposed):
    basis, side = split2(basis_ref[...]), basis_ref.shape[0]
    dims = ((1,), (0,)) if transposed else ((1,), (1,))
    parts = [dot3(split2(x[:, i : i + side]), basis, dims) for i in range(0, x.shape[1], side)]
    return parts[0] if len(parts) == 1 else jnp.concatenate(parts, axis=1)


def masks_of(places, count):
    width = places.shape[1]
    column = lax.rem(lax.broadcasted_iota(jnp.int32, (band, width), 1), order).astype(jnp.float32)
    masks = []
    for row in range(count):
        start = places[count + row : count + row + 1, :]
        masks.append((places[row : row + 1, :], (column >= start) & (column < start + band)))
    return masks


def rows_taken(x, masks):
    pieces = []
    for row, (at, _) in enumerate(masks):
        taken = jnp.zeros((band, x.shape[1]), jnp.float32)
        for step in range(steps):
            start = row * order + step * band
            taken = jnp.where(at == step * band, x[start : start + band], taken)
        pieces.append(taken)
    return jnp.concatenate(pieces, axis=0)


def selected(x, masks, basis_ref):
    taken = rows_taken(on_rows(basis_ref, x, False), masks)
    return within(on_columns(basis_ref, taken, False), masks)


def within(x, masks):
    return jnp.concatenate(
        [jnp.where(inside, x[i * band : (i + 1) * band], 0.0) for i, (_, inside) in enumerate(masks)], axis=0
    )


def restored(x, masks, basis_ref):
    by_columns = on_columns(basis_ref, x, True)
    pieces = []
    for row, (at, _) in enumerate(masks):
        part = by_columns[row * band : (row + 1) * band]
        pieces += [jnp.where(at == step * band, part, 0.0) for step in range(steps)]
    return on_rows(basis_ref, jnp.concatenate(pieces, axis=0), True)


def bands_of(x, places, fold_ref, basis_ref):
    return folded(selected(x, masks_of(places, x.shape[0] // order), basis_ref), fold_ref[...])


def folded(x, fold):
    return dot(jnp.concatenate(split3(x), axis=1), jnp.concatenate([fold] * 3, axis=0))


def spread(x, fold):
    return dot(jnp.concatenate(split3(x), axis=1), jnp.concatenate([fold] * 3, axis=1), ((1,), (1,)))


def bands_kernel(m_ref, places_ref, *refs):
    *matrix_refs, bands_ref = refs
    bands_ref[...] = bands_of(m_ref[...], places_ref[...], *matrix_refs)


def coded(x):
    top = jnp.max(jnp.abs(x), axis=0, keepdims=True)
    exponent = jnp.ceil(jnp.log2(jnp.maximum(top, 1e-30)) + 0.01)
    scaled = x * jnp.exp2(15.0 - exponent)
    values = jnp.clip(jnp.round(scaled), -32767.0, 32767.0).astype(jnp.int32).astype(jnp.int16)
    row = jnp.broadcast_to(exponent, (code_rows, x.shape[1])).astype(jnp.int32).astype(jnp.int16)
    return values, row


def decoded(ref):
    values = ref[: ref.shape[0] - code_rows].astype(jnp.int32).astype(jnp.float32)
    exponents = ref[ref.shape[0] - code_rows :].astype(jnp.int32).astype(jnp.float32)
    return values * jnp.exp2(exponents[:1] - 15.0)


def swapped_kernel(m_ref, far_hidden_ref, cross_hidden_ref, cross_ref, swapped_ref, places_ref, *refs):
    *matrix_refs, out_ref, helped_ref, own_turned_ref, end_turned_ref, end_places_ref, bands_ref = refs
    handed, side = swapped_ref.shape[0] - place_rows, out_ref.shape[0]
    alone = cross_ref.shape[0] - handed
    out_ref[...] = m_ref[...] + dot(cross_hidden_ref[...], swapped_ref[:handed], ((0,), (0,)))
    helped_ref[...] = dot(swapped_ref[:alone, :side], cross_ref[handed:], ((0,), (0,)))
    own_turned_ref[...] = far_hidden_ref[...].T
    end_turned_ref[:, : handed - alone] = swapped_ref[alone:handed, :side].T
    end_turned_ref[:, handed - alone :] = swapped_ref[:handed, side:].T
    end_places_ref[...] = swapped_ref[handed:].astype(jnp.float32)
    bands_ref[...] = bands_of(out_ref[...], places_ref[...], *matrix_refs)


def helped_kernel(helped_ref, turned_ref, far_ref, places_ref, *refs):
    *matrix_refs, code_ref, bands_ref = refs
    product = helped_ref[...] + dot(turned_ref[...], far_ref[...])
    bands_ref[...] = bands_of(product, places_ref[...], *matrix_refs)
    side = product.shape[0]
    code_ref[:side], code_ref[side:] = coded(product)


def last_rows_kernel(end_ref, m_ref, own_bands_ref, turned_ref, far_ref, places_ref, *refs):
    *matrix_refs, out_ref, bands_ref = refs

    @pl.when(end_ref[0] == 1)
    def _():
        out_ref[...] = m_ref[...]
        bands_ref[...] = own_bands_ref[...]

    @pl.when(end_ref[0] == 0)
    def _():
        out_ref[...] = m_ref[...] + dot(turned_ref[...], far_ref[...])
        bands_ref[...] = bands_of(out_ref[...], places_ref[...], *matrix_refs)


def remove_kernel(m_ref, *refs):
    *code_refs, places_ref, basis_ref, out_ref = refs
    m = m_ref[...]
    for ref in code_refs:
        m = m + decoded(ref)
    masks = masks_of(places_ref[...], m.shape[0] // order)
    out_ref[...] = m - restored(selected(m, masks, basis_ref), masks, basis_ref)


def update_kernel(*refs):
    *part_refs, places_ref, fold_ref, basis_ref, out_ref = refs
    bands = pair_sum([ref[...] for ref in part_refs])
    masks = masks_of(places_ref[...], out_ref.shape[0] // order)
    coefficients = within(spread(bands, fold_ref[...]), masks)
    out_ref[...] = restored(coefficients, masks, basis_ref).astype(out_ref.dtype)


def pair_sum(parts):
    while len(parts) > 1:
        parts = [sum(parts[i + 1 : i + 2], parts[i]) for i in range(0, len(parts), 2)]
    return parts[0]


def call(kernel, out_shapes, *operands):
    spaces = [pltpu.SMEM if x.dtype == jnp.int32 else pltpu.VMEM for x in operands]
    return pl.pallas_call(
        kernel,
        out_shape=out_shapes,
        in_specs=[pl.BlockSpec(memory_space=space) for space in spaces],
        compiler_params=pltpu.CompilerParams(vmem_limit_bytes=16 * 2**20),
        cost_estimate=pl.CostEstimate(flops=22 * 10**7, bytes_accessed=3 * 10**6, transcendentals=0),
    )(*operands)


def spread_sum(x, axis):
    size = lax.axis_size(axis)
    if size & (size - 1):
        return [lax.psum(x, axis)]
    stride, parts = 1, [x]
    while stride < size:
        count = min(4, size // stride)
        x = pair_sum(parts)
        parts = [x] + [
            lax.ppermute(x, axis, [(i, i ^ (stride * k)) for i in range(size)]) for k in range(1, count)
        ]
        stride *= count
    return parts


def product(hidden_rows, grad_rows):
    return dot(hidden_rows, grad_rows, ((0,), (0,)))


def after(x, *others):
    return lax.optimization_barrier((x, *others))[0]


def gathered(hidden, out_grad, carried, places, matrices):
    m = carried + product(hidden, lax.all_gather(out_grad, "tp", axis=0, tiled=True))
    folded = jax.ShapeDtypeStruct((m.shape[0] // steps, m.shape[1] // steps), jnp.float32)
    bands = call(bands_kernel, folded, m, places, *matrices)
    return [m], spread_sum(bands, "rep"), places, matrices


def lined(hidden, out_grad, carried, places, matrices):
    tok = out_grad.shape[0]
    me = lax.axis_index("tp")
    left = me < 2
    end = (me == 0) | (me == 3)
    cross = jnp.where(left, 2, 1)
    far = jnp.where(left, 3, 0)
    handed = tok * 2 // 3
    alone = tok - handed

    def rows_of(part, start=0, stop=tok):
        return lax.dynamic_slice_in_dim(hidden, part * tok + start, stop - start, 0)

    def send(x, perm):
        return lax.ppermute(x, "tp", perm)

    both_ways = [(0, 1), (1, 0), (2, 3), (3, 2)]
    across = [(1, 2), (2, 1)]
    outward = [(1, 0), (2, 3)]

    pair_grad = send(out_grad, both_ways)
    cross_grad = send(out_grad, across)
    m = carried + product(rows_of(me), out_grad)
    far_hidden = rows_of(far)
    helped_hidden = jnp.concatenate(
        [
            jnp.concatenate([rows_of(cross, handed), far_hidden[: handed - alone]], axis=0),
            far_hidden[handed - alone :],
        ],
        axis=1,
    )
    place_part = jnp.pad(places.astype(hidden.dtype), ((0, place_rows - places.shape[0]), (0, 0)))
    helped_hidden = jnp.concatenate([helped_hidden, place_part], axis=0)
    cross_hidden = jnp.where(end, rows_of(cross, 0, handed), 0)
    helped_hidden, cross_hidden, m = lax.optimization_barrier((helped_hidden, cross_hidden, m))

    far_grad = send(pair_grad, across)
    cross_grad, matrices, places = after((cross_grad, matrices, places), pair_grad, m)
    swapped = send(jnp.where(end, helped_hidden, cross_grad[: handed + place_rows]), both_ways)
    m = m + product(rows_of(me ^ 1), pair_grad) + product(rows_of(cross), cross_grad)

    height, width = m.shape[0] // steps, m.shape[1] // steps
    full = jax.ShapeDtypeStruct(m.shape, jnp.float32)
    turned = jax.ShapeDtypeStruct((m.shape[0], tok), hidden.dtype)
    table = jax.ShapeDtypeStruct((place_rows, m.shape[1]), jnp.float32)
    folded = jax.ShapeDtypeStruct((height, width), jnp.float32)
    m, helped, own_turned, end_turned, end_places, own_bands = call(
        swapped_kernel,
        (full, full, turned, turned, table, folded),
        m,
        far_hidden,
        cross_hidden,
        cross_grad,
        swapped,
        places,
        *matrices,
    )
    far_grad = after(far_grad, m)
    code_shape = jax.ShapeDtypeStruct((m.shape[0] + code_rows, m.shape[1]), jnp.int16)
    code, end_bands = call(
        helped_kernel, (code_shape, folded), helped, end_turned, far_grad, end_places, *matrices
    )
    m, end_bands, code = lax.optimization_barrier((m, end_bands, code))
    end_bands = send(end_bands, both_ways)
    code = send(code, outward)
    flag = end.astype(jnp.int32).reshape(1)
    m, bands = call(
        last_rows_kernel, (full, folded), flag, m, own_bands, own_turned, far_grad, places, *matrices
    )
    end_bands, bands = lax.optimization_barrier((end_bands, bands))
    bands = bands + jnp.where(end, end_bands, 0.0)
    parts = spread_sum(bands, "rep")
    return [m, code], parts, places, matrices


def local(hidden, out_grad, momentum, band_rows, band_start_columns):
    row_count = hidden.shape[1]
    col_count = out_grad.shape[1]
    one_hot = jnp.asarray(np.kron(np.eye(col_count // order), np.ones((1, order))), jnp.float32)
    matrices = (jnp.asarray(fold_matrix(col_count)), jnp.asarray(diagonal_blocks(row_count, col_count)))
    places = jnp.concatenate([band_rows, band_start_columns], axis=0).astype(jnp.float32)
    places = dot(places, one_hot)
    fits = out_grad.shape[0] % 384 == 0 and 2 * row_count == col_count and places.shape[0] <= place_rows
    form = lined if fits and lax.axis_size("tp") == 4 else gathered
    m_parts, band_parts, places, matrices = form(
        hidden, out_grad, decay_rate * momentum[0], places, matrices
    )
    shape = (row_count, col_count)
    momentum_out = call(
        remove_kernel, jax.ShapeDtypeStruct(shape, jnp.float32), *m_parts, places, matrices[1]
    )
    *band_parts, momentum_out = lax.optimization_barrier((*band_parts, momentum_out))
    update = call(update_kernel, jax.ShapeDtypeStruct(shape, jnp.bfloat16), *band_parts, places, *matrices)
    return (momentum_out[None], update)


def solution(mesh):
    return jax.shard_map(
        local,
        mesh=mesh,
        in_specs=(
            P("rep", "tp"),
            P(("rep", "tp"), None),
            P("rep", "tp", None),
            P("tp", None),
            P("tp", None),
        ),
        out_specs=(P("rep", "tp", None), P("tp", None)),
        check_vma=False,
    )
```

```python
import jax
import jax.numpy as jnp
import numpy as np
from jax import lax
from jax.experimental import pallas as pl
from jax.experimental.pallas import tpu as pltpu
from jax.sharding import PartitionSpec as P

decay_rate = 0.9
order = 64
band = 16
steps = order // band
place_rows = 16
code_rows = 16


def basis_matrix():
    frequency = np.arange(order, dtype=np.float64)[:, None]
    sample_pos = np.arange(order, dtype=np.float64)[None, :]
    norm_scale = np.where(frequency == 0, np.sqrt(1.0 / order), np.sqrt(2.0 / order))
    return norm_scale * np.cos(np.pi * (sample_pos + 0.5) * frequency / order)


def diagonal_blocks(*widths):
    count = next(c for c in (4, 2, 1) if all(width % (c * order) == 0 for width in widths))
    return np.kron(np.eye(count), basis_matrix()).astype(np.float32)


def fold_matrix(width):
    return np.kron(np.eye(width // order), np.kron(np.ones((steps, 1)), np.eye(band))).astype(jnp.bfloat16)


def split2(x):
    high = x.astype(jnp.bfloat16)
    return high, (x - high.astype(jnp.float32)).astype(jnp.bfloat16)


def split3(x):
    high, low = split2(x)
    rest = x - high.astype(jnp.float32) - low.astype(jnp.float32)
    return high, low, rest.astype(jnp.bfloat16)


def dot(a, b, dims=((1,), (0,))):
    return lax.dot_general(a, b, (dims, ((), ())), preferred_element_type=jnp.float32)


def dot3(a, b, dims=((1,), (0,))):
    (a_high, a_low), (b_high, b_low) = a, b
    left = jnp.concatenate([a_high, a_low, a_high], axis=dims[0][0])
    right = jnp.concatenate([b_high, b_high, b_low], axis=dims[1][0])
    return dot(left, right, dims)


def on_rows(basis_ref, x, transposed):
    basis, side = split2(basis_ref[...]), basis_ref.shape[0]
    dims = ((0,), (0,)) if transposed else ((1,), (0,))
    parts = [dot3(basis, split2(x[i : i + side]), dims) for i in range(0, x.shape[0], side)]
    return parts[0] if len(parts) == 1 else jnp.concatenate(parts, axis=0)


def on_columns(basis_ref, x, transposed):
    basis, side = split2(basis_ref[...]), basis_ref.shape[0]
    dims = ((1,), (0,)) if transposed else ((1,), (1,))
    parts = [dot3(split2(x[:, i : i + side]), basis, dims) for i in range(0, x.shape[1], side)]
    return parts[0] if len(parts) == 1 else jnp.concatenate(parts, axis=1)


def masks_of(places, count):
    width = places.shape[1]
    column = lax.rem(lax.broadcasted_iota(jnp.int32, (band, width), 1), order).astype(jnp.float32)
    masks = []
    for row in range(count):
        start = places[count + row : count + row + 1, :]
        masks.append((places[row : row + 1, :], (column >= start) & (column < start + band)))
    return masks


def rows_taken(x, masks):
    pieces = []
    for row, (at, _) in enumerate(masks):
        taken = jnp.zeros((band, x.shape[1]), jnp.float32)
        for step in range(steps):
            start = row * order + step * band
            taken = jnp.where(at == step * band, x[start : start + band], taken)
        pieces.append(taken)
    return jnp.concatenate(pieces, axis=0)


def selected(x, masks, basis_ref):
    taken = rows_taken(on_rows(basis_ref, x, False), masks)
    return within(on_columns(basis_ref, taken, False), masks)


def within(x, masks):
    return jnp.concatenate(
        [jnp.where(inside, x[i * band : (i + 1) * band], 0.0) for i, (_, inside) in enumerate(masks)], axis=0
    )


def restored(x, masks, basis_ref):
    by_columns = on_columns(basis_ref, x, True)
    pieces = []
    for row, (at, _) in enumerate(masks):
        part = by_columns[row * band : (row + 1) * band]
        pieces += [jnp.where(at == step * band, part, 0.0) for step in range(steps)]
    return on_rows(basis_ref, jnp.concatenate(pieces, axis=0), True)


def bands_of(x, places, fold_ref, basis_ref):
    return folded(selected(x, masks_of(places, x.shape[0] // order), basis_ref), fold_ref[...])


def folded(x, fold):
    return dot(jnp.concatenate(split3(x), axis=1), jnp.concatenate([fold] * 3, axis=0))


def spread(x, fold):
    return dot(jnp.concatenate(split3(x), axis=1), jnp.concatenate([fold] * 3, axis=1), ((1,), (1,)))


def bands_kernel(m_ref, places_ref, *refs):
    *matrix_refs, bands_ref = refs
    bands_ref[...] = bands_of(m_ref[...], places_ref[...], *matrix_refs)


def coded(x):
    top = jnp.max(jnp.abs(x), axis=0, keepdims=True)
    exponent = jnp.ceil(jnp.log2(jnp.maximum(top, 1e-30)) + 0.01)
    scaled = x * jnp.exp2(15.0 - exponent)
    values = jnp.clip(jnp.round(scaled), -32767.0, 32767.0).astype(jnp.int32).astype(jnp.int16)
    row = jnp.broadcast_to(exponent, (code_rows, x.shape[1])).astype(jnp.int32).astype(jnp.int16)
    return values, row


def decoded(ref):
    values = ref[: ref.shape[0] - code_rows].astype(jnp.int32).astype(jnp.float32)
    exponents = ref[ref.shape[0] - code_rows :].astype(jnp.int32).astype(jnp.float32)
    return values * jnp.exp2(exponents[:1] - 15.0)


def swapped_kernel(m_ref, far_hidden_ref, cross_hidden_ref, cross_ref, swapped_ref, places_ref, *refs):
    *matrix_refs, out_ref, helped_ref, own_turned_ref, end_turned_ref, end_places_ref, bands_ref = refs
    handed, side = swapped_ref.shape[0] - place_rows, out_ref.shape[0]
    alone = cross_ref.shape[0] - handed
    out_ref[...] = m_ref[...] + dot(cross_hidden_ref[...], swapped_ref[:handed], ((0,), (0,)))
    helped_ref[...] = dot(swapped_ref[:alone, :side], cross_ref[handed:], ((0,), (0,)))
    own_turned_ref[...] = far_hidden_ref[...].T
    end_turned_ref[:, : handed - alone] = swapped_ref[alone:handed, :side].T
    end_turned_ref[:, handed - alone :] = swapped_ref[:handed, side:].T
    end_places_ref[...] = swapped_ref[handed:].astype(jnp.float32)
    bands_ref[...] = bands_of(out_ref[...], places_ref[...], *matrix_refs)


def helped_kernel(helped_ref, turned_ref, far_ref, places_ref, *refs):
    *matrix_refs, code_ref, bands_ref = refs
    product = helped_ref[...] + dot(turned_ref[...], far_ref[...])
    bands_ref[...] = bands_of(product, places_ref[...], *matrix_refs)
    side = product.shape[0]
    code_ref[:side], code_ref[side:] = coded(product)


def last_rows_kernel(end_ref, m_ref, own_bands_ref, turned_ref, far_ref, places_ref, *refs):
    *matrix_refs, out_ref, bands_ref = refs

    @pl.when(end_ref[0] == 1)
    def _():
        out_ref[...] = m_ref[...]
        bands_ref[...] = own_bands_ref[...]

    @pl.when(end_ref[0] == 0)
    def _():
        out_ref[...] = m_ref[...] + dot(turned_ref[...], far_ref[...])
        bands_ref[...] = bands_of(out_ref[...], places_ref[...], *matrix_refs)


def remove_kernel(m_ref, *refs):
    *code_refs, places_ref, basis_ref, out_ref = refs
    m = m_ref[...]
    for ref in code_refs:
        m = m + decoded(ref)
    masks = masks_of(places_ref[...], m.shape[0] // order)
    out_ref[...] = m - restored(selected(m, masks, basis_ref), masks, basis_ref)


def update_kernel(*refs):
    *part_refs, places_ref, fold_ref, basis_ref, out_ref = refs
    bands = pair_sum([ref[...] for ref in part_refs])
    masks = masks_of(places_ref[...], out_ref.shape[0] // order)
    coefficients = within(spread(bands, fold_ref[...]), masks)
    out_ref[...] = restored(coefficients, masks, basis_ref).astype(out_ref.dtype)


def pair_sum(parts):
    while len(parts) > 1:
        parts = [sum(parts[i + 1 : i + 2], parts[i]) for i in range(0, len(parts), 2)]
    return parts[0]


def call(kernel, out_shapes, *operands):
    spaces = [pltpu.SMEM if x.dtype == jnp.int32 else pltpu.VMEM for x in operands]
    return pl.pallas_call(
        kernel,
        out_shape=out_shapes,
        in_specs=[pl.BlockSpec(memory_space=space) for space in spaces],
        compiler_params=pltpu.CompilerParams(vmem_limit_bytes=8 * 2**20),
        cost_estimate=pl.CostEstimate(flops=3 * 10**8, bytes_accessed=4 * 10**6, transcendentals=0),
    )(*operands)


def spread_sum(x, axis):
    size = lax.axis_size(axis)
    if size & (size - 1):
        return [lax.psum(x, axis)]
    stride, parts = 1, [x]
    while stride < size:
        count = min(4, size // stride)
        x = pair_sum(parts)
        parts = [x] + [
            lax.ppermute(x, axis, [(i, i ^ (stride * k)) for i in range(size)]) for k in range(1, count)
        ]
        stride *= count
    return parts


def product(hidden_rows, grad_rows):
    return dot(hidden_rows, grad_rows, ((0,), (0,)))


def after(x, *others):
    return lax.optimization_barrier((x, *others))[0]


def gathered(hidden, out_grad, carried, places, matrices):
    m = carried + product(hidden, lax.all_gather(out_grad, "tp", axis=0, tiled=True))
    folded = jax.ShapeDtypeStruct((m.shape[0] // steps, m.shape[1] // steps), jnp.float32)
    bands = call(bands_kernel, folded, m, places, *matrices)
    return [m], spread_sum(bands, "rep"), places, matrices


def lined(hidden, out_grad, carried, places, matrices):
    tok = out_grad.shape[0]
    me = lax.axis_index("tp")
    left = me < 2
    end = (me == 0) | (me == 3)
    cross = jnp.where(left, 2, 1)
    far = jnp.where(left, 3, 0)
    handed = tok * 2 // 3
    alone = tok - handed

    def rows_of(part, start=0, stop=tok):
        return lax.dynamic_slice_in_dim(hidden, part * tok + start, stop - start, 0)

    def send(x, perm):
        return lax.ppermute(x, "tp", perm)

    both_ways = [(0, 1), (1, 0), (2, 3), (3, 2)]
    across = [(1, 2), (2, 1)]
    outward = [(1, 0), (2, 3)]

    pair_grad = send(out_grad, both_ways)
    cross_grad = send(out_grad, across)
    m = carried + product(rows_of(me), out_grad)
    far_hidden = rows_of(far)
    helped_hidden = jnp.concatenate(
        [
            jnp.concatenate([rows_of(cross, handed), far_hidden[: handed - alone]], axis=0),
            far_hidden[handed - alone :],
        ],
        axis=1,
    )
    place_part = jnp.pad(places.astype(hidden.dtype), ((0, place_rows - places.shape[0]), (0, 0)))
    helped_hidden = jnp.concatenate([helped_hidden, place_part], axis=0)
    cross_hidden = jnp.where(end, rows_of(cross, 0, handed), 0)
    helped_hidden, cross_hidden, m = lax.optimization_barrier((helped_hidden, cross_hidden, m))

    far_grad = send(pair_grad, across)
    cross_grad, matrices, places = after((cross_grad, matrices, places), pair_grad, m)
    swapped = send(jnp.where(end, helped_hidden, cross_grad[: handed + place_rows]), both_ways)
    m = m + product(rows_of(me ^ 1), pair_grad) + product(rows_of(cross), cross_grad)

    height, width = m.shape[0] // steps, m.shape[1] // steps
    full = jax.ShapeDtypeStruct(m.shape, jnp.float32)
    turned = jax.ShapeDtypeStruct((m.shape[0], tok), hidden.dtype)
    table = jax.ShapeDtypeStruct((place_rows, m.shape[1]), jnp.float32)
    folded = jax.ShapeDtypeStruct((height, width), jnp.float32)
    m, helped, own_turned, end_turned, end_places, own_bands = call(
        swapped_kernel,
        (full, full, turned, turned, table, folded),
        m,
        far_hidden,
        cross_hidden,
        cross_grad,
        swapped,
        places,
        *matrices,
    )
    far_grad = after(far_grad, m)
    code_shape = jax.ShapeDtypeStruct((m.shape[0] + code_rows, m.shape[1]), jnp.int16)
    code, end_bands = call(
        helped_kernel, (code_shape, folded), helped, end_turned, far_grad, end_places, *matrices
    )
    m, end_bands, code = lax.optimization_barrier((m, end_bands, code))
    end_bands = send(end_bands, both_ways)
    flag = end.astype(jnp.int32).reshape(1)
    m, bands = call(
        last_rows_kernel, (full, folded), flag, m, own_bands, own_turned, far_grad, places, *matrices
    )
    bands, code = lax.optimization_barrier((bands, code))
    code = send(code, outward)
    end_bands, bands = lax.optimization_barrier((end_bands, bands))
    bands = bands + jnp.where(end, end_bands, 0.0)
    parts = spread_sum(bands, "rep")
    return [m, code], parts, places, matrices


def local(hidden, out_grad, momentum, band_rows, band_start_columns):
    row_count = hidden.shape[1]
    col_count = out_grad.shape[1]
    one_hot = jnp.asarray(np.kron(np.eye(col_count // order), np.ones((1, order))), jnp.float32)
    matrices = (jnp.asarray(fold_matrix(col_count)), jnp.asarray(diagonal_blocks(row_count, col_count)))
    places = jnp.concatenate([band_rows, band_start_columns], axis=0).astype(jnp.float32)
    places = dot(places, one_hot)
    fits = out_grad.shape[0] % 384 == 0 and 2 * row_count == col_count and places.shape[0] <= place_rows
    form = lined if fits and lax.axis_size("tp") == 4 else gathered
    m_parts, band_parts, places, matrices = form(
        hidden, out_grad, decay_rate * momentum[0], places, matrices
    )
    shape = (row_count, col_count)
    momentum_out = call(
        remove_kernel, jax.ShapeDtypeStruct(shape, jnp.float32), *m_parts, places, matrices[1]
    )
    *band_parts, momentum_out = lax.optimization_barrier((*band_parts, momentum_out))
    update = call(update_kernel, jax.ShapeDtypeStruct(shape, jnp.bfloat16), *band_parts, places, *matrices)
    return (momentum_out[None], update)


def solution(mesh):
    return jax.shard_map(
        local,
        mesh=mesh,
        in_specs=(
            P("rep", "tp"),
            P(("rep", "tp"), None),
            P("rep", "tp", None),
            P("tp", None),
            P("tp", None),
        ),
        out_specs=(P("rep", "tp", None), P("tp", None)),
        check_vma=False,
    )
```

```python
import jax
import jax.numpy as jnp
import numpy as np
from jax import lax
from jax.experimental import pallas as pl
from jax.experimental.pallas import tpu as pltpu
from jax.sharding import PartitionSpec as P

decay_rate = 0.9
order = 64
band = 16
steps = order // band
place_rows = 16
code_rows = 16


def basis_matrix():
    frequency = np.arange(order, dtype=np.float64)[:, None]
    sample_pos = np.arange(order, dtype=np.float64)[None, :]
    norm_scale = np.where(frequency == 0, np.sqrt(1.0 / order), np.sqrt(2.0 / order))
    return norm_scale * np.cos(np.pi * (sample_pos + 0.5) * frequency / order)


def diagonal_blocks(*widths):
    count = next(c for c in (4, 2, 1) if all(width % (c * order) == 0 for width in widths))
    return np.kron(np.eye(count), basis_matrix()).astype(np.float32)


def fold_matrix(width):
    return np.kron(np.eye(width // order), np.kron(np.ones((steps, 1)), np.eye(band))).astype(jnp.bfloat16)


def split2(x):
    high = x.astype(jnp.bfloat16)
    return high, (x - high.astype(jnp.float32)).astype(jnp.bfloat16)


def split3(x):
    high, low = split2(x)
    rest = x - high.astype(jnp.float32) - low.astype(jnp.float32)
    return high, low, rest.astype(jnp.bfloat16)


def dot(a, b, dims=((1,), (0,))):
    return lax.dot_general(a, b, (dims, ((), ())), preferred_element_type=jnp.float32)


def dot3(a, b, dims=((1,), (0,))):
    (a_high, a_low), (b_high, b_low) = a, b
    left = jnp.concatenate([a_high, a_low, a_high], axis=dims[0][0])
    right = jnp.concatenate([b_high, b_high, b_low], axis=dims[1][0])
    return dot(left, right, dims)


def on_rows(basis_ref, x, transposed):
    basis, side = split2(basis_ref[...]), basis_ref.shape[0]
    dims = ((0,), (0,)) if transposed else ((1,), (0,))
    parts = [dot3(basis, split2(x[i : i + side]), dims) for i in range(0, x.shape[0], side)]
    return parts[0] if len(parts) == 1 else jnp.concatenate(parts, axis=0)


def on_columns(basis_ref, x, transposed):
    basis, side = split2(basis_ref[...]), basis_ref.shape[0]
    dims = ((1,), (0,)) if transposed else ((1,), (1,))
    parts = [dot3(split2(x[:, i : i + side]), basis, dims) for i in range(0, x.shape[1], side)]
    return parts[0] if len(parts) == 1 else jnp.concatenate(parts, axis=1)


def masks_of(places, count):
    width = places.shape[1]
    column = lax.rem(lax.broadcasted_iota(jnp.int32, (band, width), 1), order).astype(jnp.float32)
    masks = []
    for row in range(count):
        start = places[count + row : count + row + 1, :]
        masks.append((places[row : row + 1, :], (column >= start) & (column < start + band)))
    return masks


def rows_taken(x, masks):
    pieces = []
    for row, (at, _) in enumerate(masks):
        taken = jnp.zeros((band, x.shape[1]), jnp.float32)
        for step in range(steps):
            start = row * order + step * band
            taken = jnp.where(at == step * band, x[start : start + band], taken)
        pieces.append(taken)
    return jnp.concatenate(pieces, axis=0)


def selected(x, masks, basis_ref):
    taken = rows_taken(on_rows(basis_ref, x, False), masks)
    return within(on_columns(basis_ref, taken, False), masks)


def within(x, masks):
    return jnp.concatenate(
        [jnp.where(inside, x[i * band : (i + 1) * band], 0.0) for i, (_, inside) in enumerate(masks)], axis=0
    )


def restored(x, masks, basis_ref):
    by_columns = on_columns(basis_ref, x, True)
    pieces = []
    for row, (at, _) in enumerate(masks):
        part = by_columns[row * band : (row + 1) * band]
        pieces += [jnp.where(at == step * band, part, 0.0) for step in range(steps)]
    return on_rows(basis_ref, jnp.concatenate(pieces, axis=0), True)


def bands_of(x, places, fold_ref, basis_ref):
    return folded(selected(x, masks_of(places, x.shape[0] // order), basis_ref), fold_ref[...])


def folded(x, fold):
    return dot(jnp.concatenate(split3(x), axis=1), jnp.concatenate([fold] * 3, axis=0))


def spread(x, fold):
    return dot(jnp.concatenate(split3(x), axis=1), jnp.concatenate([fold] * 3, axis=1), ((1,), (1,)))


def bands_kernel(m_ref, places_ref, *refs):
    *matrix_refs, bands_ref = refs
    bands_ref[...] = bands_of(m_ref[...], places_ref[...], *matrix_refs)


def coded(x):
    top = jnp.max(jnp.abs(x), axis=0, keepdims=True)
    exponent = jnp.ceil(jnp.log2(jnp.maximum(top, 1e-30)) + 0.01)
    scaled = x * jnp.exp2(15.0 - exponent)
    values = jnp.clip(jnp.round(scaled), -32767.0, 32767.0).astype(jnp.int32).astype(jnp.int16)
    row = jnp.broadcast_to(exponent, (code_rows, x.shape[1])).astype(jnp.int32).astype(jnp.int16)
    return values, row


def decoded(ref):
    values = ref[: ref.shape[0] - code_rows].astype(jnp.int32).astype(jnp.float32)
    exponents = ref[ref.shape[0] - code_rows :].astype(jnp.int32).astype(jnp.float32)
    return values * jnp.exp2(exponents[:1] - 15.0)


def swapped_kernel(m_ref, far_hidden_ref, cross_hidden_ref, cross_ref, swapped_ref, places_ref, *refs):
    *matrix_refs, out_ref, helped_ref, own_turned_ref, end_turned_ref, end_places_ref, bands_ref = refs
    handed, side = swapped_ref.shape[0] - place_rows, out_ref.shape[0]
    alone = cross_ref.shape[0] - handed
    out_ref[...] = m_ref[...] + dot(cross_hidden_ref[...], swapped_ref[:handed], ((0,), (0,)))
    helped_ref[...] = dot(swapped_ref[:alone, :side], cross_ref[handed:], ((0,), (0,)))
    own_turned_ref[...] = far_hidden_ref[...].T
    end_turned_ref[:, : handed - alone] = swapped_ref[alone:handed, :side].T
    end_turned_ref[:, handed - alone :] = swapped_ref[:handed, side:].T
    end_places_ref[...] = swapped_ref[handed:].astype(jnp.float32)
    bands_ref[...] = bands_of(out_ref[...], places_ref[...], *matrix_refs)


def helped_kernel(helped_ref, turned_ref, far_ref, places_ref, *refs):
    *matrix_refs, code_ref, bands_ref = refs
    product = helped_ref[...] + dot(turned_ref[...], far_ref[...])
    bands_ref[...] = bands_of(product, places_ref[...], *matrix_refs)
    side = product.shape[0]
    code_ref[:side], code_ref[side:] = coded(product)


def last_rows_kernel(end_ref, m_ref, own_bands_ref, turned_ref, far_ref, places_ref, *refs):
    *matrix_refs, out_ref, bands_ref = refs

    @pl.when(end_ref[0] == 1)
    def _():
        out_ref[...] = m_ref[...]
        bands_ref[...] = own_bands_ref[...]

    @pl.when(end_ref[0] == 0)
    def _():
        out_ref[...] = m_ref[...] + dot(turned_ref[...], far_ref[...])
        bands_ref[...] = bands_of(out_ref[...], places_ref[...], *matrix_refs)


def remove_kernel(m_ref, bands_ref, places_ref, fold_ref, basis_ref, out_ref):
    masks = masks_of(places_ref[...], out_ref.shape[0] // order)
    coefficients = within(spread(bands_ref[...], fold_ref[...]), masks)
    out_ref[...] = m_ref[...] - restored(coefficients, masks, basis_ref)


def add_kernel(x_ref, code_ref, out_ref):
    out_ref[...] = x_ref[...] + decoded(code_ref)


def update_kernel(*refs):
    *part_refs, places_ref, fold_ref, basis_ref, out_ref = refs
    bands = pair_sum([ref[...] for ref in part_refs])
    masks = masks_of(places_ref[...], out_ref.shape[0] // order)
    coefficients = within(spread(bands, fold_ref[...]), masks)
    out_ref[...] = restored(coefficients, masks, basis_ref).astype(out_ref.dtype)


def pair_sum(parts):
    while len(parts) > 1:
        parts = [sum(parts[i + 1 : i + 2], parts[i]) for i in range(0, len(parts), 2)]
    return parts[0]


def call(kernel, out_shapes, *operands):
    spaces = [pltpu.SMEM if x.dtype == jnp.int32 else pltpu.VMEM for x in operands]
    return pl.pallas_call(
        kernel,
        out_shape=out_shapes,
        in_specs=[pl.BlockSpec(memory_space=space) for space in spaces],
        compiler_params=pltpu.CompilerParams(vmem_limit_bytes=16 * 2**20),
        cost_estimate=pl.CostEstimate(flops=4 * 10**8, bytes_accessed=4 * 10**6, transcendentals=0),
    )(*operands)


def spread_sum(x, axis):
    size = lax.axis_size(axis)
    if size & (size - 1):
        return [lax.psum(x, axis)]
    stride, parts = 1, [x]
    while stride < size:
        count = min(4, size // stride)
        x = pair_sum(parts)
        parts = [x] + [
            lax.ppermute(x, axis, [(i, i ^ (stride * k)) for i in range(size)]) for k in range(1, count)
        ]
        stride *= count
    return parts


def product(hidden_rows, grad_rows):
    return dot(hidden_rows, grad_rows, ((0,), (0,)))


def after(x, *others):
    return lax.optimization_barrier((x, *others))[0]


def gathered(hidden, out_grad, carried, places, matrices):
    m = carried + product(hidden, lax.all_gather(out_grad, "tp", axis=0, tiled=True))
    folded = jax.ShapeDtypeStruct((m.shape[0] // steps, m.shape[1] // steps), jnp.float32)
    bands = call(bands_kernel, folded, m, places, *matrices)
    return m, bands, None, spread_sum(bands, "rep"), places, matrices


def lined(hidden, out_grad, carried, places, matrices):
    tok = out_grad.shape[0]
    me = lax.axis_index("tp")
    left = me < 2
    end = (me == 0) | (me == 3)
    cross = jnp.where(left, 2, 1)
    far = jnp.where(left, 3, 0)
    handed = tok * 2 // 3
    alone = tok - handed

    def rows_of(part, start=0, stop=tok):
        return lax.dynamic_slice_in_dim(hidden, part * tok + start, stop - start, 0)

    def send(x, perm):
        return lax.ppermute(x, "tp", perm)

    both_ways = [(0, 1), (1, 0), (2, 3), (3, 2)]
    across = [(1, 2), (2, 1)]
    outward = [(1, 0), (2, 3)]

    pair_grad = send(out_grad, both_ways)
    cross_grad = send(out_grad, across)
    m = carried + product(rows_of(me), out_grad)
    far_hidden = rows_of(far)
    helped_hidden = jnp.concatenate(
        [
            jnp.concatenate([rows_of(cross, handed), far_hidden[: handed - alone]], axis=0),
            far_hidden[handed - alone :],
        ],
        axis=1,
    )
    place_part = jnp.pad(places.astype(hidden.dtype), ((0, place_rows - places.shape[0]), (0, 0)))
    helped_hidden = jnp.concatenate([helped_hidden, place_part], axis=0)
    cross_hidden = jnp.where(end, rows_of(cross, 0, handed), 0)
    helped_hidden, cross_hidden, m = lax.optimization_barrier((helped_hidden, cross_hidden, m))

    far_grad = send(pair_grad, across)
    cross_grad, matrices, places = after((cross_grad, matrices, places), pair_grad, m)
    swapped = send(jnp.where(end, helped_hidden, cross_grad[: handed + place_rows]), both_ways)
    m = m + product(rows_of(me ^ 1), pair_grad) + product(rows_of(cross), cross_grad)

    height, width = m.shape[0] // steps, m.shape[1] // steps
    full = jax.ShapeDtypeStruct(m.shape, jnp.float32)
    turned = jax.ShapeDtypeStruct((m.shape[0], tok), hidden.dtype)
    table = jax.ShapeDtypeStruct((place_rows, m.shape[1]), jnp.float32)
    folded = jax.ShapeDtypeStruct((height, width), jnp.float32)
    m, helped, own_turned, end_turned, end_places, own_bands = call(
        swapped_kernel,
        (full, full, turned, turned, table, folded),
        m,
        far_hidden,
        cross_hidden,
        cross_grad,
        swapped,
        places,
        *matrices,
    )
    far_grad = after(far_grad, m)
    code_shape = jax.ShapeDtypeStruct((m.shape[0] + code_rows, m.shape[1]), jnp.int16)
    code, end_bands = call(
        helped_kernel, (code_shape, folded), helped, end_turned, far_grad, end_places, *matrices
    )
    m, end_bands, code = lax.optimization_barrier((m, end_bands, code))
    end_bands = send(end_bands, both_ways)
    flag = end.astype(jnp.int32).reshape(1)
    m, bands = call(
        last_rows_kernel, (full, folded), flag, m, own_bands, own_turned, far_grad, places, *matrices
    )
    bands, code = lax.optimization_barrier((bands, code))
    code = send(code, outward)
    end_bands, bands = lax.optimization_barrier((end_bands, bands))
    bands = bands + jnp.where(end, end_bands, 0.0)
    parts = spread_sum(bands, "rep")
    return m, bands, code, parts, places, matrices


def local(hidden, out_grad, momentum, band_rows, band_start_columns):
    row_count = hidden.shape[1]
    col_count = out_grad.shape[1]
    one_hot = jnp.asarray(np.kron(np.eye(col_count // order), np.ones((1, order))), jnp.float32)
    matrices = (jnp.asarray(fold_matrix(col_count)), jnp.asarray(diagonal_blocks(row_count, col_count)))
    places = jnp.concatenate([band_rows, band_start_columns], axis=0).astype(jnp.float32)
    places = dot(places, one_hot)
    fits = out_grad.shape[0] % 384 == 0 and 2 * row_count == col_count and places.shape[0] <= place_rows
    form = lined if fits and lax.axis_size("tp") == 4 else gathered
    m, bands, code, band_parts, places, matrices = form(
        hidden, out_grad, decay_rate * momentum[0], places, matrices
    )
    full = jax.ShapeDtypeStruct(m.shape, jnp.float32)
    momentum_out = call(remove_kernel, full, m, bands, places, *matrices)
    if code is not None:
        momentum_out = call(add_kernel, full, momentum_out, code)
    *band_parts, momentum_out = lax.optimization_barrier((*band_parts, momentum_out))
    update = call(update_kernel, jax.ShapeDtypeStruct(m.shape, jnp.bfloat16), *band_parts, places, *matrices)
    return (momentum_out[None], update)


def solution(mesh):
    return jax.shard_map(
        local,
        mesh=mesh,
        in_specs=(
            P("rep", "tp"),
            P(("rep", "tp"), None),
            P("rep", "tp", None),
            P("tp", None),
            P("tp", None),
        ),
        out_specs=(P("rep", "tp", None), P("tp", None)),
        check_vma=False,
    )
```

```python
import jax
import jax.numpy as jnp
import numpy as np
from jax import lax
from jax.experimental import pallas as pl
from jax.experimental.pallas import tpu as pltpu
from jax.sharding import PartitionSpec as P

decay_rate = 0.9
order = 64
band = 16
steps = order // band
place_rows = 16
code_rows = 16


def basis_matrix():
    frequency = np.arange(order, dtype=np.float64)[:, None]
    sample_pos = np.arange(order, dtype=np.float64)[None, :]
    norm_scale = np.where(frequency == 0, np.sqrt(1.0 / order), np.sqrt(2.0 / order))
    return norm_scale * np.cos(np.pi * (sample_pos + 0.5) * frequency / order)


def diagonal_blocks(*widths):
    count = next(c for c in (4, 2, 1) if all(width % (c * order) == 0 for width in widths))
    return np.kron(np.eye(count), basis_matrix()).astype(np.float32)


def fold_matrix(width):
    return np.kron(np.eye(width // order), np.kron(np.ones((steps, 1)), np.eye(band))).astype(jnp.bfloat16)


def split2(x):
    high = x.astype(jnp.bfloat16)
    return high, (x - high.astype(jnp.float32)).astype(jnp.bfloat16)


def split3(x):
    high, low = split2(x)
    rest = x - high.astype(jnp.float32) - low.astype(jnp.float32)
    return high, low, rest.astype(jnp.bfloat16)


def dot(a, b, dims=((1,), (0,))):
    return lax.dot_general(a, b, (dims, ((), ())), preferred_element_type=jnp.float32)


def dot3(a, b, dims=((1,), (0,))):
    (a_high, a_low), (b_high, b_low) = a, b
    left = jnp.concatenate([a_high, a_low, a_high], axis=dims[0][0])
    right = jnp.concatenate([b_high, b_high, b_low], axis=dims[1][0])
    return dot(left, right, dims)


def on_rows(basis_ref, x, transposed):
    basis, side = split2(basis_ref[...]), basis_ref.shape[0]
    dims = ((0,), (0,)) if transposed else ((1,), (0,))
    parts = [dot3(basis, split2(x[i : i + side]), dims) for i in range(0, x.shape[0], side)]
    return parts[0] if len(parts) == 1 else jnp.concatenate(parts, axis=0)


def on_columns(basis_ref, x, transposed):
    basis, side = split2(basis_ref[...]), basis_ref.shape[0]
    dims = ((1,), (0,)) if transposed else ((1,), (1,))
    parts = [dot3(split2(x[:, i : i + side]), basis, dims) for i in range(0, x.shape[1], side)]
    return parts[0] if len(parts) == 1 else jnp.concatenate(parts, axis=1)


def masks_of(places, count):
    width = places.shape[1]
    column = lax.rem(lax.broadcasted_iota(jnp.int32, (band, width), 1), order).astype(jnp.float32)
    masks = []
    for row in range(count):
        start = places[count + row : count + row + 1, :]
        masks.append((places[row : row + 1, :], (column >= start) & (column < start + band)))
    return masks


def rows_taken(x, masks):
    pieces = []
    for row, (at, _) in enumerate(masks):
        taken = jnp.zeros((band, x.shape[1]), jnp.float32)
        for step in range(steps):
            start = row * order + step * band
            taken = jnp.where(at == step * band, x[start : start + band], taken)
        pieces.append(taken)
    return jnp.concatenate(pieces, axis=0)


def selected(x, masks, basis_ref):
    taken = rows_taken(on_rows(basis_ref, x, False), masks)
    return within(on_columns(basis_ref, taken, False), masks)


def within(x, masks):
    return jnp.concatenate(
        [jnp.where(inside, x[i * band : (i + 1) * band], 0.0) for i, (_, inside) in enumerate(masks)], axis=0
    )


def restored(x, masks, basis_ref):
    by_columns = on_columns(basis_ref, x, True)
    pieces = []
    for row, (at, _) in enumerate(masks):
        part = by_columns[row * band : (row + 1) * band]
        pieces += [jnp.where(at == step * band, part, 0.0) for step in range(steps)]
    return on_rows(basis_ref, jnp.concatenate(pieces, axis=0), True)


def bands_of(x, places, fold_ref, basis_ref):
    return folded(selected(x, masks_of(places, x.shape[0] // order), basis_ref), fold_ref[...])


def folded(x, fold):
    return dot(jnp.concatenate(split3(x), axis=1), jnp.concatenate([fold] * 3, axis=0))


def spread(x, fold):
    return dot(jnp.concatenate(split3(x), axis=1), jnp.concatenate([fold] * 3, axis=1), ((1,), (1,)))


def bands_kernel(m_ref, places_ref, *refs):
    *matrix_refs, bands_ref = refs
    bands_ref[...] = bands_of(m_ref[...], places_ref[...], *matrix_refs)


def coded(x):
    top = jnp.max(jnp.abs(x), axis=0, keepdims=True)
    exponent = jnp.ceil(jnp.log2(jnp.maximum(top, 1e-30)) + 0.01)
    scaled = x * jnp.exp2(15.0 - exponent)
    values = jnp.clip(jnp.round(scaled), -32767.0, 32767.0).astype(jnp.int32).astype(jnp.int16)
    row = jnp.broadcast_to(exponent, (code_rows, x.shape[1])).astype(jnp.int32).astype(jnp.int16)
    return values, row


def decoded(ref):
    values = ref[: ref.shape[0] - code_rows].astype(jnp.int32).astype(jnp.float32)
    exponents = ref[ref.shape[0] - code_rows :].astype(jnp.int32).astype(jnp.float32)
    return values * jnp.exp2(exponents[:1] - 15.0)


def swapped_kernel(m_ref, far_hidden_ref, cross_hidden_ref, cross_ref, swapped_ref, places_ref, *refs):
    *matrix_refs, out_ref, helped_ref, own_turned_ref, end_turned_ref, end_places_ref, bands_ref = refs
    handed, side = swapped_ref.shape[0] - place_rows, out_ref.shape[0]
    alone = cross_ref.shape[0] - handed
    out_ref[...] = m_ref[...] + dot(cross_hidden_ref[...], swapped_ref[:handed], ((0,), (0,)))
    helped_ref[...] = dot(swapped_ref[:alone, :side], cross_ref[handed:], ((0,), (0,)))
    own_turned_ref[...] = far_hidden_ref[...].T
    end_turned_ref[:, : handed - alone] = swapped_ref[alone:handed, :side].T
    end_turned_ref[:, handed - alone :] = swapped_ref[:handed, side:].T
    end_places_ref[...] = swapped_ref[handed:].astype(jnp.float32)
    bands_ref[...] = bands_of(out_ref[...], places_ref[...], *matrix_refs)


def helped_kernel(helped_ref, turned_ref, far_ref, places_ref, *refs):
    *matrix_refs, code_ref, bands_ref = refs
    product = helped_ref[...] + dot(turned_ref[...], far_ref[...])
    bands_ref[...] = bands_of(product, places_ref[...], *matrix_refs)
    side = product.shape[0]
    code_ref[:side], code_ref[side:] = coded(product)


def last_rows_kernel(end_ref, m_ref, own_bands_ref, turned_ref, far_ref, places_ref, *refs):
    *matrix_refs, out_ref, bands_ref = refs

    @pl.when(end_ref[0] == 1)
    def _():
        out_ref[...] = m_ref[...]
        bands_ref[...] = own_bands_ref[...]

    @pl.when(end_ref[0] == 0)
    def _():
        out_ref[...] = m_ref[...] + dot(turned_ref[...], far_ref[...])
        bands_ref[...] = bands_of(out_ref[...], places_ref[...], *matrix_refs)


def remove_kernel(m_ref, bands_ref, places_ref, fold_ref, basis_ref, out_ref):
    masks = masks_of(places_ref[...], out_ref.shape[0] // order)
    coefficients = within(spread(bands_ref[...], fold_ref[...]), masks)
    out_ref[...] = m_ref[...] - restored(coefficients, masks, basis_ref)


def add_kernel(x_ref, code_ref, out_ref):
    out_ref[...] = x_ref[...] + decoded(code_ref)


def update_kernel(*refs):
    *part_refs, places_ref, fold_ref, basis_ref, out_ref = refs
    bands = pair_sum([ref[...] for ref in part_refs])
    masks = masks_of(places_ref[...], out_ref.shape[0] // order)
    coefficients = within(spread(bands, fold_ref[...]), masks)
    out_ref[...] = restored(coefficients, masks, basis_ref).astype(out_ref.dtype)


def pair_sum(parts):
    while len(parts) > 1:
        parts = [sum(parts[i + 1 : i + 2], parts[i]) for i in range(0, len(parts), 2)]
    return parts[0]


def call(kernel, out_shapes, *operands):
    spaces = [pltpu.SMEM if x.dtype == jnp.int32 else pltpu.VMEM for x in operands]
    return pl.pallas_call(
        kernel,
        out_shape=out_shapes,
        in_specs=[pl.BlockSpec(memory_space=space) for space in spaces],
        compiler_params=pltpu.CompilerParams(vmem_limit_bytes=16 * 2**20),
        cost_estimate=pl.CostEstimate(flops=4 * 10**8, bytes_accessed=4 * 10**6, transcendentals=0),
    )(*operands)


def spread_sum(x, axis):
    size = lax.axis_size(axis)
    if size & (size - 1):
        return [lax.psum(x, axis)]
    stride, parts = 1, [x]
    while stride < size:
        count = min(4 if stride > 1 else 2, size // stride)
        x = pair_sum(parts)
        parts = [x] + [
            lax.ppermute(x, axis, [(i, i ^ (stride * k)) for i in range(size)]) for k in range(1, count)
        ]
        stride *= count
    return parts


def product(hidden_rows, grad_rows):
    return dot(hidden_rows, grad_rows, ((0,), (0,)))


def after(x, *others):
    return lax.optimization_barrier((x, *others))[0]


def gathered(hidden, out_grad, carried, places, matrices):
    m = carried + product(hidden, lax.all_gather(out_grad, "tp", axis=0, tiled=True))
    folded = jax.ShapeDtypeStruct((m.shape[0] // steps, m.shape[1] // steps), jnp.float32)
    bands = call(bands_kernel, folded, m, places, *matrices)
    return m, bands, None, spread_sum(bands, "rep"), places, matrices


def lined(hidden, out_grad, carried, places, matrices):
    tok = out_grad.shape[0]
    me = lax.axis_index("tp")
    left = me < 2
    end = (me == 0) | (me == 3)
    cross = jnp.where(left, 2, 1)
    far = jnp.where(left, 3, 0)
    handed = tok * 2 // 3
    alone = tok - handed

    def rows_of(part, start=0, stop=tok):
        return lax.dynamic_slice_in_dim(hidden, part * tok + start, stop - start, 0)

    def send(x, perm):
        return lax.ppermute(x, "tp", perm)

    both_ways = [(0, 1), (1, 0), (2, 3), (3, 2)]
    across = [(1, 2), (2, 1)]
    outward = [(1, 0), (2, 3)]

    pair_grad = send(out_grad, both_ways)
    cross_grad = send(out_grad, across)
    m = carried + product(rows_of(me), out_grad)
    far_hidden = rows_of(far)
    helped_hidden = jnp.concatenate(
        [
            jnp.concatenate([rows_of(cross, handed), far_hidden[: handed - alone]], axis=0),
            far_hidden[handed - alone :],
        ],
        axis=1,
    )
    place_part = jnp.pad(places.astype(hidden.dtype), ((0, place_rows - places.shape[0]), (0, 0)))
    helped_hidden = jnp.concatenate([helped_hidden, place_part], axis=0)
    cross_hidden = jnp.where(end, rows_of(cross, 0, handed), 0)
    helped_hidden, cross_hidden, m = lax.optimization_barrier((helped_hidden, cross_hidden, m))

    far_grad = send(pair_grad, across)
    cross_grad, matrices, places = after((cross_grad, matrices, places), pair_grad, m)
    swapped = send(jnp.where(end, helped_hidden, cross_grad[: handed + place_rows]), both_ways)
    m = m + product(rows_of(me ^ 1), pair_grad) + product(rows_of(cross), cross_grad)

    height, width = m.shape[0] // steps, m.shape[1] // steps
    full = jax.ShapeDtypeStruct(m.shape, jnp.float32)
    turned = jax.ShapeDtypeStruct((m.shape[0], tok), hidden.dtype)
    table = jax.ShapeDtypeStruct((place_rows, m.shape[1]), jnp.float32)
    folded = jax.ShapeDtypeStruct((height, width), jnp.float32)
    m, helped, own_turned, end_turned, end_places, own_bands = call(
        swapped_kernel,
        (full, full, turned, turned, table, folded),
        m,
        far_hidden,
        cross_hidden,
        cross_grad,
        swapped,
        places,
        *matrices,
    )
    far_grad = after(far_grad, m)
    code_shape = jax.ShapeDtypeStruct((m.shape[0] + code_rows, m.shape[1]), jnp.int16)
    code, end_bands = call(
        helped_kernel, (code_shape, folded), helped, end_turned, far_grad, end_places, *matrices
    )
    m, end_bands, code = lax.optimization_barrier((m, end_bands, code))
    end_bands = send(end_bands, both_ways)
    flag = end.astype(jnp.int32).reshape(1)
    m, bands = call(
        last_rows_kernel, (full, folded), flag, m, own_bands, own_turned, far_grad, places, *matrices
    )
    bands, code = lax.optimization_barrier((bands, code))
    code = send(code, outward)
    end_bands, bands = lax.optimization_barrier((end_bands, bands))
    bands = bands + jnp.where(end, end_bands, 0.0)
    parts = spread_sum(bands, "rep")
    return m, bands, code, parts, places, matrices


def local(hidden, out_grad, momentum, band_rows, band_start_columns):
    row_count = hidden.shape[1]
    col_count = out_grad.shape[1]
    one_hot = jnp.asarray(np.kron(np.eye(col_count // order), np.ones((1, order))), jnp.float32)
    matrices = (jnp.asarray(fold_matrix(col_count)), jnp.asarray(diagonal_blocks(row_count, col_count)))
    places = jnp.concatenate([band_rows, band_start_columns], axis=0).astype(jnp.float32)
    places = dot(places, one_hot)
    fits = out_grad.shape[0] % 384 == 0 and 2 * row_count == col_count and places.shape[0] <= place_rows
    form = lined if fits and lax.axis_size("tp") == 4 else gathered
    m, bands, code, band_parts, places, matrices = form(
        hidden, out_grad, decay_rate * momentum[0], places, matrices
    )
    full = jax.ShapeDtypeStruct(m.shape, jnp.float32)
    momentum_out = call(remove_kernel, full, m, bands, places, *matrices)
    if code is not None:
        momentum_out = call(add_kernel, full, momentum_out, code)
    *band_parts, momentum_out = lax.optimization_barrier((*band_parts, momentum_out))
    update = call(update_kernel, jax.ShapeDtypeStruct(m.shape, jnp.bfloat16), *band_parts, places, *matrices)
    return (momentum_out[None], update)


def solution(mesh):
    return jax.shard_map(
        local,
        mesh=mesh,
        in_specs=(
            P("rep", "tp"),
            P(("rep", "tp"), None),
            P("rep", "tp", None),
            P("tp", None),
            P("tp", None),
        ),
        out_specs=(P("rep", "tp", None), P("tp", None)),
        check_vma=False,
    )
```

```python
import jax
import jax.numpy as jnp
import numpy as np
from jax import lax
from jax.experimental import pallas as pl
from jax.experimental.pallas import tpu as pltpu
from jax.sharding import PartitionSpec as P

decay_rate = 0.9
order = 64
band = 16
steps = order // band
place_rows = 16
code_rows = 16


def basis_matrix():
    frequency = np.arange(order, dtype=np.float64)[:, None]
    sample_pos = np.arange(order, dtype=np.float64)[None, :]
    norm_scale = np.where(frequency == 0, np.sqrt(1.0 / order), np.sqrt(2.0 / order))
    return norm_scale * np.cos(np.pi * (sample_pos + 0.5) * frequency / order)


def diagonal_blocks(*widths):
    count = next(c for c in (4, 2, 1) if all(width % (c * order) == 0 for width in widths))
    return np.kron(np.eye(count), basis_matrix()).astype(np.float32)


def fold_matrix(width):
    return np.kron(np.eye(width // order), np.kron(np.ones((steps, 1)), np.eye(band))).astype(jnp.bfloat16)


def split2(x):
    high = x.astype(jnp.bfloat16)
    return high, (x - high.astype(jnp.float32)).astype(jnp.bfloat16)


def split3(x):
    high, low = split2(x)
    rest = x - high.astype(jnp.float32) - low.astype(jnp.float32)
    return high, low, rest.astype(jnp.bfloat16)


def dot(a, b, dims=((1,), (0,))):
    return lax.dot_general(a, b, (dims, ((), ())), preferred_element_type=jnp.float32)


def dot3(a, b, dims=((1,), (0,))):
    (a_high, a_low), (b_high, b_low) = a, b
    left = jnp.concatenate([a_high, a_low, a_high], axis=dims[0][0])
    right = jnp.concatenate([b_high, b_high, b_low], axis=dims[1][0])
    return dot(left, right, dims)


def on_rows(basis_ref, x, transposed):
    basis, side = split2(basis_ref[...]), basis_ref.shape[0]
    dims = ((0,), (0,)) if transposed else ((1,), (0,))
    parts = [dot3(basis, split2(x[i : i + side]), dims) for i in range(0, x.shape[0], side)]
    return parts[0] if len(parts) == 1 else jnp.concatenate(parts, axis=0)


def on_columns(basis_ref, x, transposed):
    basis, side = split2(basis_ref[...]), basis_ref.shape[0]
    dims = ((1,), (0,)) if transposed else ((1,), (1,))
    parts = [dot3(split2(x[:, i : i + side]), basis, dims) for i in range(0, x.shape[1], side)]
    return parts[0] if len(parts) == 1 else jnp.concatenate(parts, axis=1)


def masks_of(places, count):
    width = places.shape[1]
    column = lax.rem(lax.broadcasted_iota(jnp.int32, (band, width), 1), order).astype(jnp.float32)
    masks = []
    for row in range(count):
        start = places[count + row : count + row + 1, :]
        masks.append((places[row : row + 1, :], (column >= start) & (column < start + band)))
    return masks


def rows_taken(x, masks):
    pieces = []
    for row, (at, _) in enumerate(masks):
        taken = jnp.zeros((band, x.shape[1]), jnp.float32)
        for step in range(steps):
            start = row * order + step * band
            taken = jnp.where(at == step * band, x[start : start + band], taken)
        pieces.append(taken)
    return jnp.concatenate(pieces, axis=0)


def selected(x, masks, basis_ref):
    taken = rows_taken(on_rows(basis_ref, x, False), masks)
    return within(on_columns(basis_ref, taken, False), masks)


def within(x, masks):
    return jnp.concatenate(
        [jnp.where(inside, x[i * band : (i + 1) * band], 0.0) for i, (_, inside) in enumerate(masks)], axis=0
    )


def restored(x, masks, basis_ref):
    by_columns = on_columns(basis_ref, x, True)
    pieces = []
    for row, (at, _) in enumerate(masks):
        part = by_columns[row * band : (row + 1) * band]
        pieces += [jnp.where(at == step * band, part, 0.0) for step in range(steps)]
    return on_rows(basis_ref, jnp.concatenate(pieces, axis=0), True)


def bands_of(x, places, fold_ref, basis_ref):
    return folded(selected(x, masks_of(places, x.shape[0] // order), basis_ref), fold_ref[...])


def folded(x, fold):
    return dot(jnp.concatenate(split3(x), axis=1), jnp.concatenate([fold] * 3, axis=0))


def spread(x, fold):
    return dot(jnp.concatenate(split3(x), axis=1), jnp.concatenate([fold] * 3, axis=1), ((1,), (1,)))


def bands_kernel(m_ref, places_ref, *refs):
    *matrix_refs, bands_ref = refs
    bands_ref[...] = bands_of(m_ref[...], places_ref[...], *matrix_refs)


def coded(x):
    top = jnp.max(jnp.abs(x), axis=0, keepdims=True)
    exponent = jnp.ceil(jnp.log2(jnp.maximum(top, 1e-30)) + 0.01)
    scaled = x * jnp.exp2(15.0 - exponent)
    values = jnp.clip(jnp.round(scaled), -32767.0, 32767.0).astype(jnp.int32).astype(jnp.int16)
    row = jnp.broadcast_to(exponent, (code_rows, x.shape[1])).astype(jnp.int32).astype(jnp.int16)
    return values, row


def decoded(ref):
    values = ref[: ref.shape[0] - code_rows].astype(jnp.int32).astype(jnp.float32)
    exponents = ref[ref.shape[0] - code_rows :].astype(jnp.int32).astype(jnp.float32)
    return values * jnp.exp2(exponents[:1] - 15.0)


def swapped_kernel(m_ref, far_hidden_ref, cross_hidden_ref, cross_ref, swapped_ref, places_ref, *refs):
    *matrix_refs, out_ref, helped_ref, own_turned_ref, end_turned_ref, end_places_ref, bands_ref = refs
    handed, side = swapped_ref.shape[0] - place_rows, out_ref.shape[0]
    alone = cross_ref.shape[0] - handed
    out_ref[...] = m_ref[...] + dot(cross_hidden_ref[...], swapped_ref[:handed], ((0,), (0,)))
    helped_ref[...] = dot(swapped_ref[:alone, :side], cross_ref[handed:], ((0,), (0,)))
    own_turned_ref[...] = far_hidden_ref[...].T
    end_turned_ref[:, : handed - alone] = swapped_ref[alone:handed, :side].T
    end_turned_ref[:, handed - alone :] = swapped_ref[:handed, side:].T
    end_places_ref[...] = swapped_ref[handed:].astype(jnp.float32)
    bands_ref[...] = bands_of(out_ref[...], places_ref[...], *matrix_refs)


def helped_kernel(helped_ref, turned_ref, far_ref, places_ref, *refs):
    *matrix_refs, code_ref, bands_ref = refs
    product = helped_ref[...] + dot(turned_ref[...], far_ref[...])
    bands_ref[...] = bands_of(product, places_ref[...], *matrix_refs)
    side = product.shape[0]
    code_ref[:side], code_ref[side:] = coded(product)


def last_rows_kernel(end_ref, m_ref, own_bands_ref, turned_ref, far_ref, places_ref, *refs):
    *matrix_refs, out_ref, bands_ref = refs

    @pl.when(end_ref[0] == 1)
    def _():
        out_ref[...] = m_ref[...]
        bands_ref[...] = own_bands_ref[...]

    @pl.when(end_ref[0] == 0)
    def _():
        out_ref[...] = m_ref[...] + dot(turned_ref[...], far_ref[...])
        bands_ref[...] = bands_of(out_ref[...], places_ref[...], *matrix_refs)


def remove_kernel(m_ref, bands_ref, places_ref, fold_ref, basis_ref, out_ref):
    masks = masks_of(places_ref[...], out_ref.shape[0] // order)
    coefficients = within(spread(bands_ref[...], fold_ref[...]), masks)
    out_ref[...] = m_ref[...] - restored(coefficients, masks, basis_ref)


def add_kernel(x_ref, code_ref, out_ref):
    out_ref[...] = x_ref[...] + decoded(code_ref)


def update_kernel(*refs):
    *part_refs, places_ref, fold_ref, basis_ref, out_ref = refs
    bands = pair_sum([ref[...] for ref in part_refs])
    masks = masks_of(places_ref[...], out_ref.shape[0] // order)
    coefficients = within(spread(bands, fold_ref[...]), masks)
    out_ref[...] = restored(coefficients, masks, basis_ref).astype(out_ref.dtype)


def pair_sum(parts):
    while len(parts) > 1:
        parts = [sum(parts[i + 1 : i + 2], parts[i]) for i in range(0, len(parts), 2)]
    return parts[0]


def call(kernel, out_shapes, *operands):
    spaces = [pltpu.SMEM if x.dtype == jnp.int32 else pltpu.VMEM for x in operands]
    return pl.pallas_call(
        kernel,
        out_shape=out_shapes,
        in_specs=[pl.BlockSpec(memory_space=space) for space in spaces],
        compiler_params=pltpu.CompilerParams(vmem_limit_bytes=16 * 2**20),
        cost_estimate=pl.CostEstimate(flops=4 * 10**8, bytes_accessed=4 * 10**6, transcendentals=0),
    )(*operands)


def spread_sum(x, axis):
    size = lax.axis_size(axis)
    if size & (size - 1):
        return [lax.psum(x, axis)]
    stride, parts = 1, [x]
    while stride < size:
        count = min(4, size // stride)
        x = pair_sum(parts)
        parts = [x] + [
            lax.ppermute(x, axis, [(i, i ^ (stride * k)) for i in range(size)]) for k in range(1, count)
        ]
        stride *= count
    return parts


def product(hidden_rows, grad_rows):
    return dot(hidden_rows, grad_rows, ((0,), (0,)))


def after(x, *others):
    return lax.optimization_barrier((x, *others))[0]


def gathered(hidden, out_grad, carried, places, matrices):
    m = carried + product(hidden, lax.all_gather(out_grad, "tp", axis=0, tiled=True))
    folded = jax.ShapeDtypeStruct((m.shape[0] // steps, m.shape[1] // steps), jnp.float32)
    bands = call(bands_kernel, folded, m, places, *matrices)
    return m, bands, None, spread_sum(bands, "rep"), places, matrices


def lined(hidden, out_grad, carried, places, matrices):
    tok = out_grad.shape[0]
    me = lax.axis_index("tp")
    left = me < 2
    end = (me == 0) | (me == 3)
    cross = jnp.where(left, 2, 1)
    far = jnp.where(left, 3, 0)
    handed = tok * 2 // 3
    alone = tok - handed

    def rows_of(part, start=0, stop=tok):
        return lax.dynamic_slice_in_dim(hidden, part * tok + start, stop - start, 0)

    def send(x, perm):
        return lax.ppermute(x, "tp", perm)

    both_ways = [(0, 1), (1, 0), (2, 3), (3, 2)]
    across = [(1, 2), (2, 1), (0, 0), (3, 3)]
    outward = [(1, 0), (2, 3)]

    pair_grad = send(out_grad, both_ways)
    cross_grad = send(out_grad, across)
    m = carried + product(rows_of(me), out_grad)
    far_hidden = rows_of(far)
    helped_hidden = jnp.concatenate(
        [
            jnp.concatenate([rows_of(cross, handed), far_hidden[: handed - alone]], axis=0),
            far_hidden[handed - alone :],
        ],
        axis=1,
    )
    place_part = jnp.pad(places.astype(hidden.dtype), ((0, place_rows - places.shape[0]), (0, 0)))
    helped_hidden = jnp.concatenate([helped_hidden, place_part], axis=0)
    cross_hidden = jnp.where(end, rows_of(cross, 0, handed), 0)
    middle_hidden = jnp.where(end, 0, rows_of(cross))
    helped_hidden, cross_hidden, middle_hidden, m = lax.optimization_barrier(
        (helped_hidden, cross_hidden, middle_hidden, m)
    )

    far_grad = send(pair_grad, across)
    cross_grad, matrices, places = after((cross_grad, matrices, places), pair_grad, m)
    swapped = send(jnp.where(end, helped_hidden, cross_grad[: handed + place_rows]), both_ways)
    m = m + product(rows_of(me ^ 1), pair_grad) + product(middle_hidden, cross_grad)

    height, width = m.shape[0] // steps, m.shape[1] // steps
    full = jax.ShapeDtypeStruct(m.shape, jnp.float32)
    turned = jax.ShapeDtypeStruct((m.shape[0], tok), hidden.dtype)
    table = jax.ShapeDtypeStruct((place_rows, m.shape[1]), jnp.float32)
    folded = jax.ShapeDtypeStruct((height, width), jnp.float32)
    m, helped, own_turned, end_turned, end_places, own_bands = call(
        swapped_kernel,
        (full, full, turned, turned, table, folded),
        m,
        far_hidden,
        cross_hidden,
        cross_grad,
        swapped,
        places,
        *matrices,
    )
    far_grad = after(far_grad, m)
    code_shape = jax.ShapeDtypeStruct((m.shape[0] + code_rows, m.shape[1]), jnp.int16)
    code, end_bands = call(
        helped_kernel, (code_shape, folded), helped, end_turned, far_grad, end_places, *matrices
    )
    m, end_bands, code = lax.optimization_barrier((m, end_bands, code))
    end_bands = send(end_bands, both_ways)
    flag = end.astype(jnp.int32).reshape(1)
    m, bands = call(
        last_rows_kernel, (full, folded), flag, m, own_bands, own_turned, far_grad, places, *matrices
    )
    bands, code = lax.optimization_barrier((bands, code))
    code = send(code, outward)
    end_bands, bands = lax.optimization_barrier((end_bands, bands))
    bands = bands + jnp.where(end, end_bands, 0.0)
    parts = spread_sum(bands, "rep")
    return m, bands, code, parts, places, matrices


def local(hidden, out_grad, momentum, band_rows, band_start_columns):
    row_count = hidden.shape[1]
    col_count = out_grad.shape[1]
    one_hot = jnp.asarray(np.kron(np.eye(col_count // order), np.ones((1, order))), jnp.float32)
    matrices = (jnp.asarray(fold_matrix(col_count)), jnp.asarray(diagonal_blocks(row_count, col_count)))
    places = jnp.concatenate([band_rows, band_start_columns], axis=0).astype(jnp.float32)
    places = dot(places, one_hot)
    fits = out_grad.shape[0] % 384 == 0 and 2 * row_count == col_count and places.shape[0] <= place_rows
    form = lined if fits and lax.axis_size("tp") == 4 else gathered
    m, bands, code, band_parts, places, matrices = form(
        hidden, out_grad, decay_rate * momentum[0], places, matrices
    )
    full = jax.ShapeDtypeStruct(m.shape, jnp.float32)
    momentum_out = call(remove_kernel, full, m, bands, places, *matrices)
    if code is not None:
        momentum_out = call(add_kernel, full, momentum_out, code)
    *band_parts, momentum_out = lax.optimization_barrier((*band_parts, momentum_out))
    update = call(update_kernel, jax.ShapeDtypeStruct(m.shape, jnp.bfloat16), *band_parts, places, *matrices)
    return (momentum_out[None], update)


def solution(mesh):
    return jax.shard_map(
        local,
        mesh=mesh,
        in_specs=(
            P("rep", "tp"),
            P(("rep", "tp"), None),
            P("rep", "tp", None),
            P("tp", None),
            P("tp", None),
        ),
        out_specs=(P("rep", "tp", None), P("tp", None)),
        check_vma=False,
    )
```

```python
import jax
import jax.numpy as jnp
import numpy as np
from jax import lax
from jax.experimental import pallas as pl
from jax.experimental.pallas import tpu as pltpu
from jax.sharding import PartitionSpec as P

decay_rate = 0.9
order = 64
band = 16
steps = order // band
place_rows = 16
code_rows = 16


def basis_matrix():
    frequency = np.arange(order, dtype=np.float64)[:, None]
    sample_pos = np.arange(order, dtype=np.float64)[None, :]
    norm_scale = np.where(frequency == 0, np.sqrt(1.0 / order), np.sqrt(2.0 / order))
    return norm_scale * np.cos(np.pi * (sample_pos + 0.5) * frequency / order)


def diagonal_blocks(*widths):
    count = next(c for c in (4, 2, 1) if all(width % (c * order) == 0 for width in widths))
    return np.kron(np.eye(count), basis_matrix()).astype(np.float32)


def fold_matrix(width):
    return np.kron(np.eye(width // order), np.kron(np.ones((steps, 1)), np.eye(band))).astype(jnp.bfloat16)


def split2(x):
    high = x.astype(jnp.bfloat16)
    return high, (x - high.astype(jnp.float32)).astype(jnp.bfloat16)


def split3(x):
    high, low = split2(x)
    rest = x - high.astype(jnp.float32) - low.astype(jnp.float32)
    return high, low, rest.astype(jnp.bfloat16)


def dot(a, b, dims=((1,), (0,))):
    return lax.dot_general(a, b, (dims, ((), ())), preferred_element_type=jnp.float32)


def dot3(a, b, dims=((1,), (0,))):
    (a_high, a_low), (b_high, b_low) = a, b
    left = jnp.concatenate([a_high, a_low, a_high], axis=dims[0][0])
    right = jnp.concatenate([b_high, b_high, b_low], axis=dims[1][0])
    return dot(left, right, dims)


def on_rows(basis_ref, x, transposed):
    basis, side = split2(basis_ref[...]), basis_ref.shape[0]
    dims = ((0,), (0,)) if transposed else ((1,), (0,))
    parts = [dot3(basis, split2(x[i : i + side]), dims) for i in range(0, x.shape[0], side)]
    return parts[0] if len(parts) == 1 else jnp.concatenate(parts, axis=0)


def on_columns(basis_ref, x, transposed):
    basis, side = split2(basis_ref[...]), basis_ref.shape[0]
    dims = ((1,), (0,)) if transposed else ((1,), (1,))
    parts = [dot3(split2(x[:, i : i + side]), basis, dims) for i in range(0, x.shape[1], side)]
    return parts[0] if len(parts) == 1 else jnp.concatenate(parts, axis=1)


def masks_of(places, count):
    width = places.shape[1]
    column = lax.rem(lax.broadcasted_iota(jnp.int32, (band, width), 1), order).astype(jnp.float32)
    masks = []
    for row in range(count):
        start = places[count + row : count + row + 1, :]
        masks.append((places[row : row + 1, :], (column >= start) & (column < start + band)))
    return masks


def rows_taken(x, masks):
    pieces = []
    for row, (at, _) in enumerate(masks):
        taken = jnp.zeros((band, x.shape[1]), jnp.float32)
        for step in range(steps):
            start = row * order + step * band
            taken = jnp.where(at == step * band, x[start : start + band], taken)
        pieces.append(taken)
    return jnp.concatenate(pieces, axis=0)


def selected(x, masks, basis_ref):
    taken = rows_taken(on_rows(basis_ref, x, False), masks)
    return within(on_columns(basis_ref, taken, False), masks)


def within(x, masks):
    return jnp.concatenate(
        [jnp.where(inside, x[i * band : (i + 1) * band], 0.0) for i, (_, inside) in enumerate(masks)], axis=0
    )


def restored(x, masks, basis_ref):
    by_columns = on_columns(basis_ref, x, True)
    pieces = []
    for row, (at, _) in enumerate(masks):
        part = by_columns[row * band : (row + 1) * band]
        pieces += [jnp.where(at == step * band, part, 0.0) for step in range(steps)]
    return on_rows(basis_ref, jnp.concatenate(pieces, axis=0), True)


def bands_of(x, places, fold_ref, basis_ref):
    return folded(selected(x, masks_of(places, x.shape[0] // order), basis_ref), fold_ref[...])


def folded(x, fold):
    return dot(jnp.concatenate(split3(x), axis=1), jnp.concatenate([fold] * 3, axis=0))


def spread(x, fold):
    return dot(jnp.concatenate(split3(x), axis=1), jnp.concatenate([fold] * 3, axis=1), ((1,), (1,)))


def bands_kernel(m_ref, places_ref, *refs):
    *matrix_refs, bands_ref = refs
    bands_ref[...] = bands_of(m_ref[...], places_ref[...], *matrix_refs)


def coded(x):
    top = jnp.max(jnp.abs(x), axis=0, keepdims=True)
    exponent = jnp.ceil(jnp.log2(jnp.maximum(top, 1e-30)) + 0.01)
    scaled = x * jnp.exp2(15.0 - exponent)
    values = jnp.clip(jnp.round(scaled), -32767.0, 32767.0).astype(jnp.int32).astype(jnp.int16)
    row = jnp.broadcast_to(exponent, (code_rows, x.shape[1])).astype(jnp.int32).astype(jnp.int16)
    return values, row


def decoded(ref):
    values = ref[: ref.shape[0] - code_rows].astype(jnp.int32).astype(jnp.float32)
    exponents = ref[ref.shape[0] - code_rows :].astype(jnp.int32).astype(jnp.float32)
    return values * jnp.exp2(exponents[:1] - 15.0)


def swapped_kernel(m_ref, hidden_ref, cross_hidden_ref, cross_ref, far_ref, swapped_ref, places_ref, *refs):
    *matrix_refs, out_ref, helped_ref, own_turned_ref, end_turned_ref, end_places_ref, bands_ref = refs
    handed, side = far_ref.shape[0], out_ref.shape[0]
    alone = cross_ref.shape[0] - handed
    out_ref[...] = m_ref[...] + dot(cross_hidden_ref[...], swapped_ref[:handed], ((0,), (0,)))
    helped_ref[...] = (
        dot(swapped_ref[:alone, :side], cross_ref[handed:], ((0,), (0,)))
        + dot(swapped_ref[alone:handed, :side], far_ref[: handed - alone], ((0,), (0,)))
        + dot(swapped_ref[:alone, side:], far_ref[handed - alone :], ((0,), (0,)))
    )
    own_turned_ref[...] = hidden_ref[...].T
    end_turned_ref[...] = swapped_ref[alone:handed, side:].T
    end_places_ref[...] = swapped_ref[handed:].astype(jnp.float32)
    bands_ref[...] = bands_of(out_ref[...], places_ref[...], *matrix_refs)


def helped_kernel(helped_ref, turned_ref, far_ref, places_ref, *refs):
    *matrix_refs, code_ref, bands_ref = refs
    product = helped_ref[...] + dot(turned_ref[...], far_ref[...])
    bands_ref[...] = bands_of(product, places_ref[...], *matrix_refs)
    side = product.shape[0]
    code_ref[:side], code_ref[side:] = coded(product)


def last_rows_kernel(end_ref, m_ref, own_bands_ref, turned_ref, far_ref, places_ref, *refs):
    *matrix_refs, out_ref, bands_ref = refs

    @pl.when(end_ref[0] == 1)
    def _():
        out_ref[...] = m_ref[...]
        bands_ref[...] = own_bands_ref[...]

    @pl.when(end_ref[0] == 0)
    def _():
        out_ref[...] = m_ref[...] + dot(turned_ref[...], far_ref[...])
        bands_ref[...] = bands_of(out_ref[...], places_ref[...], *matrix_refs)


def remove_kernel(m_ref, bands_ref, places_ref, fold_ref, basis_ref, out_ref):
    masks = masks_of(places_ref[...], out_ref.shape[0] // order)
    coefficients = within(spread(bands_ref[...], fold_ref[...]), masks)
    out_ref[...] = m_ref[...] - restored(coefficients, masks, basis_ref)


def add_kernel(x_ref, code_ref, out_ref):
    out_ref[...] = x_ref[...] + decoded(code_ref)


def update_kernel(*refs):
    *part_refs, places_ref, fold_ref, basis_ref, out_ref = refs
    bands = pair_sum([ref[...] for ref in part_refs])
    masks = masks_of(places_ref[...], out_ref.shape[0] // order)
    coefficients = within(spread(bands, fold_ref[...]), masks)
    out_ref[...] = restored(coefficients, masks, basis_ref).astype(out_ref.dtype)


def pair_sum(parts):
    while len(parts) > 1:
        parts = [sum(parts[i + 1 : i + 2], parts[i]) for i in range(0, len(parts), 2)]
    return parts[0]


def call(kernel, out_shapes, *operands):
    spaces = [pltpu.SMEM if x.dtype == jnp.int32 else pltpu.VMEM for x in operands]
    return pl.pallas_call(
        kernel,
        out_shape=out_shapes,
        in_specs=[pl.BlockSpec(memory_space=space) for space in spaces],
        compiler_params=pltpu.CompilerParams(vmem_limit_bytes=16 * 2**20),
        cost_estimate=pl.CostEstimate(flops=4 * 10**8, bytes_accessed=4 * 10**6, transcendentals=0),
    )(*operands)


def spread_sum(x, axis):
    size = lax.axis_size(axis)
    if size & (size - 1):
        return [lax.psum(x, axis)]
    stride, parts = 1, [x]
    while stride < size:
        count = min(4, size // stride)
        x = pair_sum(parts)
        parts = [x] + [
            lax.ppermute(x, axis, [(i, i ^ (stride * k)) for i in range(size)]) for k in range(1, count)
        ]
        stride *= count
    return parts


def product(hidden_rows, grad_rows):
    return dot(hidden_rows, grad_rows, ((0,), (0,)))


def after(x, *others):
    return lax.optimization_barrier((x, *others))[0]


def gathered(hidden, out_grad, carried, places, matrices):
    m = carried + product(hidden, lax.all_gather(out_grad, "tp", axis=0, tiled=True))
    folded = jax.ShapeDtypeStruct((m.shape[0] // steps, m.shape[1] // steps), jnp.float32)
    bands = call(bands_kernel, folded, m, places, *matrices)
    return m, bands, None, spread_sum(bands, "rep"), places, matrices


def lined(hidden, out_grad, carried, places, matrices):
    tok = out_grad.shape[0]
    me = lax.axis_index("tp")
    left = me < 2
    end = (me == 0) | (me == 3)
    cross = jnp.where(left, 2, 1)
    far = jnp.where(left, 3, 0)
    handed = tok * 2 // 3
    alone = tok - handed

    def rows_of(part, start=0, stop=tok):
        return lax.dynamic_slice_in_dim(hidden, part * tok + start, stop - start, 0)

    def send(x, perm):
        return lax.ppermute(x, "tp", perm)

    both_ways = [(0, 1), (1, 0), (2, 3), (3, 2)]
    across = [(1, 2), (2, 1)]
    outward = [(1, 0), (2, 3)]

    cross_grad = send(out_grad, across)
    m = carried + product(rows_of(me), out_grad)
    own, m = lax.optimization_barrier((out_grad, m))
    pair_parts = [send(own[:handed], both_ways), send(own[handed:], both_ways)]
    far_hidden = rows_of(far)
    helped_hidden = jnp.concatenate(
        [
            jnp.concatenate([rows_of(cross, handed), far_hidden[: handed - alone]], axis=0),
            far_hidden[handed - alone :],
        ],
        axis=1,
    )
    place_part = jnp.pad(places.astype(hidden.dtype), ((0, place_rows - places.shape[0]), (0, 0)))
    helped_hidden = jnp.concatenate([helped_hidden, place_part], axis=0)
    cross_hidden = jnp.where(end, rows_of(cross, 0, handed), 0)
    helped_hidden, cross_hidden, m = lax.optimization_barrier((helped_hidden, cross_hidden, m))

    far_head = send(pair_parts[0], across)
    m = m + product(rows_of(me ^ 1, 0, handed), pair_parts[0])
    pair_rest, m = lax.optimization_barrier((pair_parts[1], m))
    far_parts = [far_head, send(pair_rest, across)]
    cross_grad, matrices, places = after((cross_grad, matrices, places), pair_parts[0], m)
    swapped = send(jnp.where(end, helped_hidden, cross_grad[: handed + place_rows]), both_ways)
    far_parts[0], pair_rest, cross_grad = lax.optimization_barrier((far_parts[0], pair_rest, cross_grad))
    m = m + product(rows_of(me ^ 1, handed), pair_rest)
    m = m + product(rows_of(cross), cross_grad) + product(far_hidden[:handed], far_parts[0])
    m, swapped = lax.optimization_barrier((m, swapped))

    height, width = m.shape[0] // steps, m.shape[1] // steps
    full = jax.ShapeDtypeStruct(m.shape, jnp.float32)
    turned = jax.ShapeDtypeStruct((m.shape[0], alone), hidden.dtype)
    table = jax.ShapeDtypeStruct((place_rows, m.shape[1]), jnp.float32)
    folded = jax.ShapeDtypeStruct((height, width), jnp.float32)
    m, helped, own_turned, end_turned, end_places, own_bands = call(
        swapped_kernel,
        (full, full, turned, turned, table, folded),
        m,
        far_hidden[handed:],
        cross_hidden,
        cross_grad,
        far_parts[0],
        swapped,
        places,
        *matrices,
    )
    far_grad = after(far_parts[1], m)
    code_shape = jax.ShapeDtypeStruct((m.shape[0] + code_rows, m.shape[1]), jnp.int16)
    code, end_bands = call(
        helped_kernel, (code_shape, folded), helped, end_turned, far_grad, end_places, *matrices
    )
    m, end_bands, code = lax.optimization_barrier((m, end_bands, code))
    end_bands = send(end_bands, both_ways)
    flag = end.astype(jnp.int32).reshape(1)
    m, bands = call(
        last_rows_kernel, (full, folded), flag, m, own_bands, own_turned, far_grad, places, *matrices
    )
    bands, code = lax.optimization_barrier((bands, code))
    code = send(code, outward)
    end_bands, bands = lax.optimization_barrier((end_bands, bands))
    bands = bands + jnp.where(end, end_bands, 0.0)
    parts = spread_sum(bands, "rep")
    return m, bands, code, parts, places, matrices


def local(hidden, out_grad, momentum, band_rows, band_start_columns):
    row_count = hidden.shape[1]
    col_count = out_grad.shape[1]
    one_hot = jnp.asarray(np.kron(np.eye(col_count // order), np.ones((1, order))), jnp.float32)
    matrices = (jnp.asarray(fold_matrix(col_count)), jnp.asarray(diagonal_blocks(row_count, col_count)))
    places = jnp.concatenate([band_rows, band_start_columns], axis=0).astype(jnp.float32)
    places = dot(places, one_hot)
    fits = out_grad.shape[0] % 384 == 0 and 2 * row_count == col_count and places.shape[0] <= place_rows
    form = lined if fits and lax.axis_size("tp") == 4 else gathered
    m, bands, code, band_parts, places, matrices = form(
        hidden, out_grad, decay_rate * momentum[0], places, matrices
    )
    full = jax.ShapeDtypeStruct(m.shape, jnp.float32)
    momentum_out = call(remove_kernel, full, m, bands, places, *matrices)
    if code is not None:
        momentum_out = call(add_kernel, full, momentum_out, code)
    *band_parts, momentum_out = lax.optimization_barrier((*band_parts, momentum_out))
    update = call(update_kernel, jax.ShapeDtypeStruct(m.shape, jnp.bfloat16), *band_parts, places, *matrices)
    return (momentum_out[None], update)


def solution(mesh):
    return jax.shard_map(
        local,
        mesh=mesh,
        in_specs=(
            P("rep", "tp"),
            P(("rep", "tp"), None),
            P("rep", "tp", None),
            P("tp", None),
            P("tp", None),
        ),
        out_specs=(P("rep", "tp", None), P("tp", None)),
        check_vma=False,
    )
```

```python
import jax
import jax.numpy as jnp
import numpy as np
from jax import lax
from jax.experimental import pallas as pl
from jax.experimental.pallas import tpu as pltpu
from jax.sharding import PartitionSpec as P

decay_rate = 0.9
order = 64
band = 16
steps = order // band
place_rows = 16
code_rows = 16


def basis_matrix():
    frequency = np.arange(order, dtype=np.float64)[:, None]
    sample_pos = np.arange(order, dtype=np.float64)[None, :]
    norm_scale = np.where(frequency == 0, np.sqrt(1.0 / order), np.sqrt(2.0 / order))
    return norm_scale * np.cos(np.pi * (sample_pos + 0.5) * frequency / order)


def diagonal_blocks(*widths):
    count = next(c for c in (4, 2, 1) if all(width % (c * order) == 0 for width in widths))
    return np.kron(np.eye(count), basis_matrix()).astype(np.float32)


def fold_matrix(width):
    return np.kron(np.eye(width // order), np.kron(np.ones((steps, 1)), np.eye(band))).astype(jnp.bfloat16)


def split2(x):
    high = x.astype(jnp.bfloat16)
    return high, (x - high.astype(jnp.float32)).astype(jnp.bfloat16)


def split3(x):
    high, low = split2(x)
    rest = x - high.astype(jnp.float32) - low.astype(jnp.float32)
    return high, low, rest.astype(jnp.bfloat16)


def dot(a, b, dims=((1,), (0,))):
    return lax.dot_general(a, b, (dims, ((), ())), preferred_element_type=jnp.float32)


def dot3(a, b, dims=((1,), (0,))):
    (a_high, a_low), (b_high, b_low) = a, b
    left = jnp.concatenate([a_high, a_low, a_high], axis=dims[0][0])
    right = jnp.concatenate([b_high, b_high, b_low], axis=dims[1][0])
    return dot(left, right, dims)


def on_rows(basis_ref, x, transposed):
    basis, side = split2(basis_ref[...]), basis_ref.shape[0]
    dims = ((0,), (0,)) if transposed else ((1,), (0,))
    parts = [dot3(basis, split2(x[i : i + side]), dims) for i in range(0, x.shape[0], side)]
    return parts[0] if len(parts) == 1 else jnp.concatenate(parts, axis=0)


def on_columns(basis_ref, x, transposed):
    basis, side = split2(basis_ref[...]), basis_ref.shape[0]
    dims = ((1,), (0,)) if transposed else ((1,), (1,))
    parts = [dot3(split2(x[:, i : i + side]), basis, dims) for i in range(0, x.shape[1], side)]
    return parts[0] if len(parts) == 1 else jnp.concatenate(parts, axis=1)


def masks_of(places, count):
    width = places.shape[1]
    column = lax.rem(lax.broadcasted_iota(jnp.int32, (band, width), 1), order).astype(jnp.float32)
    masks = []
    for row in range(count):
        start = places[count + row : count + row + 1, :]
        masks.append((places[row : row + 1, :], (column >= start) & (column < start + band)))
    return masks


def rows_taken(x, masks):
    pieces = []
    for row, (at, _) in enumerate(masks):
        taken = jnp.zeros((band, x.shape[1]), jnp.float32)
        for step in range(steps):
            start = row * order + step * band
            taken = jnp.where(at == step * band, x[start : start + band], taken)
        pieces.append(taken)
    return jnp.concatenate(pieces, axis=0)


def selected(x, masks, basis_ref):
    taken = rows_taken(on_rows(basis_ref, x, False), masks)
    return within(on_columns(basis_ref, taken, False), masks)


def within(x, masks):
    return jnp.concatenate(
        [jnp.where(inside, x[i * band : (i + 1) * band], 0.0) for i, (_, inside) in enumerate(masks)], axis=0
    )


def restored(x, masks, basis_ref):
    by_columns = on_columns(basis_ref, x, True)
    pieces = []
    for row, (at, _) in enumerate(masks):
        part = by_columns[row * band : (row + 1) * band]
        pieces += [jnp.where(at == step * band, part, 0.0) for step in range(steps)]
    return on_rows(basis_ref, jnp.concatenate(pieces, axis=0), True)


def bands_of(x, places, fold_ref, basis_ref):
    return folded(selected(x, masks_of(places, x.shape[0] // order), basis_ref), fold_ref[...])


def folded(x, fold):
    return dot(jnp.concatenate(split3(x), axis=1), jnp.concatenate([fold] * 3, axis=0))


def spread(x, fold):
    return dot(jnp.concatenate(split3(x), axis=1), jnp.concatenate([fold] * 3, axis=1), ((1,), (1,)))


def bands_kernel(m_ref, places_ref, *refs):
    *matrix_refs, bands_ref = refs
    bands_ref[...] = bands_of(m_ref[...], places_ref[...], *matrix_refs)


def coded(x):
    top = jnp.max(jnp.abs(x), axis=0, keepdims=True)
    exponent = jnp.ceil(jnp.log2(jnp.maximum(top, 1e-30)) + 0.01)
    scaled = x * jnp.exp2(15.0 - exponent)
    values = jnp.clip(jnp.round(scaled), -32767.0, 32767.0).astype(jnp.int32).astype(jnp.int16)
    row = jnp.broadcast_to(exponent, (code_rows, x.shape[1])).astype(jnp.int32).astype(jnp.int16)
    return values, row


def decoded(ref):
    values = ref[: ref.shape[0] - code_rows].astype(jnp.int32).astype(jnp.float32)
    exponents = ref[ref.shape[0] - code_rows :].astype(jnp.int32).astype(jnp.float32)
    return values * jnp.exp2(exponents[:1] - 15.0)


def swapped_kernel(m_ref, hidden_ref, cross_hidden_ref, cross_ref, far_ref, swapped_ref, places_ref, *refs):
    *matrix_refs, out_ref, helped_ref, own_turned_ref, end_turned_ref, end_places_ref, bands_ref = refs
    handed, side = far_ref.shape[0], out_ref.shape[0]
    alone = cross_ref.shape[0] - handed
    out_ref[...] = m_ref[...] + dot(cross_hidden_ref[...], swapped_ref[:handed], ((0,), (0,)))
    helped_ref[...] = (
        dot(swapped_ref[:alone, :side], cross_ref[handed:], ((0,), (0,)))
        + dot(swapped_ref[alone:handed, :side], far_ref[: handed - alone], ((0,), (0,)))
        + dot(swapped_ref[:alone, side:], far_ref[handed - alone :], ((0,), (0,)))
    )
    own_turned_ref[...] = hidden_ref[...].T
    end_turned_ref[...] = swapped_ref[alone:handed, side:].T
    end_places_ref[...] = swapped_ref[handed:].astype(jnp.float32)
    bands_ref[...] = bands_of(out_ref[...], places_ref[...], *matrix_refs)


def helped_kernel(helped_ref, turned_ref, far_ref, places_ref, *refs):
    *matrix_refs, code_ref, bands_ref = refs
    product = helped_ref[...] + dot(turned_ref[...], far_ref[...])
    bands_ref[...] = bands_of(product, places_ref[...], *matrix_refs)
    side = product.shape[0]
    code_ref[:side], code_ref[side:] = coded(product)


def last_rows_kernel(end_ref, m_ref, own_bands_ref, turned_ref, far_ref, places_ref, *refs):
    *matrix_refs, out_ref, bands_ref = refs

    @pl.when(end_ref[0] == 1)
    def _():
        out_ref[...] = m_ref[...]
        bands_ref[...] = own_bands_ref[...]

    @pl.when(end_ref[0] == 0)
    def _():
        out_ref[...] = m_ref[...] + dot(turned_ref[...], far_ref[...])
        bands_ref[...] = bands_of(out_ref[...], places_ref[...], *matrix_refs)


def remove_kernel(m_ref, bands_ref, places_ref, fold_ref, basis_ref, out_ref):
    masks = masks_of(places_ref[...], out_ref.shape[0] // order)
    coefficients = within(spread(bands_ref[...], fold_ref[...]), masks)
    out_ref[...] = m_ref[...] - restored(coefficients, masks, basis_ref)


def add_kernel(x_ref, code_ref, out_ref):
    out_ref[...] = x_ref[...] + decoded(code_ref)


def update_kernel(*refs):
    *part_refs, places_ref, fold_ref, basis_ref, out_ref = refs
    bands = pair_sum([ref[...] for ref in part_refs])
    masks = masks_of(places_ref[...], out_ref.shape[0] // order)
    coefficients = within(spread(bands, fold_ref[...]), masks)
    out_ref[...] = restored(coefficients, masks, basis_ref).astype(out_ref.dtype)


def pair_sum(parts):
    while len(parts) > 1:
        parts = [sum(parts[i + 1 : i + 2], parts[i]) for i in range(0, len(parts), 2)]
    return parts[0]


def call(kernel, out_shapes, *operands):
    spaces = [pltpu.SMEM if x.dtype == jnp.int32 else pltpu.VMEM for x in operands]
    return pl.pallas_call(
        kernel,
        out_shape=out_shapes,
        in_specs=[pl.BlockSpec(memory_space=space) for space in spaces],
        compiler_params=pltpu.CompilerParams(vmem_limit_bytes=16 * 2**20),
        cost_estimate=pl.CostEstimate(flops=4 * 10**8, bytes_accessed=4 * 10**6, transcendentals=0),
    )(*operands)


def spread_sum(x, axis):
    size = lax.axis_size(axis)
    if size & (size - 1):
        return [lax.psum(x, axis)]
    stride, parts = 1, [x]
    while stride < size:
        count = min(4, size // stride)
        x = pair_sum(parts)
        parts = [x] + [
            lax.ppermute(x, axis, [(i, i ^ (stride * k)) for i in range(size)]) for k in range(1, count)
        ]
        stride *= count
    return parts


def product(hidden_rows, grad_rows):
    return dot(hidden_rows, grad_rows, ((0,), (0,)))


def after(x, *others):
    return lax.optimization_barrier((x, *others))[0]


def gathered(hidden, out_grad, carried, places, matrices):
    m = carried + product(hidden, lax.all_gather(out_grad, "tp", axis=0, tiled=True))
    folded = jax.ShapeDtypeStruct((m.shape[0] // steps, m.shape[1] // steps), jnp.float32)
    bands = call(bands_kernel, folded, m, places, *matrices)
    return m, bands, None, spread_sum(bands, "rep"), places, matrices


def lined(hidden, out_grad, carried, places, matrices):
    tok = out_grad.shape[0]
    me = lax.axis_index("tp")
    left = me < 2
    end = (me == 0) | (me == 3)
    cross = jnp.where(left, 2, 1)
    far = jnp.where(left, 3, 0)
    handed = tok * 2 // 3
    alone = tok - handed

    def rows_of(part, start=0, stop=tok):
        return lax.dynamic_slice_in_dim(hidden, part * tok + start, stop - start, 0)

    def send(x, perm):
        return lax.ppermute(x, "tp", perm)

    both_ways = [(0, 1), (1, 0), (2, 3), (3, 2)]
    across = [(1, 2), (2, 1)]
    outward = [(1, 0), (2, 3)]

    cross_grad = send(out_grad, across)
    m = carried + product(rows_of(me), out_grad)
    pair_parts = [send(out_grad[:handed], both_ways), send(out_grad[handed:], both_ways)]
    far_hidden = rows_of(far)
    helped_hidden = jnp.concatenate(
        [
            jnp.concatenate([rows_of(cross, handed), far_hidden[: handed - alone]], axis=0),
            far_hidden[handed - alone :],
        ],
        axis=1,
    )
    place_part = jnp.pad(places.astype(hidden.dtype), ((0, place_rows - places.shape[0]), (0, 0)))
    helped_hidden = jnp.concatenate([helped_hidden, place_part], axis=0)
    cross_hidden = jnp.where(end, rows_of(cross, 0, handed), 0)
    helped_hidden, cross_hidden, m = lax.optimization_barrier((helped_hidden, cross_hidden, m))

    far_head = send(pair_parts[0], across)
    m = m + product(rows_of(me ^ 1, 0, handed), pair_parts[0])
    pair_rest, m = lax.optimization_barrier((pair_parts[1], m))
    far_parts = [far_head, send(pair_rest, across)]
    cross_grad, matrices, places = after((cross_grad, matrices, places), pair_parts[0], m)
    swapped = send(jnp.where(end, helped_hidden, cross_grad[: handed + place_rows]), both_ways)
    far_parts[0], pair_rest, cross_grad = lax.optimization_barrier((far_parts[0], pair_rest, cross_grad))
    m = m + product(rows_of(me ^ 1, handed), pair_rest)
    m = m + product(rows_of(cross), cross_grad) + product(far_hidden[:handed], far_parts[0])
    m, swapped = lax.optimization_barrier((m, swapped))

    height, width = m.shape[0] // steps, m.shape[1] // steps
    full = jax.ShapeDtypeStruct(m.shape, jnp.float32)
    turned = jax.ShapeDtypeStruct((m.shape[0], alone), hidden.dtype)
    table = jax.ShapeDtypeStruct((place_rows, m.shape[1]), jnp.float32)
    folded = jax.ShapeDtypeStruct((height, width), jnp.float32)
    m, helped, own_turned, end_turned, end_places, own_bands = call(
        swapped_kernel,
        (full, full, turned, turned, table, folded),
        m,
        far_hidden[handed:],
        cross_hidden,
        cross_grad,
        far_parts[0],
        swapped,
        places,
        *matrices,
    )
    far_grad = after(far_parts[1], m)
    code_shape = jax.ShapeDtypeStruct((m.shape[0] + code_rows, m.shape[1]), jnp.int16)
    code, end_bands = call(
        helped_kernel, (code_shape, folded), helped, end_turned, far_grad, end_places, *matrices
    )
    m, end_bands, code = lax.optimization_barrier((m, end_bands, code))
    end_bands = send(end_bands, both_ways)
    flag = end.astype(jnp.int32).reshape(1)
    m, bands = call(
        last_rows_kernel, (full, folded), flag, m, own_bands, own_turned, far_grad, places, *matrices
    )
    bands, code = lax.optimization_barrier((bands, code))
    code = send(code, outward)
    end_bands, bands = lax.optimization_barrier((end_bands, bands))
    bands = bands + jnp.where(end, end_bands, 0.0)
    parts = spread_sum(bands, "rep")
    return m, bands, code, parts, places, matrices


def local(hidden, out_grad, momentum, band_rows, band_start_columns):
    row_count = hidden.shape[1]
    col_count = out_grad.shape[1]
    one_hot = jnp.asarray(np.kron(np.eye(col_count // order), np.ones((1, order))), jnp.float32)
    matrices = (jnp.asarray(fold_matrix(col_count)), jnp.asarray(diagonal_blocks(row_count, col_count)))
    places = jnp.concatenate([band_rows, band_start_columns], axis=0).astype(jnp.float32)
    places = dot(places, one_hot)
    fits = out_grad.shape[0] % 384 == 0 and 2 * row_count == col_count and places.shape[0] <= place_rows
    form = lined if fits and lax.axis_size("tp") == 4 else gathered
    m, bands, code, band_parts, places, matrices = form(
        hidden, out_grad, decay_rate * momentum[0], places, matrices
    )
    full = jax.ShapeDtypeStruct(m.shape, jnp.float32)
    momentum_out = call(remove_kernel, full, m, bands, places, *matrices)
    if code is not None:
        momentum_out = call(add_kernel, full, momentum_out, code)
    *band_parts, momentum_out = lax.optimization_barrier((*band_parts, momentum_out))
    update = call(update_kernel, jax.ShapeDtypeStruct(m.shape, jnp.bfloat16), *band_parts, places, *matrices)
    return (momentum_out[None], update)


def solution(mesh):
    return jax.shard_map(
        local,
        mesh=mesh,
        in_specs=(
            P("rep", "tp"),
            P(("rep", "tp"), None),
            P("rep", "tp", None),
            P("tp", None),
            P("tp", None),
        ),
        out_specs=(P("rep", "tp", None), P("tp", None)),
        check_vma=False,
    )
```

```python
import jax
import jax.numpy as jnp
import numpy as np
from jax import lax
from jax.experimental import pallas as pl
from jax.experimental.pallas import tpu as pltpu
from jax.sharding import PartitionSpec as P

decay_rate = 0.9
order = 64
band = 16
steps = order // band
place_rows = 16
code_rows = 16


def basis_matrix():
    frequency = np.arange(order, dtype=np.float64)[:, None]
    sample_pos = np.arange(order, dtype=np.float64)[None, :]
    norm_scale = np.where(frequency == 0, np.sqrt(1.0 / order), np.sqrt(2.0 / order))
    return norm_scale * np.cos(np.pi * (sample_pos + 0.5) * frequency / order)


def diagonal_blocks(*widths):
    count = next(c for c in (4, 2, 1) if all(width % (c * order) == 0 for width in widths))
    return np.kron(np.eye(count), basis_matrix()).astype(np.float32)


def fold_matrix(width):
    return np.kron(np.eye(width // order), np.kron(np.ones((steps, 1)), np.eye(band))).astype(jnp.bfloat16)


def split2(x):
    high = x.astype(jnp.bfloat16)
    return high, (x - high.astype(jnp.float32)).astype(jnp.bfloat16)


def split3(x):
    high, low = split2(x)
    rest = x - high.astype(jnp.float32) - low.astype(jnp.float32)
    return high, low, rest.astype(jnp.bfloat16)


def dot(a, b, dims=((1,), (0,))):
    return lax.dot_general(a, b, (dims, ((), ())), preferred_element_type=jnp.float32)


def dot3(a, b, dims=((1,), (0,))):
    (a_high, a_low), (b_high, b_low) = a, b
    left = jnp.concatenate([a_high, a_low, a_high], axis=dims[0][0])
    right = jnp.concatenate([b_high, b_high, b_low], axis=dims[1][0])
    return dot(left, right, dims)


def on_rows(basis_ref, x, transposed):
    basis, side = split2(basis_ref[...]), basis_ref.shape[0]
    dims = ((0,), (0,)) if transposed else ((1,), (0,))
    parts = [dot3(basis, split2(x[i : i + side]), dims) for i in range(0, x.shape[0], side)]
    return parts[0] if len(parts) == 1 else jnp.concatenate(parts, axis=0)


def on_columns(basis_ref, x, transposed):
    basis, side = split2(basis_ref[...]), basis_ref.shape[0]
    dims = ((1,), (0,)) if transposed else ((1,), (1,))
    parts = [dot3(split2(x[:, i : i + side]), basis, dims) for i in range(0, x.shape[1], side)]
    return parts[0] if len(parts) == 1 else jnp.concatenate(parts, axis=1)


def masks_of(places, count):
    width = places.shape[1]
    column = lax.rem(lax.broadcasted_iota(jnp.int32, (band, width), 1), order).astype(jnp.float32)
    masks = []
    for row in range(count):
        start = places[count + row : count + row + 1, :]
        masks.append((places[row : row + 1, :], (column >= start) & (column < start + band)))
    return masks


def rows_taken(x, masks):
    pieces = []
    for row, (at, _) in enumerate(masks):
        taken = jnp.zeros((band, x.shape[1]), jnp.float32)
        for step in range(steps):
            start = row * order + step * band
            taken = jnp.where(at == step * band, x[start : start + band], taken)
        pieces.append(taken)
    return jnp.concatenate(pieces, axis=0)


def selected(x, masks, basis_ref):
    taken = rows_taken(on_rows(basis_ref, x, False), masks)
    return within(on_columns(basis_ref, taken, False), masks)


def within(x, masks):
    return jnp.concatenate(
        [jnp.where(inside, x[i * band : (i + 1) * band], 0.0) for i, (_, inside) in enumerate(masks)], axis=0
    )


def restored(x, masks, basis_ref):
    by_columns = on_columns(basis_ref, x, True)
    pieces = []
    for row, (at, _) in enumerate(masks):
        part = by_columns[row * band : (row + 1) * band]
        pieces += [jnp.where(at == step * band, part, 0.0) for step in range(steps)]
    return on_rows(basis_ref, jnp.concatenate(pieces, axis=0), True)


def bands_of(x, places, fold_ref, basis_ref):
    return folded(selected(x, masks_of(places, x.shape[0] // order), basis_ref), fold_ref[...])


def folded(x, fold):
    return dot(jnp.concatenate(split3(x), axis=1), jnp.concatenate([fold] * 3, axis=0))


def spread(x, fold):
    return dot(jnp.concatenate(split3(x), axis=1), jnp.concatenate([fold] * 3, axis=1), ((1,), (1,)))


def bands_kernel(m_ref, places_ref, *refs):
    *matrix_refs, bands_ref = refs
    bands_ref[...] = bands_of(m_ref[...], places_ref[...], *matrix_refs)


def coded(x):
    top = jnp.max(jnp.abs(x), axis=0, keepdims=True)
    exponent = jnp.ceil(jnp.log2(jnp.maximum(top, 1e-30)) + 0.01)
    scaled = x * jnp.exp2(15.0 - exponent)
    values = jnp.clip(jnp.round(scaled), -32767.0, 32767.0).astype(jnp.int32).astype(jnp.int16)
    row = jnp.broadcast_to(exponent, (code_rows, x.shape[1])).astype(jnp.int32).astype(jnp.int16)
    return values, row


def decoded(ref):
    values = ref[: ref.shape[0] - code_rows].astype(jnp.int32).astype(jnp.float32)
    exponents = ref[ref.shape[0] - code_rows :].astype(jnp.int32).astype(jnp.float32)
    return values * jnp.exp2(exponents[:1] - 15.0)


def swapped_kernel(m_ref, hidden_ref, cross_hidden_ref, cross_ref, far_ref, swapped_ref, places_ref, *refs):
    *matrix_refs, out_ref, helped_ref, own_turned_ref, end_turned_ref, end_places_ref, bands_ref = refs
    handed, side = far_ref.shape[0], out_ref.shape[0]
    alone = cross_ref.shape[0] - handed
    out_ref[...] = m_ref[...] + dot(cross_hidden_ref[...], swapped_ref[:handed], ((0,), (0,)))
    helped_ref[...] = (
        dot(swapped_ref[:alone, :side], cross_ref[handed:], ((0,), (0,)))
        + dot(swapped_ref[alone:handed, :side], far_ref[: handed - alone], ((0,), (0,)))
        + dot(swapped_ref[:alone, side:], far_ref[handed - alone :], ((0,), (0,)))
    )
    own_turned_ref[...] = hidden_ref[...].T
    end_turned_ref[...] = swapped_ref[alone:handed, side:].T
    end_places_ref[...] = swapped_ref[handed:].astype(jnp.float32)
    bands_ref[...] = bands_of(out_ref[...], places_ref[...], *matrix_refs)


def helped_kernel(helped_ref, turned_ref, far_ref, places_ref, *refs):
    *matrix_refs, code_ref, bands_ref = refs
    product = helped_ref[...] + dot(turned_ref[...], far_ref[...])
    bands_ref[...] = bands_of(product, places_ref[...], *matrix_refs)
    side = product.shape[0]
    code_ref[:side], code_ref[side:] = coded(product)


def last_rows_kernel(end_ref, m_ref, own_bands_ref, turned_ref, far_ref, places_ref, *refs):
    *matrix_refs, out_ref, bands_ref = refs

    @pl.when(end_ref[0] == 1)
    def _():
        out_ref[...] = m_ref[...]
        bands_ref[...] = own_bands_ref[...]

    @pl.when(end_ref[0] == 0)
    def _():
        out_ref[...] = m_ref[...] + dot(turned_ref[...], far_ref[...])
        bands_ref[...] = bands_of(out_ref[...], places_ref[...], *matrix_refs)


def remove_kernel(m_ref, bands_ref, places_ref, fold_ref, basis_ref, out_ref):
    masks = masks_of(places_ref[...], out_ref.shape[0] // order)
    coefficients = within(spread(bands_ref[...], fold_ref[...]), masks)
    out_ref[...] = m_ref[...] - restored(coefficients, masks, basis_ref)


def add_kernel(x_ref, code_ref, out_ref):
    out_ref[...] = x_ref[...] + decoded(code_ref)


def update_kernel(*refs):
    *part_refs, places_ref, fold_ref, basis_ref, out_ref = refs
    bands = pair_sum([ref[...] for ref in part_refs])
    masks = masks_of(places_ref[...], out_ref.shape[0] // order)
    coefficients = within(spread(bands, fold_ref[...]), masks)
    out_ref[...] = restored(coefficients, masks, basis_ref).astype(out_ref.dtype)


def pair_sum(parts):
    while len(parts) > 1:
        parts = [sum(parts[i + 1 : i + 2], parts[i]) for i in range(0, len(parts), 2)]
    return parts[0]


def call(kernel, out_shapes, *operands):
    spaces = [pltpu.SMEM if x.dtype == jnp.int32 else pltpu.VMEM for x in operands]
    return pl.pallas_call(
        kernel,
        out_shape=out_shapes,
        in_specs=[pl.BlockSpec(memory_space=space) for space in spaces],
        compiler_params=pltpu.CompilerParams(vmem_limit_bytes=16 * 2**20),
        cost_estimate=pl.CostEstimate(flops=4 * 10**8, bytes_accessed=4 * 10**6, transcendentals=0),
    )(*operands)


def spread_sum(x, axis):
    size = lax.axis_size(axis)
    if size & (size - 1):
        return [lax.psum(x, axis)]
    stride, parts = 1, [x]
    while stride < size:
        count = min(4, size // stride)
        x = pair_sum(parts)
        parts = [x] + [
            lax.ppermute(x, axis, [(i, i ^ (stride * k)) for i in range(size)]) for k in range(1, count)
        ]
        stride *= count
    return parts


def product(hidden_rows, grad_rows):
    return dot(hidden_rows, grad_rows, ((0,), (0,)))


def after(x, *others):
    return lax.optimization_barrier((x, *others))[0]


def gathered(hidden, out_grad, carried, places, matrices):
    m = carried + product(hidden, lax.all_gather(out_grad, "tp", axis=0, tiled=True))
    folded = jax.ShapeDtypeStruct((m.shape[0] // steps, m.shape[1] // steps), jnp.float32)
    bands = call(bands_kernel, folded, m, places, *matrices)
    return m, bands, None, spread_sum(bands, "rep"), places, matrices


def lined(hidden, out_grad, carried, places, matrices):
    tok = out_grad.shape[0]
    me = lax.axis_index("tp")
    left = me < 2
    end = (me == 0) | (me == 3)
    cross = jnp.where(left, 2, 1)
    far = jnp.where(left, 3, 0)
    handed = tok * 2 // 3
    alone = tok - handed

    def rows_of(part, start=0, stop=tok):
        return lax.dynamic_slice_in_dim(hidden, part * tok + start, stop - start, 0)

    def send(x, perm):
        return lax.ppermute(x, "tp", perm)

    both_ways = [(0, 1), (1, 0), (2, 3), (3, 2)]
    across = [(1, 2), (2, 1)]
    outward = [(1, 0), (2, 3)]

    cross_grad = send(out_grad, across)
    m = carried + product(rows_of(me), out_grad)
    pair_parts = [send(out_grad[:handed], both_ways), send(out_grad[handed:], both_ways)]
    far_hidden = rows_of(far)
    helped_hidden = jnp.concatenate(
        [
            jnp.concatenate([rows_of(cross, handed), far_hidden[: handed - alone]], axis=0),
            far_hidden[handed - alone :],
        ],
        axis=1,
    )
    place_part = jnp.pad(places.astype(hidden.dtype), ((0, place_rows - places.shape[0]), (0, 0)))
    helped_hidden = jnp.concatenate([helped_hidden, place_part], axis=0)
    cross_hidden = jnp.where(end, rows_of(cross, 0, handed), 0)
    pair_head, helped_hidden, cross_hidden, m = lax.optimization_barrier(
        (pair_parts[0], helped_hidden, cross_hidden, m)
    )
    far_head = send(pair_head, across)
    first = pair_head[:16]
    pair_rest, first = lax.optimization_barrier((pair_parts[1], first))
    far_parts = [far_head, send(pair_rest, across)]
    cross_grad, matrices, places = after((cross_grad, matrices, places), pair_head, m)
    swapped = send(jnp.where(end, helped_hidden, cross_grad[: handed + place_rows]), both_ways)
    far_parts[0], pair_head, pair_rest, cross_grad = lax.optimization_barrier(
        (far_parts[0], pair_head, pair_rest, cross_grad)
    )
    m = m + product(rows_of(me ^ 1, 0, 16), first) + product(rows_of(me ^ 1, 16, handed), pair_head[16:])
    m = m + product(rows_of(me ^ 1, handed), pair_rest)
    m = m + product(rows_of(cross), cross_grad) + product(far_hidden[:handed], far_parts[0])
    m, swapped = lax.optimization_barrier((m, swapped))

    height, width = m.shape[0] // steps, m.shape[1] // steps
    full = jax.ShapeDtypeStruct(m.shape, jnp.float32)
    turned = jax.ShapeDtypeStruct((m.shape[0], alone), hidden.dtype)
    table = jax.ShapeDtypeStruct((place_rows, m.shape[1]), jnp.float32)
    folded = jax.ShapeDtypeStruct((height, width), jnp.float32)
    m, helped, own_turned, end_turned, end_places, own_bands = call(
        swapped_kernel,
        (full, full, turned, turned, table, folded),
        m,
        far_hidden[handed:],
        cross_hidden,
        cross_grad,
        far_parts[0],
        swapped,
        places,
        *matrices,
    )
    far_grad = after(far_parts[1], m)
    code_shape = jax.ShapeDtypeStruct((m.shape[0] + code_rows, m.shape[1]), jnp.int16)
    code, end_bands = call(
        helped_kernel, (code_shape, folded), helped, end_turned, far_grad, end_places, *matrices
    )
    m, end_bands, code = lax.optimization_barrier((m, end_bands, code))
    end_bands = send(end_bands, both_ways)
    flag = end.astype(jnp.int32).reshape(1)
    m, bands = call(
        last_rows_kernel, (full, folded), flag, m, own_bands, own_turned, far_grad, places, *matrices
    )
    bands, code = lax.optimization_barrier((bands, code))
    code = send(code, outward)
    end_bands, bands = lax.optimization_barrier((end_bands, bands))
    bands = bands + jnp.where(end, end_bands, 0.0)
    parts = spread_sum(bands, "rep")
    return m, bands, code, parts, places, matrices


def local(hidden, out_grad, momentum, band_rows, band_start_columns):
    row_count = hidden.shape[1]
    col_count = out_grad.shape[1]
    one_hot = jnp.asarray(np.kron(np.eye(col_count // order), np.ones((1, order))), jnp.float32)
    matrices = (jnp.asarray(fold_matrix(col_count)), jnp.asarray(diagonal_blocks(row_count, col_count)))
    places = jnp.concatenate([band_rows, band_start_columns], axis=0).astype(jnp.float32)
    places = dot(places, one_hot)
    fits = out_grad.shape[0] % 384 == 0 and 2 * row_count == col_count and places.shape[0] <= place_rows
    form = lined if fits and lax.axis_size("tp") == 4 else gathered
    m, bands, code, band_parts, places, matrices = form(
        hidden, out_grad, decay_rate * momentum[0], places, matrices
    )
    full = jax.ShapeDtypeStruct(m.shape, jnp.float32)
    momentum_out = call(remove_kernel, full, m, bands, places, *matrices)
    if code is not None:
        momentum_out = call(add_kernel, full, momentum_out, code)
    *band_parts, momentum_out = lax.optimization_barrier((*band_parts, momentum_out))
    update = call(update_kernel, jax.ShapeDtypeStruct(m.shape, jnp.bfloat16), *band_parts, places, *matrices)
    return (momentum_out[None], update)


def solution(mesh):
    return jax.shard_map(
        local,
        mesh=mesh,
        in_specs=(
            P("rep", "tp"),
            P(("rep", "tp"), None),
            P("rep", "tp", None),
            P("tp", None),
            P("tp", None),
        ),
        out_specs=(P("rep", "tp", None), P("tp", None)),
        check_vma=False,
    )
```

```python
import jax
import jax.numpy as jnp
import numpy as np
from jax import lax
from jax.experimental import pallas as pl
from jax.experimental.pallas import tpu as pltpu
from jax.sharding import PartitionSpec as P

decay_rate = 0.9
order = 64
band = 16
steps = order // band
place_rows = 16
code_rows = 16


def basis_matrix():
    frequency = np.arange(order, dtype=np.float64)[:, None]
    sample_pos = np.arange(order, dtype=np.float64)[None, :]
    norm_scale = np.where(frequency == 0, np.sqrt(1.0 / order), np.sqrt(2.0 / order))
    return norm_scale * np.cos(np.pi * (sample_pos + 0.5) * frequency / order)


def diagonal_blocks(*widths):
    count = next(c for c in (4, 2, 1) if all(width % (c * order) == 0 for width in widths))
    return np.kron(np.eye(count), basis_matrix()).astype(np.float32)


def fold_matrix(width):
    return np.kron(np.eye(width // order), np.kron(np.ones((steps, 1)), np.eye(band))).astype(jnp.bfloat16)


def split2(x):
    high = x.astype(jnp.bfloat16)
    return high, (x - high.astype(jnp.float32)).astype(jnp.bfloat16)


def split3(x):
    high, low = split2(x)
    rest = x - high.astype(jnp.float32) - low.astype(jnp.float32)
    return high, low, rest.astype(jnp.bfloat16)


def dot(a, b, dims=((1,), (0,))):
    return lax.dot_general(a, b, (dims, ((), ())), preferred_element_type=jnp.float32)


def dot3(a, b, dims=((1,), (0,))):
    (a_high, a_low), (b_high, b_low) = a, b
    left = jnp.concatenate([a_high, a_low, a_high], axis=dims[0][0])
    right = jnp.concatenate([b_high, b_high, b_low], axis=dims[1][0])
    return dot(left, right, dims)


def on_rows(basis_ref, x, transposed):
    basis, side = split2(basis_ref[...]), basis_ref.shape[0]
    dims = ((0,), (0,)) if transposed else ((1,), (0,))
    parts = [dot3(basis, split2(x[i : i + side]), dims) for i in range(0, x.shape[0], side)]
    return parts[0] if len(parts) == 1 else jnp.concatenate(parts, axis=0)


def on_columns(basis_ref, x, transposed):
    basis, side = split2(basis_ref[...]), basis_ref.shape[0]
    dims = ((1,), (0,)) if transposed else ((1,), (1,))
    parts = [dot3(split2(x[:, i : i + side]), basis, dims) for i in range(0, x.shape[1], side)]
    return parts[0] if len(parts) == 1 else jnp.concatenate(parts, axis=1)


def masks_of(places, count):
    width = places.shape[1]
    column = lax.rem(lax.broadcasted_iota(jnp.int32, (band, width), 1), order).astype(jnp.float32)
    masks = []
    for row in range(count):
        start = places[count + row : count + row + 1, :]
        masks.append((places[row : row + 1, :], (column >= start) & (column < start + band)))
    return masks


def rows_taken(x, masks):
    pieces = []
    for row, (at, _) in enumerate(masks):
        taken = jnp.zeros((band, x.shape[1]), jnp.float32)
        for step in range(steps):
            start = row * order + step * band
            taken = jnp.where(at == step * band, x[start : start + band], taken)
        pieces.append(taken)
    return jnp.concatenate(pieces, axis=0)


def selected(x, masks, basis_ref):
    taken = rows_taken(on_rows(basis_ref, x, False), masks)
    return within(on_columns(basis_ref, taken, False), masks)


def within(x, masks):
    return jnp.concatenate(
        [jnp.where(inside, x[i * band : (i + 1) * band], 0.0) for i, (_, inside) in enumerate(masks)], axis=0
    )


def restored(x, masks, basis_ref):
    by_columns = on_columns(basis_ref, x, True)
    pieces = []
    for row, (at, _) in enumerate(masks):
        part = by_columns[row * band : (row + 1) * band]
        pieces += [jnp.where(at == step * band, part, 0.0) for step in range(steps)]
    return on_rows(basis_ref, jnp.concatenate(pieces, axis=0), True)


def bands_of(x, places, fold_ref, basis_ref):
    return folded(selected(x, masks_of(places, x.shape[0] // order), basis_ref), fold_ref[...])


def folded(x, fold):
    return dot(jnp.concatenate(split3(x), axis=1), jnp.concatenate([fold] * 3, axis=0))


def spread(x, fold):
    return dot(jnp.concatenate(split3(x), axis=1), jnp.concatenate([fold] * 3, axis=1), ((1,), (1,)))


def bands_kernel(m_ref, places_ref, *refs):
    *matrix_refs, bands_ref = refs
    bands_ref[...] = bands_of(m_ref[...], places_ref[...], *matrix_refs)


def coded(x):
    top = jnp.max(jnp.abs(x), axis=0, keepdims=True)
    exponent = jnp.ceil(jnp.log2(jnp.maximum(top, 1e-30)) + 0.01)
    scaled = x * jnp.exp2(15.0 - exponent)
    values = jnp.clip(jnp.round(scaled), -32767.0, 32767.0).astype(jnp.int32).astype(jnp.int16)
    row = jnp.broadcast_to(exponent, (code_rows, x.shape[1])).astype(jnp.int32).astype(jnp.int16)
    return values, row


def decoded(ref):
    values = ref[: ref.shape[0] - code_rows].astype(jnp.int32).astype(jnp.float32)
    exponents = ref[ref.shape[0] - code_rows :].astype(jnp.int32).astype(jnp.float32)
    return values * jnp.exp2(exponents[:1] - 15.0)


def swapped_kernel(m_ref, hidden_ref, cross_hidden_ref, cross_ref, far_ref, swapped_ref, places_ref, *refs):
    *matrix_refs, out_ref, helped_ref, own_turned_ref, end_turned_ref, end_places_ref, bands_ref = refs
    handed, side = far_ref.shape[0], out_ref.shape[0]
    alone = cross_ref.shape[0] - handed
    out_ref[...] = m_ref[...] + dot(cross_hidden_ref[...], swapped_ref[:handed], ((0,), (0,)))
    helped_ref[...] = (
        dot(swapped_ref[:alone, :side], cross_ref[handed:], ((0,), (0,)))
        + dot(swapped_ref[alone:handed, :side], far_ref[: handed - alone], ((0,), (0,)))
        + dot(swapped_ref[:alone, side:], far_ref[handed - alone :], ((0,), (0,)))
    )
    own_turned_ref[...] = hidden_ref[...].T
    end_turned_ref[...] = swapped_ref[alone:handed, side:].T
    end_places_ref[...] = swapped_ref[handed:].astype(jnp.float32)
    bands_ref[...] = bands_of(out_ref[...], places_ref[...], *matrix_refs)


def helped_kernel(helped_ref, turned_ref, far_ref, places_ref, *refs):
    *matrix_refs, code_ref, bands_ref = refs
    product = helped_ref[...] + dot(turned_ref[...], far_ref[...])
    bands_ref[...] = bands_of(product, places_ref[...], *matrix_refs)
    side = product.shape[0]
    code_ref[:side], code_ref[side:] = coded(product)


def last_rows_kernel(end_ref, m_ref, own_bands_ref, turned_ref, far_ref, places_ref, *refs):
    *matrix_refs, out_ref, bands_ref = refs

    @pl.when(end_ref[0] == 1)
    def _():
        out_ref[...] = m_ref[...]
        bands_ref[...] = own_bands_ref[...]

    @pl.when(end_ref[0] == 0)
    def _():
        out_ref[...] = m_ref[...] + dot(turned_ref[...], far_ref[...])
        bands_ref[...] = bands_of(out_ref[...], places_ref[...], *matrix_refs)


def remove_kernel(m_ref, bands_ref, places_ref, fold_ref, basis_ref, out_ref):
    masks = masks_of(places_ref[...], out_ref.shape[0] // order)
    coefficients = within(spread(bands_ref[...], fold_ref[...]), masks)
    out_ref[...] = m_ref[...] - restored(coefficients, masks, basis_ref)


def add_kernel(x_ref, code_ref, out_ref):
    out_ref[...] = x_ref[...] + decoded(code_ref)


def update_kernel(*refs):
    *part_refs, places_ref, fold_ref, basis_ref, out_ref = refs
    bands = pair_sum([ref[...] for ref in part_refs])
    masks = masks_of(places_ref[...], out_ref.shape[0] // order)
    coefficients = within(spread(bands, fold_ref[...]), masks)
    out_ref[...] = restored(coefficients, masks, basis_ref).astype(out_ref.dtype)


def pair_sum(parts):
    while len(parts) > 1:
        parts = [sum(parts[i + 1 : i + 2], parts[i]) for i in range(0, len(parts), 2)]
    return parts[0]


def call(kernel, out_shapes, *operands):
    spaces = [pltpu.SMEM if x.dtype == jnp.int32 else pltpu.VMEM for x in operands]
    return pl.pallas_call(
        kernel,
        out_shape=out_shapes,
        in_specs=[pl.BlockSpec(memory_space=space) for space in spaces],
        compiler_params=pltpu.CompilerParams(vmem_limit_bytes=16 * 2**20),
        cost_estimate=pl.CostEstimate(flops=4 * 10**8, bytes_accessed=4 * 10**6, transcendentals=0),
    )(*operands)


def spread_sum(x, axis):
    size = lax.axis_size(axis)
    if size & (size - 1):
        return [lax.psum(x, axis)]
    stride, parts = 1, [x]
    while stride < size:
        count = min(4, size // stride)
        x = pair_sum(parts)
        parts = [x] + [
            lax.ppermute(x, axis, [(i, i ^ (stride * k)) for i in range(size)]) for k in range(1, count)
        ]
        stride *= count
    return parts


def product(hidden_rows, grad_rows):
    return dot(hidden_rows, grad_rows, ((0,), (0,)))


def after(x, *others):
    return lax.optimization_barrier((x, *others))[0]


def gathered(hidden, out_grad, carried, places, matrices):
    m = carried + product(hidden, lax.all_gather(out_grad, "tp", axis=0, tiled=True))
    folded = jax.ShapeDtypeStruct((m.shape[0] // steps, m.shape[1] // steps), jnp.float32)
    bands = call(bands_kernel, folded, m, places, *matrices)
    return m, bands, None, spread_sum(bands, "rep"), places, matrices


def lined(hidden, out_grad, carried, places, matrices):
    tok = out_grad.shape[0]
    me = lax.axis_index("tp")
    left = me < 2
    end = (me == 0) | (me == 3)
    cross = jnp.where(left, 2, 1)
    far = jnp.where(left, 3, 0)
    handed = tok * 2 // 3
    alone = tok - handed

    def rows_of(part, start=0, stop=tok):
        return lax.dynamic_slice_in_dim(hidden, part * tok + start, stop - start, 0)

    def send(x, perm):
        return lax.ppermute(x, "tp", perm)

    both_ways = [(0, 1), (1, 0), (2, 3), (3, 2)]
    across = [(1, 2), (2, 1)]
    outward = [(1, 0), (2, 3)]

    cross_grad = send(out_grad, across)
    m = carried + product(rows_of(me), out_grad)
    pair_parts = [send(out_grad[:handed], both_ways), send(out_grad[handed:], both_ways)]
    far_hidden = rows_of(far)
    helped_hidden = jnp.concatenate(
        [
            jnp.concatenate([rows_of(cross, handed), far_hidden[: handed - alone]], axis=0),
            far_hidden[handed - alone :],
        ],
        axis=1,
    )
    place_part = jnp.pad(places.astype(hidden.dtype), ((0, place_rows - places.shape[0]), (0, 0)))
    helped_hidden = jnp.concatenate([helped_hidden, place_part], axis=0)
    cross_hidden = jnp.where(end, rows_of(cross, 0, handed), 0)
    pair_head, helped_hidden, cross_hidden, m = lax.optimization_barrier(
        (pair_parts[0], helped_hidden, cross_hidden, m)
    )
    far_head = send(pair_head, across)
    m = m + product(rows_of(me ^ 1, 0, handed), pair_head)
    pair_rest, m = lax.optimization_barrier((pair_parts[1], m))
    far_parts = [far_head, send(pair_rest, across)]
    cross_grad, matrices, places = after((cross_grad, matrices, places), pair_head, m)
    swapped = send(jnp.where(end, helped_hidden, cross_grad[: handed + place_rows]), both_ways)
    far_parts[0], pair_rest, cross_grad = lax.optimization_barrier((far_parts[0], pair_rest, cross_grad))
    m = m + product(rows_of(me ^ 1, handed), pair_rest)
    m = m + product(rows_of(cross), cross_grad) + product(far_hidden[:handed], far_parts[0])
    m, swapped = lax.optimization_barrier((m, swapped))

    height, width = m.shape[0] // steps, m.shape[1] // steps
    full = jax.ShapeDtypeStruct(m.shape, jnp.float32)
    turned = jax.ShapeDtypeStruct((m.shape[0], alone), hidden.dtype)
    table = jax.ShapeDtypeStruct((place_rows, m.shape[1]), jnp.float32)
    folded = jax.ShapeDtypeStruct((height, width), jnp.float32)
    m, helped, own_turned, end_turned, end_places, own_bands = call(
        swapped_kernel,
        (full, full, turned, turned, table, folded),
        m,
        far_hidden[handed:],
        cross_hidden,
        cross_grad,
        far_parts[0],
        swapped,
        places,
        *matrices,
    )
    far_grad = after(far_parts[1], m)
    code_shape = jax.ShapeDtypeStruct((m.shape[0] + code_rows, m.shape[1]), jnp.int16)
    code, end_bands = call(
        helped_kernel, (code_shape, folded), helped, end_turned, far_grad, end_places, *matrices
    )
    m, end_bands, code = lax.optimization_barrier((m, end_bands, code))
    end_bands = send(end_bands, both_ways)
    flag = end.astype(jnp.int32).reshape(1)
    m, bands = call(
        last_rows_kernel, (full, folded), flag, m, own_bands, own_turned, far_grad, places, *matrices
    )
    bands, code = lax.optimization_barrier((bands, code))
    code = send(code, outward)
    end_bands, bands = lax.optimization_barrier((end_bands, bands))
    bands = bands + jnp.where(end, end_bands, 0.0)
    parts = spread_sum(bands, "rep")
    return m, bands, code, parts, places, matrices


def local(hidden, out_grad, momentum, band_rows, band_start_columns):
    row_count = hidden.shape[1]
    col_count = out_grad.shape[1]
    one_hot = jnp.asarray(np.kron(np.eye(col_count // order), np.ones((1, order))), jnp.float32)
    matrices = (jnp.asarray(fold_matrix(col_count)), jnp.asarray(diagonal_blocks(row_count, col_count)))
    places = jnp.concatenate([band_rows, band_start_columns], axis=0).astype(jnp.float32)
    places = dot(places, one_hot)
    fits = out_grad.shape[0] % 384 == 0 and 2 * row_count == col_count and places.shape[0] <= place_rows
    form = lined if fits and lax.axis_size("tp") == 4 else gathered
    m, bands, code, band_parts, places, matrices = form(
        hidden, out_grad, decay_rate * momentum[0], places, matrices
    )
    full = jax.ShapeDtypeStruct(m.shape, jnp.float32)
    momentum_out = call(remove_kernel, full, m, bands, places, *matrices)
    if code is not None:
        momentum_out = call(add_kernel, full, momentum_out, code)
    *band_parts, momentum_out = lax.optimization_barrier((*band_parts, momentum_out))
    update = call(update_kernel, jax.ShapeDtypeStruct(m.shape, jnp.bfloat16), *band_parts, places, *matrices)
    return (momentum_out[None], update)


def solution(mesh):
    return jax.shard_map(
        local,
        mesh=mesh,
        in_specs=(
            P("rep", "tp"),
            P(("rep", "tp"), None),
            P("rep", "tp", None),
            P("tp", None),
            P("tp", None),
        ),
        out_specs=(P("rep", "tp", None), P("tp", None)),
        check_vma=False,
    )
```

```python
import jax
import jax.numpy as jnp
import numpy as np
from jax import lax
from jax.experimental import pallas as pl
from jax.experimental.pallas import tpu as pltpu
from jax.sharding import PartitionSpec as P

decay_rate = 0.9
order = 64
band = 16
steps = order // band
place_rows = 16
code_rows = 16


def basis_matrix():
    frequency = np.arange(order, dtype=np.float64)[:, None]
    sample_pos = np.arange(order, dtype=np.float64)[None, :]
    norm_scale = np.where(frequency == 0, np.sqrt(1.0 / order), np.sqrt(2.0 / order))
    return norm_scale * np.cos(np.pi * (sample_pos + 0.5) * frequency / order)


def diagonal_blocks(*widths):
    count = next(c for c in (4, 2, 1) if all(width % (c * order) == 0 for width in widths))
    return np.kron(np.eye(count), basis_matrix()).astype(np.float32)


def fold_matrix(width):
    return np.kron(np.eye(width // order), np.kron(np.ones((steps, 1)), np.eye(band))).astype(jnp.bfloat16)


def split2(x):
    high = x.astype(jnp.bfloat16)
    return high, (x - high.astype(jnp.float32)).astype(jnp.bfloat16)


def split3(x):
    high, low = split2(x)
    rest = x - high.astype(jnp.float32) - low.astype(jnp.float32)
    return high, low, rest.astype(jnp.bfloat16)


def dot(a, b, dims=((1,), (0,))):
    return lax.dot_general(a, b, (dims, ((), ())), preferred_element_type=jnp.float32)


def dot3(a, b, dims=((1,), (0,))):
    (a_high, a_low), (b_high, b_low) = a, b
    left = jnp.concatenate([a_high, a_low, a_high], axis=dims[0][0])
    right = jnp.concatenate([b_high, b_high, b_low], axis=dims[1][0])
    return dot(left, right, dims)


def on_rows(basis_ref, x, transposed):
    basis, side = split2(basis_ref[...]), basis_ref.shape[0]
    dims = ((0,), (0,)) if transposed else ((1,), (0,))
    parts = [dot3(basis, split2(x[i : i + side]), dims) for i in range(0, x.shape[0], side)]
    return parts[0] if len(parts) == 1 else jnp.concatenate(parts, axis=0)


def on_columns(basis_ref, x, transposed):
    basis, side = split2(basis_ref[...]), basis_ref.shape[0]
    dims = ((1,), (0,)) if transposed else ((1,), (1,))
    parts = [dot3(split2(x[:, i : i + side]), basis, dims) for i in range(0, x.shape[1], side)]
    return parts[0] if len(parts) == 1 else jnp.concatenate(parts, axis=1)


def masks_of(places, count):
    width = places.shape[1]
    column = lax.rem(lax.broadcasted_iota(jnp.int32, (band, width), 1), order).astype(jnp.float32)
    masks = []
    for row in range(count):
        start = places[count + row : count + row + 1, :]
        masks.append((places[row : row + 1, :], (column >= start) & (column < start + band)))
    return masks


def rows_taken(x, masks):
    pieces = []
    for row, (at, _) in enumerate(masks):
        taken = jnp.zeros((band, x.shape[1]), jnp.float32)
        for step in range(steps):
            start = row * order + step * band
            taken = jnp.where(at == step * band, x[start : start + band], taken)
        pieces.append(taken)
    return jnp.concatenate(pieces, axis=0)


def selected(x, masks, basis_ref):
    taken = rows_taken(on_rows(basis_ref, x, False), masks)
    return within(on_columns(basis_ref, taken, False), masks)


def within(x, masks):
    return jnp.concatenate(
        [jnp.where(inside, x[i * band : (i + 1) * band], 0.0) for i, (_, inside) in enumerate(masks)], axis=0
    )


def restored(x, masks, basis_ref):
    by_columns = on_columns(basis_ref, x, True)
    pieces = []
    for row, (at, _) in enumerate(masks):
        part = by_columns[row * band : (row + 1) * band]
        pieces += [jnp.where(at == step * band, part, 0.0) for step in range(steps)]
    return on_rows(basis_ref, jnp.concatenate(pieces, axis=0), True)


def bands_of(x, places, fold_ref, basis_ref):
    return folded(selected(x, masks_of(places, x.shape[0] // order), basis_ref), fold_ref[...])


def folded(x, fold):
    return dot(jnp.concatenate(split3(x), axis=1), jnp.concatenate([fold] * 3, axis=0))


def spread(x, fold):
    return dot(jnp.concatenate(split3(x), axis=1), jnp.concatenate([fold] * 3, axis=1), ((1,), (1,)))


def bands_kernel(m_ref, places_ref, *refs):
    *matrix_refs, bands_ref = refs
    bands_ref[...] = bands_of(m_ref[...], places_ref[...], *matrix_refs)


def coded(x):
    top = jnp.max(jnp.abs(x), axis=0, keepdims=True)
    exponent = jnp.ceil(jnp.log2(jnp.maximum(top, 1e-30)) + 0.01)
    scaled = x * jnp.exp2(15.0 - exponent)
    values = jnp.clip(jnp.round(scaled), -32767.0, 32767.0).astype(jnp.int32).astype(jnp.int16)
    row = jnp.broadcast_to(exponent, (code_rows, x.shape[1])).astype(jnp.int32).astype(jnp.int16)
    return values, row


def decoded(ref):
    values = ref[: ref.shape[0] - code_rows].astype(jnp.int32).astype(jnp.float32)
    exponents = ref[ref.shape[0] - code_rows :].astype(jnp.int32).astype(jnp.float32)
    return values * jnp.exp2(exponents[:1] - 15.0)


def swapped_kernel(m_ref, hidden_ref, cross_hidden_ref, cross_ref, far_ref, swapped_ref, places_ref, *refs):
    *matrix_refs, out_ref, helped_ref, own_turned_ref, end_turned_ref, end_places_ref, bands_ref = refs
    handed, side = far_ref.shape[0], out_ref.shape[0]
    alone = cross_ref.shape[0] - handed
    out_ref[...] = m_ref[...] + dot(cross_hidden_ref[...], swapped_ref[:handed], ((0,), (0,)))
    helped_ref[...] = (
        dot(swapped_ref[:alone, :side], cross_ref[handed:], ((0,), (0,)))
        + dot(swapped_ref[alone:handed, :side], far_ref[: handed - alone], ((0,), (0,)))
        + dot(swapped_ref[:alone, side:], far_ref[handed - alone :], ((0,), (0,)))
    )
    own_turned_ref[...] = hidden_ref[...].T
    end_turned_ref[...] = swapped_ref[alone:handed, side:].T
    end_places_ref[...] = swapped_ref[handed:].astype(jnp.float32)
    bands_ref[...] = bands_of(out_ref[...], places_ref[...], *matrix_refs)


def helped_kernel(helped_ref, turned_ref, far_ref, places_ref, *refs):
    *matrix_refs, code_ref, bands_ref = refs
    product = helped_ref[...] + dot(turned_ref[...], far_ref[...])
    bands_ref[...] = bands_of(product, places_ref[...], *matrix_refs)
    side = product.shape[0]
    code_ref[:side], code_ref[side:] = coded(product)


def last_rows_kernel(end_ref, m_ref, own_bands_ref, turned_ref, far_ref, places_ref, *refs):
    *matrix_refs, out_ref, bands_ref = refs

    @pl.when(end_ref[0] == 1)
    def _():
        out_ref[...] = m_ref[...]
        bands_ref[...] = own_bands_ref[...]

    @pl.when(end_ref[0] == 0)
    def _():
        out_ref[...] = m_ref[...] + dot(turned_ref[...], far_ref[...])
        bands_ref[...] = bands_of(out_ref[...], places_ref[...], *matrix_refs)


def remove_kernel(m_ref, bands_ref, places_ref, fold_ref, basis_ref, out_ref):
    masks = masks_of(places_ref[...], out_ref.shape[0] // order)
    coefficients = within(spread(bands_ref[...], fold_ref[...]), masks)
    out_ref[...] = m_ref[...] - restored(coefficients, masks, basis_ref)


def add_kernel(x_ref, code_ref, out_ref):
    out_ref[...] = x_ref[...] + decoded(code_ref)


def update_kernel(*refs):
    *part_refs, places_ref, fold_ref, basis_ref, out_ref = refs
    bands = pair_sum([ref[...] for ref in part_refs])
    masks = masks_of(places_ref[...], out_ref.shape[0] // order)
    coefficients = within(spread(bands, fold_ref[...]), masks)
    out_ref[...] = restored(coefficients, masks, basis_ref).astype(out_ref.dtype)


def pair_sum(parts):
    while len(parts) > 1:
        parts = [sum(parts[i + 1 : i + 2], parts[i]) for i in range(0, len(parts), 2)]
    return parts[0]


def call(kernel, out_shapes, *operands):
    spaces = [pltpu.SMEM if x.dtype == jnp.int32 else pltpu.VMEM for x in operands]
    return pl.pallas_call(
        kernel,
        out_shape=out_shapes,
        in_specs=[pl.BlockSpec(memory_space=space) for space in spaces],
        compiler_params=pltpu.CompilerParams(vmem_limit_bytes=16 * 2**20),
        cost_estimate=pl.CostEstimate(flops=4 * 10**8, bytes_accessed=4 * 10**6, transcendentals=0),
    )(*operands)


def spread_sum(x, axis):
    size = lax.axis_size(axis)
    if size & (size - 1):
        return [lax.psum(x, axis)]
    stride, parts = 1, [x]
    while stride < size:
        count = min(4, size // stride)
        x = pair_sum(parts)
        parts = [x] + [
            lax.ppermute(x, axis, [(i, i ^ (stride * k)) for i in range(size)]) for k in range(1, count)
        ]
        stride *= count
    return parts


def product(hidden_rows, grad_rows):
    return dot(hidden_rows, grad_rows, ((0,), (0,)))


def after(x, *others):
    return lax.optimization_barrier((x, *others))[0]


def gathered(hidden, out_grad, carried, places, matrices):
    m = carried + product(hidden, lax.all_gather(out_grad, "tp", axis=0, tiled=True))
    folded = jax.ShapeDtypeStruct((m.shape[0] // steps, m.shape[1] // steps), jnp.float32)
    bands = call(bands_kernel, folded, m, places, *matrices)
    return m, bands, None, spread_sum(bands, "rep"), places, matrices


def lined(hidden, out_grad, carried, places, matrices):
    tok = out_grad.shape[0]
    me = lax.axis_index("tp")
    left = me < 2
    end = (me == 0) | (me == 3)
    cross = jnp.where(left, 2, 1)
    far = jnp.where(left, 3, 0)
    handed = tok * 2 // 3
    alone = tok - handed

    def rows_of(part, start=0, stop=tok):
        return lax.dynamic_slice_in_dim(hidden, part * tok + start, stop - start, 0)

    def send(x, perm):
        return lax.ppermute(x, "tp", perm)

    both_ways = [(0, 1), (1, 0), (2, 3), (3, 2)]
    across = [(1, 2), (2, 1)]
    outward = [(1, 0), (2, 3)]

    cross_grad = send(out_grad, across)
    m = carried + product(rows_of(me), out_grad)
    pair_parts = [send(out_grad[:handed], both_ways), send(out_grad[handed:], both_ways)]
    far_hidden = rows_of(far)
    helped_hidden = jnp.concatenate(
        [
            jnp.concatenate([rows_of(cross, handed), far_hidden[: handed - alone]], axis=0),
            far_hidden[handed - alone :],
        ],
        axis=1,
    )
    place_part = jnp.pad(places.astype(hidden.dtype), ((0, place_rows - places.shape[0]), (0, 0)))
    helped_hidden = jnp.concatenate([helped_hidden, place_part], axis=0)
    cross_hidden = jnp.where(end, rows_of(cross, 0, handed), 0)
    pair_head, helped_hidden, cross_hidden, m = lax.optimization_barrier(
        (pair_parts[0], helped_hidden, cross_hidden, m)
    )
    far_head = send(pair_head, across)
    m = m + product(rows_of(me ^ 1, 0, handed), pair_head)
    cross_grad, matrices, places = after((cross_grad, matrices, places), pair_head, m)
    to_swap = jnp.where(end, helped_hidden, cross_grad[: handed + place_rows])
    swapped = send(to_swap, both_ways)
    pair_rest, m, to_swap = lax.optimization_barrier((pair_parts[1], m, to_swap))
    far_parts = [far_head, send(pair_rest, across)]
    far_parts[0], pair_rest, cross_grad = lax.optimization_barrier((far_parts[0], pair_rest, cross_grad))
    m = m + product(rows_of(me ^ 1, handed), pair_rest)
    m = m + product(rows_of(cross), cross_grad) + product(far_hidden[:handed], far_parts[0])
    m, swapped = lax.optimization_barrier((m, swapped))

    height, width = m.shape[0] // steps, m.shape[1] // steps
    full = jax.ShapeDtypeStruct(m.shape, jnp.float32)
    turned = jax.ShapeDtypeStruct((m.shape[0], alone), hidden.dtype)
    table = jax.ShapeDtypeStruct((place_rows, m.shape[1]), jnp.float32)
    folded = jax.ShapeDtypeStruct((height, width), jnp.float32)
    m, helped, own_turned, end_turned, end_places, own_bands = call(
        swapped_kernel,
        (full, full, turned, turned, table, folded),
        m,
        far_hidden[handed:],
        cross_hidden,
        cross_grad,
        far_parts[0],
        swapped,
        places,
        *matrices,
    )
    far_grad = after(far_parts[1], m)
    code_shape = jax.ShapeDtypeStruct((m.shape[0] + code_rows, m.shape[1]), jnp.int16)
    code, end_bands = call(
        helped_kernel, (code_shape, folded), helped, end_turned, far_grad, end_places, *matrices
    )
    m, end_bands, code = lax.optimization_barrier((m, end_bands, code))
    end_bands = send(end_bands, both_ways)
    flag = end.astype(jnp.int32).reshape(1)
    m, bands = call(
        last_rows_kernel, (full, folded), flag, m, own_bands, own_turned, far_grad, places, *matrices
    )
    bands, code = lax.optimization_barrier((bands, code))
    code = send(code, outward)
    end_bands, bands = lax.optimization_barrier((end_bands, bands))
    bands = bands + jnp.where(end, end_bands, 0.0)
    parts = spread_sum(bands, "rep")
    return m, bands, code, parts, places, matrices


def local(hidden, out_grad, momentum, band_rows, band_start_columns):
    row_count = hidden.shape[1]
    col_count = out_grad.shape[1]
    one_hot = jnp.asarray(np.kron(np.eye(col_count // order), np.ones((1, order))), jnp.float32)
    matrices = (jnp.asarray(fold_matrix(col_count)), jnp.asarray(diagonal_blocks(row_count, col_count)))
    places = jnp.concatenate([band_rows, band_start_columns], axis=0).astype(jnp.float32)
    places = dot(places, one_hot)
    fits = out_grad.shape[0] % 384 == 0 and 2 * row_count == col_count and places.shape[0] <= place_rows
    form = lined if fits and lax.axis_size("tp") == 4 else gathered
    m, bands, code, band_parts, places, matrices = form(
        hidden, out_grad, decay_rate * momentum[0], places, matrices
    )
    full = jax.ShapeDtypeStruct(m.shape, jnp.float32)
    momentum_out = call(remove_kernel, full, m, bands, places, *matrices)
    if code is not None:
        momentum_out = call(add_kernel, full, momentum_out, code)
    *band_parts, momentum_out = lax.optimization_barrier((*band_parts, momentum_out))
    update = call(update_kernel, jax.ShapeDtypeStruct(m.shape, jnp.bfloat16), *band_parts, places, *matrices)
    return (momentum_out[None], update)


def solution(mesh):
    return jax.shard_map(
        local,
        mesh=mesh,
        in_specs=(
            P("rep", "tp"),
            P(("rep", "tp"), None),
            P("rep", "tp", None),
            P("tp", None),
            P("tp", None),
        ),
        out_specs=(P("rep", "tp", None), P("tp", None)),
        check_vma=False,
    )
```

```python
import jax
import jax.numpy as jnp
import numpy as np
from jax import lax
from jax.experimental import pallas as pl
from jax.experimental.pallas import tpu as pltpu
from jax.sharding import PartitionSpec as P

decay_rate = 0.9
order = 64
band = 16
steps = order // band
place_rows = 16
code_rows = 16


def basis_matrix():
    frequency = np.arange(order, dtype=np.float64)[:, None]
    sample_pos = np.arange(order, dtype=np.float64)[None, :]
    norm_scale = np.where(frequency == 0, np.sqrt(1.0 / order), np.sqrt(2.0 / order))
    return norm_scale * np.cos(np.pi * (sample_pos + 0.5) * frequency / order)


def diagonal_blocks(*widths):
    count = next(c for c in (4, 2, 1) if all(width % (c * order) == 0 for width in widths))
    return np.kron(np.eye(count), basis_matrix()).astype(np.float32)


def fold_matrix(width):
    return np.kron(np.eye(width // order), np.kron(np.ones((steps, 1)), np.eye(band))).astype(jnp.bfloat16)


def split2(x):
    high = x.astype(jnp.bfloat16)
    return high, (x - high.astype(jnp.float32)).astype(jnp.bfloat16)


def split3(x):
    high, low = split2(x)
    rest = x - high.astype(jnp.float32) - low.astype(jnp.float32)
    return high, low, rest.astype(jnp.bfloat16)


def dot(a, b, dims=((1,), (0,))):
    return lax.dot_general(a, b, (dims, ((), ())), preferred_element_type=jnp.float32)


def dot3(a, b, dims=((1,), (0,))):
    (a_high, a_low), (b_high, b_low) = a, b
    left = jnp.concatenate([a_high, a_low, a_high], axis=dims[0][0])
    right = jnp.concatenate([b_high, b_high, b_low], axis=dims[1][0])
    return dot(left, right, dims)


def on_rows(basis_ref, x, transposed):
    basis, side = split2(basis_ref[...]), basis_ref.shape[0]
    dims = ((0,), (0,)) if transposed else ((1,), (0,))
    parts = [dot3(basis, split2(x[i : i + side]), dims) for i in range(0, x.shape[0], side)]
    return parts[0] if len(parts) == 1 else jnp.concatenate(parts, axis=0)


def on_columns(basis_ref, x, transposed):
    basis, side = split2(basis_ref[...]), basis_ref.shape[0]
    dims = ((1,), (0,)) if transposed else ((1,), (1,))
    parts = [dot3(split2(x[:, i : i + side]), basis, dims) for i in range(0, x.shape[1], side)]
    return parts[0] if len(parts) == 1 else jnp.concatenate(parts, axis=1)


def masks_of(places, count):
    width = places.shape[1]
    column = lax.rem(lax.broadcasted_iota(jnp.int32, (band, width), 1), order).astype(jnp.float32)
    masks = []
    for row in range(count):
        start = places[count + row : count + row + 1, :]
        masks.append((places[row : row + 1, :], (column >= start) & (column < start + band)))
    return masks


def rows_taken(x, masks):
    pieces = []
    for row, (at, _) in enumerate(masks):
        taken = jnp.zeros((band, x.shape[1]), jnp.float32)
        for step in range(steps):
            start = row * order + step * band
            taken = jnp.where(at == step * band, x[start : start + band], taken)
        pieces.append(taken)
    return jnp.concatenate(pieces, axis=0)


def selected(x, masks, basis_ref):
    taken = rows_taken(on_rows(basis_ref, x, False), masks)
    return within(on_columns(basis_ref, taken, False), masks)


def within(x, masks):
    return jnp.concatenate(
        [jnp.where(inside, x[i * band : (i + 1) * band], 0.0) for i, (_, inside) in enumerate(masks)], axis=0
    )


def restored(x, masks, basis_ref):
    by_columns = on_columns(basis_ref, x, True)
    pieces = []
    for row, (at, _) in enumerate(masks):
        part = by_columns[row * band : (row + 1) * band]
        pieces += [jnp.where(at == step * band, part, 0.0) for step in range(steps)]
    return on_rows(basis_ref, jnp.concatenate(pieces, axis=0), True)


def bands_of(x, places, fold_ref, basis_ref):
    return folded(selected(x, masks_of(places, x.shape[0] // order), basis_ref), fold_ref[...])


def folded(x, fold):
    return dot(jnp.concatenate(split3(x), axis=1), jnp.concatenate([fold] * 3, axis=0))


def spread(x, fold):
    return dot(jnp.concatenate(split3(x), axis=1), jnp.concatenate([fold] * 3, axis=1), ((1,), (1,)))


def bands_kernel(m_ref, places_ref, *refs):
    *matrix_refs, bands_ref = refs
    bands_ref[...] = bands_of(m_ref[...], places_ref[...], *matrix_refs)


def coded(x):
    top = jnp.max(jnp.abs(x), axis=0, keepdims=True)
    exponent = jnp.ceil(jnp.log2(jnp.maximum(top, 1e-30)) + 0.01)
    scaled = x * jnp.exp2(15.0 - exponent)
    values = jnp.clip(jnp.round(scaled), -32767.0, 32767.0).astype(jnp.int32).astype(jnp.int16)
    row = jnp.broadcast_to(exponent, (code_rows, x.shape[1])).astype(jnp.int32).astype(jnp.int16)
    return values, row


def decoded(ref):
    values = ref[: ref.shape[0] - code_rows].astype(jnp.int32).astype(jnp.float32)
    exponents = ref[ref.shape[0] - code_rows :].astype(jnp.int32).astype(jnp.float32)
    return values * jnp.exp2(exponents[:1] - 15.0)


def swapped_kernel(m_ref, hidden_ref, cross_hidden_ref, cross_ref, far_ref, swapped_ref, places_ref, *refs):
    *matrix_refs, out_ref, helped_ref, own_turned_ref, end_turned_ref, end_places_ref, bands_ref = refs
    handed, side = swapped_ref.shape[0] - place_rows, out_ref.shape[0]
    alone = cross_ref.shape[0] - handed
    out_ref[...] = m_ref[...] + dot(cross_hidden_ref[...], swapped_ref[:handed], ((0,), (0,)))
    helped_ref[...] = dot(swapped_ref[:alone, :side], cross_ref[handed:], ((0,), (0,))) + dot(
        swapped_ref[alone:handed, :side], far_ref[...], ((0,), (0,))
    )
    own_turned_ref[...] = hidden_ref[...].T
    end_turned_ref[...] = swapped_ref[:handed, side:].T
    end_places_ref[...] = swapped_ref[handed:].astype(jnp.float32)
    bands_ref[...] = bands_of(out_ref[...], places_ref[...], *matrix_refs)


def helped_kernel(helped_ref, turned_ref, far_ref, places_ref, *refs):
    *matrix_refs, code_ref, bands_ref = refs
    product = helped_ref[...] + dot(turned_ref[...], far_ref[...])
    bands_ref[...] = bands_of(product, places_ref[...], *matrix_refs)
    side = product.shape[0]
    code_ref[:side], code_ref[side:] = coded(product)


def last_rows_kernel(end_ref, m_ref, own_bands_ref, turned_ref, far_ref, places_ref, *refs):
    *matrix_refs, out_ref, bands_ref = refs

    @pl.when(end_ref[0] == 1)
    def _():
        out_ref[...] = m_ref[...]
        bands_ref[...] = own_bands_ref[...]

    @pl.when(end_ref[0] == 0)
    def _():
        out_ref[...] = m_ref[...] + dot(turned_ref[...], far_ref[...])
        bands_ref[...] = bands_of(out_ref[...], places_ref[...], *matrix_refs)


def remove_kernel(m_ref, bands_ref, places_ref, fold_ref, basis_ref, out_ref):
    masks = masks_of(places_ref[...], out_ref.shape[0] // order)
    coefficients = within(spread(bands_ref[...], fold_ref[...]), masks)
    out_ref[...] = m_ref[...] - restored(coefficients, masks, basis_ref)


def add_kernel(x_ref, code_ref, out_ref):
    out_ref[...] = x_ref[...] + decoded(code_ref)


def update_kernel(*refs):
    *part_refs, places_ref, fold_ref, basis_ref, out_ref = refs
    bands = pair_sum([ref[...] for ref in part_refs])
    masks = masks_of(places_ref[...], out_ref.shape[0] // order)
    coefficients = within(spread(bands, fold_ref[...]), masks)
    out_ref[...] = restored(coefficients, masks, basis_ref).astype(out_ref.dtype)


def pair_sum(parts):
    while len(parts) > 1:
        parts = [sum(parts[i + 1 : i + 2], parts[i]) for i in range(0, len(parts), 2)]
    return parts[0]


def call(kernel, out_shapes, *operands):
    spaces = [pltpu.SMEM if x.dtype == jnp.int32 else pltpu.VMEM for x in operands]
    return pl.pallas_call(
        kernel,
        out_shape=out_shapes,
        in_specs=[pl.BlockSpec(memory_space=space) for space in spaces],
        compiler_params=pltpu.CompilerParams(vmem_limit_bytes=16 * 2**20),
        cost_estimate=pl.CostEstimate(flops=4 * 10**8, bytes_accessed=4 * 10**6, transcendentals=0),
    )(*operands)


def spread_sum(x, axis):
    size = lax.axis_size(axis)
    if size & (size - 1):
        return [lax.psum(x, axis)]
    stride, parts = 1, [x]
    while stride < size:
        count = min(4, size // stride)
        x = pair_sum(parts)
        parts = [x] + [
            lax.ppermute(x, axis, [(i, i ^ (stride * k)) for i in range(size)]) for k in range(1, count)
        ]
        stride *= count
    return parts


def product(hidden_rows, grad_rows):
    return dot(hidden_rows, grad_rows, ((0,), (0,)))


def after(x, *others):
    return lax.optimization_barrier((x, *others))[0]


def gathered(hidden, out_grad, carried, places, matrices):
    m = carried + product(hidden, lax.all_gather(out_grad, "tp", axis=0, tiled=True))
    folded = jax.ShapeDtypeStruct((m.shape[0] // steps, m.shape[1] // steps), jnp.float32)
    bands = call(bands_kernel, folded, m, places, *matrices)
    return m, bands, None, spread_sum(bands, "rep"), places, matrices


def lined(hidden, out_grad, carried, places, matrices):
    tok = out_grad.shape[0]
    me = lax.axis_index("tp")
    left = me < 2
    end = (me == 0) | (me == 3)
    cross = jnp.where(left, 2, 1)
    far = jnp.where(left, 3, 0)
    handed = tok * 2 // 3
    alone = tok - handed

    def rows_of(part, start=0, stop=tok):
        return lax.dynamic_slice_in_dim(hidden, part * tok + start, stop - start, 0)

    def send(x, perm):
        return lax.ppermute(x, "tp", perm)

    both_ways = [(0, 1), (1, 0), (2, 3), (3, 2)]
    across = [(1, 2), (2, 1)]
    outward = [(1, 0), (2, 3)]

    cross_grad = send(out_grad, across)
    m = carried + product(rows_of(me), out_grad)
    pair_parts = [send(out_grad[:alone], both_ways), send(out_grad[alone:], both_ways)]
    far_hidden = rows_of(far)
    helped_hidden = jnp.concatenate(
        [
            jnp.concatenate([rows_of(cross, handed), far_hidden[: handed - alone]], axis=0),
            far_hidden[handed - alone :],
        ],
        axis=1,
    )
    place_part = jnp.pad(places.astype(hidden.dtype), ((0, place_rows - places.shape[0]), (0, 0)))
    helped_hidden = jnp.concatenate([helped_hidden, place_part], axis=0)
    cross_hidden = jnp.where(end, rows_of(cross, 0, handed), 0)
    pair_head, helped_hidden, cross_hidden, m = lax.optimization_barrier(
        (pair_parts[0], helped_hidden, cross_hidden, m)
    )
    far_head = send(pair_head, across)
    m = m + product(rows_of(me ^ 1, 0, alone), pair_head)
    cross_grad, matrices, places = after((cross_grad, matrices, places), pair_head, m)
    to_swap = jnp.where(end, helped_hidden, cross_grad[: handed + place_rows])
    swapped = send(to_swap, both_ways)
    pair_rest, m, to_swap = lax.optimization_barrier((pair_parts[1], m, to_swap))
    far_parts = [far_head, send(pair_rest, across)]
    far_parts[0], pair_rest, cross_grad = lax.optimization_barrier((far_parts[0], pair_rest, cross_grad))
    m = m + product(rows_of(me ^ 1, alone), pair_rest)
    m = m + product(rows_of(cross), cross_grad) + product(far_hidden[:alone], far_parts[0])
    m, swapped = lax.optimization_barrier((m, swapped))

    height, width = m.shape[0] // steps, m.shape[1] // steps
    full = jax.ShapeDtypeStruct(m.shape, jnp.float32)
    turned = jax.ShapeDtypeStruct((m.shape[0], handed), hidden.dtype)
    table = jax.ShapeDtypeStruct((place_rows, m.shape[1]), jnp.float32)
    folded = jax.ShapeDtypeStruct((height, width), jnp.float32)
    m, helped, own_turned, end_turned, end_places, own_bands = call(
        swapped_kernel,
        (full, full, turned, turned, table, folded),
        m,
        far_hidden[alone:],
        cross_hidden,
        cross_grad,
        far_parts[0],
        swapped,
        places,
        *matrices,
    )
    far_grad = after(far_parts[1], m)
    code_shape = jax.ShapeDtypeStruct((m.shape[0] + code_rows, m.shape[1]), jnp.int16)
    code, end_bands = call(
        helped_kernel, (code_shape, folded), helped, end_turned, far_grad, end_places, *matrices
    )
    m, end_bands, code = lax.optimization_barrier((m, end_bands, code))
    end_bands = send(end_bands, both_ways)
    flag = end.astype(jnp.int32).reshape(1)
    m, bands = call(
        last_rows_kernel, (full, folded), flag, m, own_bands, own_turned, far_grad, places, *matrices
    )
    bands, code = lax.optimization_barrier((bands, code))
    code = send(code, outward)
    end_bands, bands = lax.optimization_barrier((end_bands, bands))
    bands = bands + jnp.where(end, end_bands, 0.0)
    parts = spread_sum(bands, "rep")
    return m, bands, code, parts, places, matrices


def local(hidden, out_grad, momentum, band_rows, band_start_columns):
    row_count = hidden.shape[1]
    col_count = out_grad.shape[1]
    one_hot = jnp.asarray(np.kron(np.eye(col_count // order), np.ones((1, order))), jnp.float32)
    matrices = (jnp.asarray(fold_matrix(col_count)), jnp.asarray(diagonal_blocks(row_count, col_count)))
    places = jnp.concatenate([band_rows, band_start_columns], axis=0).astype(jnp.float32)
    places = dot(places, one_hot)
    fits = out_grad.shape[0] % 384 == 0 and 2 * row_count == col_count and places.shape[0] <= place_rows
    form = lined if fits and lax.axis_size("tp") == 4 else gathered
    m, bands, code, band_parts, places, matrices = form(
        hidden, out_grad, decay_rate * momentum[0], places, matrices
    )
    full = jax.ShapeDtypeStruct(m.shape, jnp.float32)
    momentum_out = call(remove_kernel, full, m, bands, places, *matrices)
    if code is not None:
        momentum_out = call(add_kernel, full, momentum_out, code)
    *band_parts, momentum_out = lax.optimization_barrier((*band_parts, momentum_out))
    update = call(update_kernel, jax.ShapeDtypeStruct(m.shape, jnp.bfloat16), *band_parts, places, *matrices)
    return (momentum_out[None], update)


def solution(mesh):
    return jax.shard_map(
        local,
        mesh=mesh,
        in_specs=(
            P("rep", "tp"),
            P(("rep", "tp"), None),
            P("rep", "tp", None),
            P("tp", None),
            P("tp", None),
        ),
        out_specs=(P("rep", "tp", None), P("tp", None)),
        check_vma=False,
    )
```

```python
import jax
import jax.numpy as jnp
import numpy as np
from jax import lax
from jax.experimental import pallas as pl
from jax.experimental.pallas import tpu as pltpu
from jax.sharding import PartitionSpec as P

decay_rate = 0.9
order = 64
band = 16
steps = order // band
place_rows = 16
code_rows = 16


def basis_matrix():
    frequency = np.arange(order, dtype=np.float64)[:, None]
    sample_pos = np.arange(order, dtype=np.float64)[None, :]
    norm_scale = np.where(frequency == 0, np.sqrt(1.0 / order), np.sqrt(2.0 / order))
    return norm_scale * np.cos(np.pi * (sample_pos + 0.5) * frequency / order)


def diagonal_blocks(*widths):
    count = next(c for c in (4, 2, 1) if all(width % (c * order) == 0 for width in widths))
    return np.kron(np.eye(count), basis_matrix()).astype(np.float32)


def fold_matrix(width):
    return np.kron(np.eye(width // order), np.kron(np.ones((steps, 1)), np.eye(band))).astype(jnp.bfloat16)


def split2(x):
    high = x.astype(jnp.bfloat16)
    return high, (x - high.astype(jnp.float32)).astype(jnp.bfloat16)


def dot(a, b, dims=((1,), (0,))):
    return lax.dot_general(a, b, (dims, ((), ())), preferred_element_type=jnp.float32)


def dot3(a, b, dims=((1,), (0,))):
    (a_high, a_low), (b_high, b_low) = a, b
    left = jnp.concatenate([a_high, a_low, a_high], axis=dims[0][0])
    right = jnp.concatenate([b_high, b_high, b_low], axis=dims[1][0])
    return dot(left, right, dims)


def on_rows(basis_ref, x, transposed):
    basis, side = split2(basis_ref[...]), basis_ref.shape[0]
    dims = ((0,), (0,)) if transposed else ((1,), (0,))
    parts = [dot3(basis, split2(x[i : i + side]), dims) for i in range(0, x.shape[0], side)]
    return parts[0] if len(parts) == 1 else jnp.concatenate(parts, axis=0)


def on_columns(basis_ref, x, transposed):
    basis, side = split2(basis_ref[...]), basis_ref.shape[0]
    dims = ((1,), (0,)) if transposed else ((1,), (1,))
    parts = [dot3(split2(x[:, i : i + side]), basis, dims) for i in range(0, x.shape[1], side)]
    return parts[0] if len(parts) == 1 else jnp.concatenate(parts, axis=1)


def masks_of(places, count):
    width = places.shape[1]
    column = lax.rem(lax.broadcasted_iota(jnp.int32, (band, width), 1), order).astype(jnp.float32)
    masks = []
    for row in range(count):
        start = places[count + row : count + row + 1, :]
        masks.append((places[row : row + 1, :], (column >= start) & (column < start + band)))
    return masks


def rows_taken(x, masks):
    pieces = []
    for row, (at, _) in enumerate(masks):
        taken = jnp.zeros((band, x.shape[1]), jnp.float32)
        for step in range(steps):
            start = row * order + step * band
            taken = jnp.where(at == step * band, x[start : start + band], taken)
        pieces.append(taken)
    return jnp.concatenate(pieces, axis=0)


def selected(x, masks, basis_ref):
    taken = rows_taken(on_rows(basis_ref, x, False), masks)
    return within(on_columns(basis_ref, taken, False), masks)


def within(x, masks):
    return jnp.concatenate(
        [jnp.where(inside, x[i * band : (i + 1) * band], 0.0) for i, (_, inside) in enumerate(masks)], axis=0
    )


def restored(x, masks, basis_ref):
    by_columns = on_columns(basis_ref, x, True)
    pieces = []
    for row, (at, _) in enumerate(masks):
        part = by_columns[row * band : (row + 1) * band]
        pieces += [jnp.where(at == step * band, part, 0.0) for step in range(steps)]
    return on_rows(basis_ref, jnp.concatenate(pieces, axis=0), True)


def bands_of(x, places, fold_ref, basis_ref):
    return folded(selected(x, masks_of(places, x.shape[0] // order), basis_ref), fold_ref[...])


def folded(x, fold):
    return dot(jnp.concatenate(split2(x), axis=1), jnp.concatenate([fold] * 2, axis=0))


def spread(x, fold):
    return dot(jnp.concatenate(split2(x), axis=1), jnp.concatenate([fold] * 2, axis=1), ((1,), (1,)))


def bands_kernel(m_ref, places_ref, *refs):
    *matrix_refs, bands_ref = refs
    bands_ref[...] = bands_of(m_ref[...], places_ref[...], *matrix_refs)


def coded(x):
    top = jnp.max(jnp.abs(x), axis=0, keepdims=True)
    exponent = jnp.ceil(jnp.log2(jnp.maximum(top, 1e-30)) + 0.01)
    scaled = x * jnp.exp2(15.0 - exponent)
    values = jnp.clip(jnp.round(scaled), -32767.0, 32767.0).astype(jnp.int32).astype(jnp.int16)
    row = jnp.broadcast_to(exponent, (code_rows, x.shape[1])).astype(jnp.int32).astype(jnp.int16)
    return values, row


def decoded(ref):
    values = ref[: ref.shape[0] - code_rows].astype(jnp.int32).astype(jnp.float32)
    exponents = ref[ref.shape[0] - code_rows :].astype(jnp.int32).astype(jnp.float32)
    return values * jnp.exp2(exponents[:1] - 15.0)


def swapped_kernel(m_ref, hidden_ref, cross_hidden_ref, cross_ref, far_ref, swapped_ref, places_ref, *refs):
    *matrix_refs, out_ref, helped_ref, own_turned_ref, end_turned_ref, end_places_ref, bands_ref = refs
    handed, side = swapped_ref.shape[0] - place_rows, out_ref.shape[0]
    alone = cross_ref.shape[0] - handed
    out_ref[...] = m_ref[...] + dot(cross_hidden_ref[...], swapped_ref[:handed], ((0,), (0,)))
    helped_ref[...] = dot(swapped_ref[:alone, :side], cross_ref[handed:], ((0,), (0,))) + dot(
        swapped_ref[alone:handed, :side], far_ref[...], ((0,), (0,))
    )
    own_turned_ref[...] = hidden_ref[...].T
    end_turned_ref[...] = swapped_ref[:handed, side:].T
    end_places_ref[...] = swapped_ref[handed:].astype(jnp.float32)
    bands_ref[...] = bands_of(out_ref[...], places_ref[...], *matrix_refs)


def helped_kernel(helped_ref, turned_ref, far_ref, places_ref, *refs):
    *matrix_refs, code_ref, bands_ref = refs
    product = helped_ref[...] + dot(turned_ref[...], far_ref[...])
    bands_ref[...] = bands_of(product, places_ref[...], *matrix_refs)
    side = product.shape[0]
    code_ref[:side], code_ref[side:] = coded(product)


def last_rows_kernel(end_ref, m_ref, own_bands_ref, turned_ref, far_ref, places_ref, *refs):
    *matrix_refs, out_ref, bands_ref = refs

    @pl.when(end_ref[0] == 1)
    def _():
        out_ref[...] = m_ref[...]
        bands_ref[...] = own_bands_ref[...]

    @pl.when(end_ref[0] == 0)
    def _():
        out_ref[...] = m_ref[...] + dot(turned_ref[...], far_ref[...])
        bands_ref[...] = bands_of(out_ref[...], places_ref[...], *matrix_refs)


def remove_kernel(m_ref, bands_ref, places_ref, fold_ref, basis_ref, out_ref):
    masks = masks_of(places_ref[...], out_ref.shape[0] // order)
    coefficients = within(spread(bands_ref[...], fold_ref[...]), masks)
    out_ref[...] = m_ref[...] - restored(coefficients, masks, basis_ref)


def add_kernel(x_ref, code_ref, out_ref):
    out_ref[...] = x_ref[...] + decoded(code_ref)


def update_kernel(*refs):
    *part_refs, places_ref, fold_ref, basis_ref, out_ref = refs
    bands = pair_sum([ref[...] for ref in part_refs])
    masks = masks_of(places_ref[...], out_ref.shape[0] // order)
    coefficients = within(spread(bands, fold_ref[...]), masks)
    out_ref[...] = restored(coefficients, masks, basis_ref).astype(out_ref.dtype)


def pair_sum(parts):
    while len(parts) > 1:
        parts = [sum(parts[i + 1 : i + 2], parts[i]) for i in range(0, len(parts), 2)]
    return parts[0]


def call(kernel, out_shapes, *operands):
    spaces = [pltpu.SMEM if x.dtype == jnp.int32 else pltpu.VMEM for x in operands]
    return pl.pallas_call(
        kernel,
        out_shape=out_shapes,
        in_specs=[pl.BlockSpec(memory_space=space) for space in spaces],
        compiler_params=pltpu.CompilerParams(vmem_limit_bytes=16 * 2**20),
        cost_estimate=pl.CostEstimate(flops=4 * 10**8, bytes_accessed=4 * 10**6, transcendentals=0),
    )(*operands)


def spread_sum(x, axis):
    size = lax.axis_size(axis)
    if size & (size - 1):
        return [lax.psum(x, axis)]
    stride, parts = 1, [x]
    while stride < size:
        count = min(4, size // stride)
        x = pair_sum(parts)
        parts = [x] + [
            lax.ppermute(x, axis, [(i, i ^ (stride * k)) for i in range(size)]) for k in range(1, count)
        ]
        stride *= count
    return parts


def product(hidden_rows, grad_rows):
    return dot(hidden_rows, grad_rows, ((0,), (0,)))


def after(x, *others):
    return lax.optimization_barrier((x, *others))[0]


def gathered(hidden, out_grad, carried, places, matrices):
    m = carried + product(hidden, lax.all_gather(out_grad, "tp", axis=0, tiled=True))
    folded = jax.ShapeDtypeStruct((m.shape[0] // steps, m.shape[1] // steps), jnp.float32)
    bands = call(bands_kernel, folded, m, places, *matrices)
    return m, bands, None, spread_sum(bands, "rep"), places, matrices


def lined(hidden, out_grad, carried, places, matrices):
    tok = out_grad.shape[0]
    me = lax.axis_index("tp")
    left = me < 2
    end = (me == 0) | (me == 3)
    cross = jnp.where(left, 2, 1)
    far = jnp.where(left, 3, 0)
    handed = tok * 2 // 3
    alone = tok - handed

    def rows_of(part, start=0, stop=tok):
        return lax.dynamic_slice_in_dim(hidden, part * tok + start, stop - start, 0)

    def send(x, perm):
        return lax.ppermute(x, "tp", perm)

    both_ways = [(0, 1), (1, 0), (2, 3), (3, 2)]
    across = [(1, 2), (2, 1)]
    outward = [(1, 0), (2, 3)]

    cross_grad = send(out_grad, across)
    m = carried + product(rows_of(me), out_grad)
    pair_parts = [send(out_grad[:alone], both_ways), send(out_grad[alone:], both_ways)]
    far_hidden = rows_of(far)
    helped_hidden = jnp.concatenate(
        [
            jnp.concatenate([rows_of(cross, handed), far_hidden[: handed - alone]], axis=0),
            far_hidden[handed - alone :],
        ],
        axis=1,
    )
    place_part = jnp.pad(places.astype(hidden.dtype), ((0, place_rows - places.shape[0]), (0, 0)))
    helped_hidden = jnp.concatenate([helped_hidden, place_part], axis=0)
    cross_hidden = jnp.where(end, rows_of(cross, 0, handed), 0)
    pair_head, helped_hidden, cross_hidden, m = lax.optimization_barrier(
        (pair_parts[0], helped_hidden, cross_hidden, m)
    )
    far_head = send(pair_head, across)
    m = m + product(rows_of(me ^ 1, 0, alone), pair_head)
    cross_grad, matrices, places = after((cross_grad, matrices, places), pair_head, m)
    to_swap = jnp.where(end, helped_hidden, cross_grad[: handed + place_rows])
    swapped = send(to_swap, both_ways)
    pair_rest, m, to_swap = lax.optimization_barrier((pair_parts[1], m, to_swap))
    far_parts = [far_head, send(pair_rest, across)]
    far_parts[0], pair_rest, cross_grad = lax.optimization_barrier((far_parts[0], pair_rest, cross_grad))
    m = m + product(rows_of(me ^ 1, alone), pair_rest)
    m = m + product(rows_of(cross), cross_grad) + product(far_hidden[:alone], far_parts[0])
    m, swapped = lax.optimization_barrier((m, swapped))

    height, width = m.shape[0] // steps, m.shape[1] // steps
    full = jax.ShapeDtypeStruct(m.shape, jnp.float32)
    turned = jax.ShapeDtypeStruct((m.shape[0], handed), hidden.dtype)
    table = jax.ShapeDtypeStruct((place_rows, m.shape[1]), jnp.float32)
    folded = jax.ShapeDtypeStruct((height, width), jnp.float32)
    m, helped, own_turned, end_turned, end_places, own_bands = call(
        swapped_kernel,
        (full, full, turned, turned, table, folded),
        m,
        far_hidden[alone:],
        cross_hidden,
        cross_grad,
        far_parts[0],
        swapped,
        places,
        *matrices,
    )
    far_grad = after(far_parts[1], m)
    code_shape = jax.ShapeDtypeStruct((m.shape[0] + code_rows, m.shape[1]), jnp.int16)
    code, end_bands = call(
        helped_kernel, (code_shape, folded), helped, end_turned, far_grad, end_places, *matrices
    )
    m, end_bands, code = lax.optimization_barrier((m, end_bands, code))
    end_bands = send(end_bands, both_ways)
    flag = end.astype(jnp.int32).reshape(1)
    m, bands = call(
        last_rows_kernel, (full, folded), flag, m, own_bands, own_turned, far_grad, places, *matrices
    )
    bands, code = lax.optimization_barrier((bands, code))
    code = send(code, outward)
    end_bands, bands = lax.optimization_barrier((end_bands, bands))
    bands = bands + jnp.where(end, end_bands, 0.0)
    parts = spread_sum(bands, "rep")
    return m, bands, code, parts, places, matrices


def local(hidden, out_grad, momentum, band_rows, band_start_columns):
    row_count = hidden.shape[1]
    col_count = out_grad.shape[1]
    one_hot = jnp.asarray(np.kron(np.eye(col_count // order), np.ones((1, order))), jnp.float32)
    matrices = (jnp.asarray(fold_matrix(col_count)), jnp.asarray(diagonal_blocks(row_count, col_count)))
    places = jnp.concatenate([band_rows, band_start_columns], axis=0).astype(jnp.float32)
    places = dot(places, one_hot)
    fits = out_grad.shape[0] % 384 == 0 and 2 * row_count == col_count and places.shape[0] <= place_rows
    form = lined if fits and lax.axis_size("tp") == 4 else gathered
    m, bands, code, band_parts, places, matrices = form(
        hidden, out_grad, decay_rate * momentum[0], places, matrices
    )
    full = jax.ShapeDtypeStruct(m.shape, jnp.float32)
    momentum_out = call(remove_kernel, full, m, bands, places, *matrices)
    if code is not None:
        momentum_out = call(add_kernel, full, momentum_out, code)
    *band_parts, momentum_out = lax.optimization_barrier((*band_parts, momentum_out))
    update = call(update_kernel, jax.ShapeDtypeStruct(m.shape, jnp.bfloat16), *band_parts, places, *matrices)
    return (momentum_out[None], update)


def solution(mesh):
    return jax.shard_map(
        local,
        mesh=mesh,
        in_specs=(
            P("rep", "tp"),
            P(("rep", "tp"), None),
            P("rep", "tp", None),
            P("tp", None),
            P("tp", None),
        ),
        out_specs=(P("rep", "tp", None), P("tp", None)),
        check_vma=False,
    )
```
